32 devices in a mesh: seq: 16 (over z, y, core), head: 2 (over x).
Axes of the slice: x: 2, y: 2, z: 4, core: 2. Of those that a mesh axis runs over, the one named last changes fastest.
Arguments:
- query_main: bfloat16 [512, 2048], P(('seq', 'head')), may hold values from -5 to 5
- key_main: bfloat16 [512, 2048], P(('seq', 'head')), may hold values from -5 to 5
- value_main: bfloat16 [512, 2048], P(('seq', 'head')), may hold values from -5 to 5
- query_tan: bfloat16 [512, 2048], P(('seq', 'head')), may hold values from -5 to 5
- key_tan: bfloat16 [512, 2048], P(('seq', 'head')), may hold values from -5 to 5
- value_tan: bfloat16 [512, 2048], P(('seq', 'head')), may hold values from -5 to 5
- positions: int32 [512], P(('seq', 'head')), may hold values from 0 to 1073741823, as said below
Outputs:
- attended: bfloat16 [512, 2048], P(('seq', 'head'))
- attended_tan: bfloat16 [512, 2048], P(('seq', 'head'))
The draws below stay inside these ranges and needn't reach their ends.
Inputs may be any that keep to these rules, and one draw needn't show every extreme that they name: `positions`: 512 distinct values.
All inputs are finite; a program needn't handle non-finite values.
Results may differ from the reference program's by a relative error of at most 0.035.
Values may be sent and summed in bfloat16 or wider, within the bound.
No kernel may reach another device: no remote copies, remote signals or barrier semaphores. Data moves between devices by JAX's collectives and lax.ppermute only.
A program may use at most 128 MiB of HBM per device.

```python
import math
import jax
import jax.numpy as jnp
from jax import lax

HEADS = 16
HEAD_DIM = 128
SEQ = 512


def draw_query_main(key, part):
    own = jax.random.fold_in(key, 1)
    values = jnp.clip(jax.random.normal(own, (SEQ, HEADS * HEAD_DIM), jnp.float32), -4.0, 4.0)
    return values.astype(jnp.bfloat16)


def draw_key_main(key, part):
    own = jax.random.fold_in(key, 2)
    values = jnp.clip(jax.random.normal(own, (SEQ, HEADS * HEAD_DIM), jnp.float32), -4.0, 4.0)
    return values.astype(jnp.bfloat16)


def draw_positions(key, part):
    key = jax.random.fold_in(key, 3)
    first, second = jax.random.split(key)
    top_value = 2 ** 30 - SEQ
    raw = jax.random.randint(first, (SEQ,), 0, top_value, dtype=jnp.int32)
    ranked = jnp.sort(raw)
    ranked = ranked.at[0].set(0).at[SEQ - 1].set(top_value)
    keyed = ranked + jnp.arange(SEQ, dtype=jnp.int32)
    order = jax.random.permutation(second, SEQ).astype(jnp.int32)
    return keyed[order].astype(jnp.int32)


def block_levels(rng, dims, shards, smallest, high):
    level, own = 1.0, jax.random.fold_in(rng, 6)
    for axis_at, parts in shards:
        steps = jnp.exp(jax.random.uniform(jax.random.fold_in(own, axis_at), (parts,), jnp.float32, smallest / len(shards), high / len(shards)))
        level = level * jnp.repeat(steps, dims[axis_at] // parts).reshape([-1 if axis == axis_at else 1 for axis in range(len(dims))])
    return level


def normal_values(rng, extent, scale, bound, cuts=(), kind=jnp.bfloat16):
    drawn = jax.random.normal(rng, extent, jnp.float32) * scale
    if len(cuts) > 0:
        drawn = block_levels(rng, extent, cuts, -0.22, 0.18) * drawn
    return jnp.clip(drawn, min=-bound, max=bound).astype(kind)


def setup_inputs(seed: int = 0) -> dict:
    streams_of = jax.random.split(jax.random.key(seed), 8)
    query_main = draw_query_main(jax.random.fold_in(streams_of[7], 71), 0)
    key_main = draw_key_main(jax.random.fold_in(streams_of[7], 71), 0)
    value_main = normal_values(streams_of[2], (SEQ, HEADS * HEAD_DIM), 1.0, 5.0, ((0, 32),))
    query_tan = normal_values(streams_of[3], (SEQ, HEADS * HEAD_DIM), 1.0, 5.0, ((0, 32),))
    key_tan = normal_values(streams_of[4], (SEQ, HEADS * HEAD_DIM), 1.0, 5.0, ((0, 32),))
    value_tan = normal_values(streams_of[5], (SEQ, HEADS * HEAD_DIM), 1.0, 5.0, ((0, 32),))
    positions = draw_positions(jax.random.fold_in(streams_of[7], 71), 0)
    return {"query_main": query_main, "key_main": key_main, "value_main": value_main, "query_tan": query_tan, "key_tan": key_tan, "value_tan": value_tan, "positions": positions}


def reference(query_main, key_main, value_main, query_tan, key_tan, value_tan, positions):
    scale = HEAD_DIM ** -0.5
    rows = math.gcd(SEQ, 256)
    queries = query_main.reshape(SEQ, HEADS, HEAD_DIM).astype(jnp.float32)
    keys = key_main.reshape(SEQ, HEADS, HEAD_DIM).astype(jnp.float32)
    values = value_main.reshape(SEQ, HEADS, HEAD_DIM).astype(jnp.float32)
    query_dot = query_tan.reshape(SEQ, HEADS, HEAD_DIM).astype(jnp.float32)
    key_dot = key_tan.reshape(SEQ, HEADS, HEAD_DIM).astype(jnp.float32)
    value_dot = value_tan.reshape(SEQ, HEADS, HEAD_DIM).astype(jnp.float32)

    def one_block(start):
        block_q = lax.dynamic_slice_in_dim(queries, start, rows, 0)
        block_dq = lax.dynamic_slice_in_dim(query_dot, start, rows, 0)
        block_pos = lax.dynamic_slice_in_dim(positions, start, rows, 0)
        scores = jnp.einsum('qhd,khd->hqk', block_q, keys) * scale
        visible = positions[None, :] <= block_pos[:, None]
        scores = jnp.where(visible[None], scores, -jnp.inf)
        score_tan = (jnp.einsum('qhd,khd->hqk', block_dq, keys) + jnp.einsum('qhd,khd->hqk', block_q, key_dot)) * scale
        probs = jax.nn.softmax(scores, axis=-1)
        weighted = probs * score_tan
        mass = jnp.sum(weighted, axis=-1)
        probs_low = lax.optimization_barrier(probs.astype(jnp.bfloat16)).astype(jnp.float32)
        weighted_low = lax.optimization_barrier(weighted.astype(jnp.bfloat16)).astype(jnp.float32)
        mixed = jnp.einsum('hqk,khd->hqd', probs_low, values)
        tangent = jnp.einsum('hqk,khd->hqd', weighted_low, values) + jnp.einsum('hqk,khd->hqd', probs_low, value_dot)
        tangent = tangent - mass[..., None] * mixed
        mixed = jnp.transpose(mixed, (1, 0, 2)).reshape(rows, HEADS * HEAD_DIM)
        tangent = jnp.transpose(tangent, (1, 0, 2)).reshape(rows, HEADS * HEAD_DIM)
        return mixed.astype(jnp.bfloat16), tangent.astype(jnp.bfloat16)

    starts = (jnp.arange(SEQ // rows) * rows).astype(jnp.int32)
    mixed_all, tangent_all = lax.map(one_block, starts)
    return mixed_all.reshape(SEQ, HEADS * HEAD_DIM), tangent_all.reshape(SEQ, HEADS * HEAD_DIM)
```

```python
import functools

import jax
import jax.numpy as jnp
from jax import lax
from jax.experimental import pallas as pl
from jax.experimental.pallas import tpu as pltpu
from jax.sharding import PartitionSpec as P

HEADS = 16
HEAD_DIM = 128
AXES = ("seq", "head")
PIECES = 4


def plan(mesh):
    heads_axis = mesh.shape["head"]
    peers = mesh.shape["seq"] * heads_axis // HEADS
    assert mesh.shape["seq"] % peers == 0

    def flat(peer, member):
        return (member // heads_axis * peers + peer) * heads_axis + member % heads_axis

    return peers, flat


def pack_kernel(positions, *refs):
    arrays, out = refs[:-1], refs[-1]
    rows = arrays[0].shape[0]
    token = lax.broadcasted_iota(jnp.int32, (rows, HEAD_DIM), 0)
    lane = lax.broadcasted_iota(jnp.int32, (rows, HEAD_DIM), 1)
    place = jnp.zeros((rows, HEAD_DIM), jnp.int32)
    for t in range(rows):
        place = jnp.where(token == t, positions[t], place)
    place = lax.shift_right_logical(place, lane % PIECES * 8) & 255
    place = place.astype(jnp.float32).astype(jnp.bfloat16)
    for h in range(HEADS):
        for at, array in enumerate(arrays):
            out[h, at * rows : (at + 1) * rows, :] = array[:, h * HEAD_DIM : (h + 1) * HEAD_DIM]
        out[h, len(arrays) * rows :, :] = place


def pack(positions, arrays):
    rows = arrays[0].shape[0]
    return pl.pallas_call(
        pack_kernel,
        out_shape=jax.ShapeDtypeStruct((HEADS, 7 * rows, HEAD_DIM), jnp.bfloat16),
        in_specs=[pl.BlockSpec(memory_space=pltpu.SMEM)]
        + [pl.BlockSpec(memory_space=pltpu.VMEM)] * len(arrays),
        out_specs=pl.BlockSpec(memory_space=pltpu.VMEM),
        name="pack",
    )(positions, *arrays)


def dot(a, b, contract):
    return lax.dot_general(a, b, (contract, ((), ())), preferred_element_type=jnp.float32)


def order_of(pair):
    high, low = pair
    return high.astype(jnp.int32) * 65536 + low.astype(jnp.int32)


def attention_kernel(rows, *refs):
    blocks, out = refs[:-1], refs[-1]
    count = HEADS * rows
    scale = HEAD_DIM ** (-0.5)

    def part(ref, at):
        return ref[:, at * rows : (at + 1) * rows, :].reshape(count, HEAD_DIM)

    def weights(shape, axis, first):
        at = lax.broadcasted_iota(jnp.int32, shape, axis)
        chosen = jnp.where(at == first, 1.0, jnp.where(at == first + 1, 256.0, 0.0))
        return chosen.astype(jnp.bfloat16)

    own = blocks[0]
    queries = part(own, 0)
    query_pair = jnp.concatenate([part(own, 3), queries], axis=1)
    own_order = part(own, 6)
    across = (HEAD_DIM, HEAD_DIM)
    query_order = order_of([dot(own_order, weights(across, 0, first), ((1,), (0,))) for first in (2, 0)])
    state = None
    for start in range(0, len(blocks), 2):
        group = blocks[start : start + 2]

        def keyed(at):
            return jnp.concatenate([part(ref, at) for ref in group], axis=0)

        keys, values, key_dot, value_dot, order = [keyed(at) for at in (1, 2, 4, 5, 6)]
        width = keys.shape[0]
        down = (8, HEAD_DIM)
        key_order = order_of([dot(weights(down, 1, first), order, ((1,), (1,))) for first in (2, 0)])
        wide_order = jnp.concatenate([query_order] * (width // HEAD_DIM), axis=1)
        visible = key_order[:1] <= wide_order
        scores = dot(queries, keys, ((1,), (1,))) * scale
        scores = jnp.where(visible, scores, -1e30)
        key_pair = jnp.concatenate([keys, key_dot], axis=1)
        score_tan = dot(query_pair, key_pair, ((1,), (1,))) * scale
        new_max = jnp.max(scores, axis=1, keepdims=True)
        if state is not None:
            new_max = jnp.maximum(new_max, state[0])
        expo = jnp.exp(scores - new_max)
        weighted = expo * score_tan
        total = jnp.sum(expo, axis=1, keepdims=True)
        mass = jnp.sum(weighted, axis=1, keepdims=True)
        expo_low = expo.astype(jnp.bfloat16)
        weighted_low = weighted.astype(jnp.bfloat16)
        mixed = dot(expo_low, values, ((1,), (0,)))
        tangent = dot(
            jnp.concatenate([weighted_low, expo_low], axis=1),
            jnp.concatenate([values, value_dot], axis=0),
            ((1,), (0,)),
        )
        if state is not None:
            shrink = jnp.exp(state[0] - new_max)
            total, mass, mixed, tangent = [
                new + old * shrink for new, old in zip((total, mass, mixed, tangent), state[1:])
            ]
        state = (new_max, total, mass, mixed, tangent)
    _, total, mass, mixed, tangent = state
    inverse = 1.0 / total
    mixed = mixed * inverse
    tangent = tangent * inverse - mass * inverse * mixed
    out[:, :rows, :] = mixed.astype(jnp.bfloat16).reshape(HEADS, rows, HEAD_DIM)
    out[:, rows:, :] = tangent.astype(jnp.bfloat16).reshape(HEADS, rows, HEAD_DIM)


def attention(rows, blocks):
    return pl.pallas_call(
        functools.partial(attention_kernel, rows),
        out_shape=jax.ShapeDtypeStruct((HEADS, 2 * rows, HEAD_DIM), jnp.bfloat16),
        in_specs=[pl.BlockSpec(memory_space=pltpu.VMEM)] * len(blocks),
        out_specs=pl.BlockSpec(memory_space=pltpu.VMEM),
        compiler_params=pltpu.CompilerParams(vmem_limit_bytes=48 * 2**20),
        name="attention",
    )(*blocks)


def unpack_kernel(packed, attended, attended_tan):
    rows = attended.shape[0]
    for h in range(HEADS):
        columns = slice(h * HEAD_DIM, (h + 1) * HEAD_DIM)
        attended[:, columns] = packed[h, :rows, :]
        attended_tan[:, columns] = packed[h, rows:, :]


def unpack(packed):
    rows = packed.shape[1] // 2
    shape = jax.ShapeDtypeStruct((rows, HEADS * HEAD_DIM), jnp.bfloat16)
    return pl.pallas_call(
        unpack_kernel,
        out_shape=(shape, shape),
        in_specs=[pl.BlockSpec(memory_space=pltpu.VMEM)],
        out_specs=[pl.BlockSpec(memory_space=pltpu.VMEM)] * 2,
        name="unpack",
    )(packed)


def solution(mesh):
    peers, flat = plan(mesh)
    teams = [[flat(peer, member) for member in range(HEADS)] for peer in range(peers)]

    def swap(value):
        return lax.all_to_all(value, AXES, split_axis=0, concat_axis=0, axis_index_groups=teams, tiled=True)

    def from_peer(value, by):
        pairs = [
            (flat(peer, member), flat((peer + by) % peers, member))
            for peer in range(peers)
            for member in range(HEADS)
        ]
        return lax.ppermute(value, AXES, pairs)

    def local(query_main, key_main, value_main, query_tan, key_tan, value_tan, positions):
        rows = query_main.shape[0]
        arrays = (query_main, key_main, value_main, query_tan, key_tan, value_tan)
        here = swap(pack(positions, arrays))
        blocks = [here] + [from_peer(here, by) for by in range(1, peers)]
        return unpack(swap(attention(rows, blocks)))

    placed = (P(AXES, None),) * 6 + (P(AXES),)
    return jax.shard_map(
        local,
        mesh=mesh,
        in_specs=placed,
        out_specs=(P(AXES, None), P(AXES, None)),
        check_vma=False,
    )
```

```python
import functools

import jax
import jax.numpy as jnp
from jax import lax
from jax.experimental import pallas as pl
from jax.experimental.pallas import tpu as pltpu
from jax.sharding import PartitionSpec as P

HEADS = 16
HEAD_DIM = 128
AXES = ("seq", "head")
PIECES = 4


def plan(mesh):
    heads_axis = mesh.shape["head"]
    peers = mesh.shape["seq"] * heads_axis // HEADS
    assert mesh.shape["seq"] % peers == 0

    def flat(peer, member):
        return (member // heads_axis * peers + peer) * heads_axis + member % heads_axis

    return peers, flat


def pack_kernel(member, positions, *refs):
    arrays, outs = refs[:6], refs[6:]
    rows = arrays[0].shape[0]
    token = lax.broadcasted_iota(jnp.int32, (rows, HEAD_DIM), 0)
    lane = lax.broadcasted_iota(jnp.int32, (rows, HEAD_DIM), 1)
    place = jnp.zeros((rows, HEAD_DIM), jnp.int32)
    for t in range(rows):
        place = jnp.where(token == t, positions[t], place)
    place = lax.shift_right_logical(place, lane % PIECES * 8) & 255
    place = place.astype(jnp.float32).astype(jnp.bfloat16)
    for step, out in enumerate(outs):
        columns = pl.ds(pl.multiple_of((member[0] ^ step) * HEAD_DIM, HEAD_DIM), HEAD_DIM)
        for at, array in enumerate(arrays):
            out[at * rows : (at + 1) * rows, :] = array[:, columns]
        out[len(arrays) * rows :, :] = place


def pack(member, positions, arrays):
    rows = arrays[0].shape[0]
    return pl.pallas_call(
        pack_kernel,
        out_shape=[jax.ShapeDtypeStruct((7 * rows, HEAD_DIM), jnp.bfloat16)] * HEADS,
        in_specs=[pl.BlockSpec(memory_space=pltpu.SMEM)] * 2
        + [pl.BlockSpec(memory_space=pltpu.VMEM)] * len(arrays),
        out_specs=[pl.BlockSpec(memory_space=pltpu.VMEM)] * HEADS,
        name="pack",
    )(member, positions, *arrays)


def dot(a, b, contract):
    return lax.dot_general(a, b, (contract, ((), ())), preferred_element_type=jnp.float32)


def order_of(pair):
    high, low = pair
    return high.astype(jnp.int32) * 65536 + low.astype(jnp.int32)


def attention_kernel(rows, *refs):
    blocks, outs = refs[:-HEADS], refs[-HEADS:]
    blocks = [blocks[at : at + HEADS] for at in range(0, len(blocks), HEADS)]
    scale = HEAD_DIM ** (-0.5)

    def part(refs, at):
        return jnp.concatenate([ref[at * rows : (at + 1) * rows, :] for ref in refs], axis=0)

    def weights(shape, axis, first):
        at = lax.broadcasted_iota(jnp.int32, shape, axis)
        chosen = jnp.where(at == first, 1.0, jnp.where(at == first + 1, 256.0, 0.0))
        return chosen.astype(jnp.bfloat16)

    own = blocks[0]
    queries = part(own, 0)
    query_pair = jnp.concatenate([part(own, 3), queries], axis=1)
    own_order = part(own, 6)
    across = (HEAD_DIM, HEAD_DIM)
    query_order = order_of([dot(own_order, weights(across, 0, first), ((1,), (0,))) for first in (2, 0)])
    state = None
    for start in range(0, len(blocks), 2):
        group = blocks[start : start + 2]

        def keyed(at):
            return jnp.concatenate([part(ref, at) for ref in group], axis=0)

        keys, values, key_dot, value_dot, order = [keyed(at) for at in (1, 2, 4, 5, 6)]
        width = keys.shape[0]
        down = (8, HEAD_DIM)
        key_order = order_of([dot(weights(down, 1, first), order, ((1,), (1,))) for first in (2, 0)])
        wide_order = jnp.concatenate([query_order] * (width // HEAD_DIM), axis=1)
        visible = key_order[:1] <= wide_order
        scores = dot(queries, keys, ((1,), (1,))) * scale
        scores = jnp.where(visible, scores, -1e30)
        key_pair = jnp.concatenate([keys, key_dot], axis=1)
        score_tan = dot(query_pair, key_pair, ((1,), (1,))) * scale
        new_max = jnp.max(scores, axis=1, keepdims=True)
        if state is not None:
            new_max = jnp.maximum(new_max, state[0])
        expo = jnp.exp(scores - new_max)
        weighted = expo * score_tan
        total = jnp.sum(expo, axis=1, keepdims=True)
        mass = jnp.sum(weighted, axis=1, keepdims=True)
        expo_low = expo.astype(jnp.bfloat16)
        weighted_low = weighted.astype(jnp.bfloat16)
        mixed = dot(expo_low, values, ((1,), (0,)))
        tangent = dot(
            jnp.concatenate([weighted_low, expo_low], axis=1),
            jnp.concatenate([values, value_dot], axis=0),
            ((1,), (0,)),
        )
        if state is not None:
            shrink = jnp.exp(state[0] - new_max)
            total, mass, mixed, tangent = [
                new + old * shrink for new, old in zip((total, mass, mixed, tangent), state[1:])
            ]
        state = (new_max, total, mass, mixed, tangent)
    _, total, mass, mixed, tangent = state
    inverse = 1.0 / total
    mixed = mixed * inverse
    tangent = tangent * inverse - mass * inverse * mixed
    mixed, tangent = mixed.astype(jnp.bfloat16), tangent.astype(jnp.bfloat16)
    for step, out in enumerate(outs):
        out[:rows, :] = mixed[step * rows : (step + 1) * rows]
        out[rows:, :] = tangent[step * rows : (step + 1) * rows]


def attention(rows, blocks):
    return pl.pallas_call(
        functools.partial(attention_kernel, rows),
        out_shape=[jax.ShapeDtypeStruct((2 * rows, HEAD_DIM), jnp.bfloat16)] * HEADS,
        in_specs=[pl.BlockSpec(memory_space=pltpu.VMEM)] * len(blocks),
        out_specs=[pl.BlockSpec(memory_space=pltpu.VMEM)] * HEADS,
        compiler_params=pltpu.CompilerParams(vmem_limit_bytes=48 * 2**20),
        name="attention",
    )(*blocks)


def unpack_kernel(member, *refs):
    packed, (attended, attended_tan) = refs[:HEADS], refs[HEADS:]
    rows = attended.shape[0]
    for step, block in enumerate(packed):
        columns = pl.ds(pl.multiple_of((member[0] ^ step) * HEAD_DIM, HEAD_DIM), HEAD_DIM)
        attended[:, columns] = block[:rows, :]
        attended_tan[:, columns] = block[rows:, :]


def unpack(member, packed):
    rows = packed[0].shape[0] // 2
    shape = jax.ShapeDtypeStruct((rows, HEADS * HEAD_DIM), jnp.bfloat16)
    return pl.pallas_call(
        unpack_kernel,
        out_shape=(shape, shape),
        in_specs=[pl.BlockSpec(memory_space=pltpu.SMEM)]
        + [pl.BlockSpec(memory_space=pltpu.VMEM)] * HEADS,
        out_specs=[pl.BlockSpec(memory_space=pltpu.VMEM)] * 2,
        name="unpack",
    )(member, *packed)


def solution(mesh):
    peers, flat = plan(mesh)
    heads_axis = mesh.shape["head"]

    def to_member(value, step):
        pairs = [
            (flat(peer, member), flat(peer, member ^ step))
            for peer in range(peers)
            for member in range(HEADS)
        ]
        return lax.ppermute(value, AXES, pairs) if step else value

    def from_peer(value, by):
        pairs = [
            (flat(peer, member), flat((peer + by) % peers, member))
            for peer in range(peers)
            for member in range(HEADS)
        ]
        return lax.ppermute(value, AXES, pairs)

    def forward(blocks):
        if peers == 2:
            return [from_peer(block, 1) for block in blocks]
        stacked = jnp.stack(blocks)
        moved = [from_peer(stacked, by) for by in range(1, peers)]
        return [block[at] for block in moved for at in range(HEADS)]

    def local(query_main, key_main, value_main, query_tan, key_tan, value_tan, positions):
        rows = query_main.shape[0]
        arrays = (query_main, key_main, value_main, query_tan, key_tan, value_tan)
        member = lax.axis_index("seq") // peers * heads_axis + lax.axis_index("head")
        member = member.astype(jnp.int32).reshape(1)
        here = [to_member(block, step) for step, block in enumerate(pack(member, positions, arrays))]
        outs = attention(rows, here + forward(here))
        return unpack(member, [to_member(block, step) for step, block in enumerate(outs)])

    placed = (P(AXES, None),) * 6 + (P(AXES),)
    return jax.shard_map(
        local,
        mesh=mesh,
        in_specs=placed,
        out_specs=(P(AXES, None), P(AXES, None)),
        check_vma=False,
    )
```

```python
import functools

import jax
import jax.numpy as jnp
from jax import lax
from jax.experimental import pallas as pl
from jax.experimental.pallas import tpu as pltpu
from jax.sharding import PartitionSpec as P

HEADS = 16
HEAD_DIM = 128
AXES = ("seq", "head")
TILE = 8
PIECES = 4


def plan(mesh):
    heads_axis = mesh.shape["head"]
    peers = mesh.shape["seq"] * heads_axis // HEADS
    assert mesh.shape["seq"] % peers == 0

    def flat(peer, member):
        return (member // heads_axis * peers + peer) * heads_axis + member % heads_axis

    return peers, flat


def as_tiles(array):
    rows, columns = array.shape
    return array.reshape(rows // TILE, TILE, columns // HEAD_DIM, HEAD_DIM).transpose(0, 2, 1, 3)


def from_tiles(tiles):
    row_tiles, heads = tiles.shape[:2]
    return tiles.transpose(0, 2, 1, 3).reshape(row_tiles * TILE, heads * HEAD_DIM)


def pack_kernel(positions, *refs):
    arrays, (out, place_tile, sems) = refs[:6], refs[6:]
    row_tiles = arrays[0].shape[0]
    copies = []
    for at, array in enumerate(arrays):
        for half in range(row_tiles):
            slot = at * row_tiles + half
            copies.append(pltpu.make_async_copy(array.at[half], out.at[:, slot], sems.at[slot]))
            copies[-1].start()
    token = lax.broadcasted_iota(jnp.int32, (TILE, HEAD_DIM), 0)
    lane = lax.broadcasted_iota(jnp.int32, (TILE, HEAD_DIM), 1)
    token = token + lane // (HEAD_DIM // row_tiles) * TILE
    place = jnp.zeros((TILE, HEAD_DIM), jnp.int32)
    for t in range(row_tiles * TILE):
        place = jnp.where(token == t, positions[t], place)
    place = lax.shift_right_logical(place, lane % PIECES * 8) & 255
    place = place.astype(jnp.float32).astype(jnp.bfloat16)
    for h in range(HEADS):
        place_tile[h] = place
    slot = len(arrays) * row_tiles
    copies.append(pltpu.make_async_copy(place_tile, out.at[:, slot], sems.at[slot]))
    copies[-1].start()
    for copy in copies:
        copy.wait()


def pack(positions, arrays):
    tiles = [as_tiles(array) for array in arrays]
    slots = len(tiles) * tiles[0].shape[0] + 1
    return pl.pallas_call(
        pack_kernel,
        out_shape=jax.ShapeDtypeStruct((HEADS, slots, TILE, HEAD_DIM), jnp.bfloat16),
        in_specs=[pl.BlockSpec(memory_space=pltpu.SMEM)]
        + [pl.BlockSpec(memory_space=pl.ANY)] * len(tiles),
        out_specs=pl.BlockSpec(memory_space=pl.ANY),
        scratch_shapes=[
            pltpu.VMEM((HEADS, TILE, HEAD_DIM), jnp.bfloat16),
            pltpu.SemaphoreType.DMA((slots,)),
        ],
        name="pack",
    )(positions, *tiles)


def dot(a, b, contract):
    return lax.dot_general(a, b, (contract, ((), ())), preferred_element_type=jnp.float32)


def order_of(pair):
    high, low = pair
    return high.astype(jnp.int32) * 65536 + low.astype(jnp.int32)


def attention_kernel(rows, *refs):
    blocks, out = refs[:-1], refs[-1]
    count = HEADS * rows
    scale = HEAD_DIM ** (-0.5)

    def part(ref, at):
        return ref[:, at * rows : (at + 1) * rows, :].reshape(count, HEAD_DIM)

    def places(ref):
        row_tiles = rows // TILE
        packed = ref[:, 6 * rows :, :].astype(jnp.float32)
        lane = lax.broadcasted_iota(jnp.int32, packed.shape, 2)
        span = HEAD_DIM // row_tiles
        split = [jnp.where(lane // span == half, packed, 0.0) for half in range(row_tiles)]
        return jnp.stack(split, axis=1).reshape(count, HEAD_DIM).astype(jnp.bfloat16)

    def weights(shape, axis, first):
        at = lax.broadcasted_iota(jnp.int32, shape, axis) % (HEAD_DIM * TILE // rows)
        chosen = jnp.where(at == first, 1.0, jnp.where(at == first + 1, 256.0, 0.0))
        return chosen.astype(jnp.bfloat16)

    own = blocks[0]
    queries = part(own, 0)
    query_pair = jnp.concatenate([part(own, 3), queries], axis=1)
    own_order = places(own)
    across = (HEAD_DIM, HEAD_DIM)
    query_order = order_of([dot(own_order, weights(across, 0, first), ((1,), (0,))) for first in (2, 0)])
    state = None
    for start in range(0, len(blocks), 2):
        group = blocks[start : start + 2]

        def keyed(at):
            return jnp.concatenate([part(ref, at) for ref in group], axis=0)

        keys, values, key_dot, value_dot = [keyed(at) for at in (1, 2, 4, 5)]
        order = jnp.concatenate([places(ref) for ref in group], axis=0)
        width = keys.shape[0]
        down = (8, HEAD_DIM)
        key_order = order_of([dot(weights(down, 1, first), order, ((1,), (1,))) for first in (2, 0)])
        wide_order = jnp.concatenate([query_order] * (width // HEAD_DIM), axis=1)
        visible = key_order[:1] <= wide_order
        scores = dot(queries, keys, ((1,), (1,))) * scale
        scores = jnp.where(visible, scores, -1e30)
        key_pair = jnp.concatenate([keys, key_dot], axis=1)
        score_tan = dot(query_pair, key_pair, ((1,), (1,))) * scale
        new_max = jnp.max(scores, axis=1, keepdims=True)
        if state is not None:
            new_max = jnp.maximum(new_max, state[0])
        expo = jnp.exp(scores - new_max)
        weighted = expo * score_tan
        total = jnp.sum(expo, axis=1, keepdims=True)
        mass = jnp.sum(weighted, axis=1, keepdims=True)
        expo_low = expo.astype(jnp.bfloat16)
        weighted_low = weighted.astype(jnp.bfloat16)
        mixed = dot(expo_low, values, ((1,), (0,)))
        tangent = dot(
            jnp.concatenate([weighted_low, expo_low], axis=1),
            jnp.concatenate([values, value_dot], axis=0),
            ((1,), (0,)),
        )
        if state is not None:
            shrink = jnp.exp(state[0] - new_max)
            total, mass, mixed, tangent = [
                new + old * shrink for new, old in zip((total, mass, mixed, tangent), state[1:])
            ]
        state = (new_max, total, mass, mixed, tangent)
    _, total, mass, mixed, tangent = state
    inverse = 1.0 / total
    mixed = mixed * inverse
    tangent = tangent * inverse - mass * inverse * mixed
    out[:, :rows, :] = mixed.astype(jnp.bfloat16).reshape(HEADS, rows, HEAD_DIM)
    out[:, rows:, :] = tangent.astype(jnp.bfloat16).reshape(HEADS, rows, HEAD_DIM)


def attention(rows, blocks):
    return pl.pallas_call(
        functools.partial(attention_kernel, rows),
        out_shape=jax.ShapeDtypeStruct((HEADS, 2 * rows, HEAD_DIM), jnp.bfloat16),
        in_specs=[pl.BlockSpec(memory_space=pltpu.VMEM)] * len(blocks),
        out_specs=pl.BlockSpec(memory_space=pltpu.VMEM),
        compiler_params=pltpu.CompilerParams(vmem_limit_bytes=48 * 2**20),
        name="attention",
    )(*blocks)


def unpack_kernel(packed, *refs):
    outs, sems = refs[:2], refs[2]
    row_tiles = outs[0].shape[0]
    copies = []
    for at, out in enumerate(outs):
        for half in range(row_tiles):
            slot = at * row_tiles + half
            copies.append(pltpu.make_async_copy(packed.at[:, slot], out.at[half], sems.at[slot]))
            copies[-1].start()
    for copy in copies:
        copy.wait()


def unpack(packed):
    rows = packed.shape[1] // 2
    tiles = packed.reshape(HEADS, 2 * rows // TILE, TILE, HEAD_DIM)
    shape = jax.ShapeDtypeStruct((rows // TILE, HEADS, TILE, HEAD_DIM), jnp.bfloat16)
    outs = pl.pallas_call(
        unpack_kernel,
        out_shape=(shape, shape),
        in_specs=[pl.BlockSpec(memory_space=pl.ANY)],
        out_specs=[pl.BlockSpec(memory_space=pl.ANY)] * 2,
        scratch_shapes=[pltpu.SemaphoreType.DMA((2 * rows // TILE,))],
        name="unpack",
    )(tiles)
    return tuple(from_tiles(out) for out in outs)


def solution(mesh):
    peers, flat = plan(mesh)
    teams = [[flat(peer, member) for member in range(HEADS)] for peer in range(peers)]

    def swap(value):
        return lax.all_to_all(value, AXES, split_axis=0, concat_axis=0, axis_index_groups=teams, tiled=True)

    def from_peer(value, by):
        pairs = [
            (flat(peer, member), flat((peer + by) % peers, member))
            for peer in range(peers)
            for member in range(HEADS)
        ]
        return lax.ppermute(value, AXES, pairs)

    def local(query_main, key_main, value_main, query_tan, key_tan, value_tan, positions):
        rows = query_main.shape[0]
        arrays = (query_main, key_main, value_main, query_tan, key_tan, value_tan)
        here = swap(pack(positions, arrays))
        here = here.reshape(HEADS, -1, HEAD_DIM)
        blocks = [here] + [from_peer(here, by) for by in range(1, peers)]
        return unpack(swap(attention(rows, blocks)))

    placed = (P(AXES, None),) * 6 + (P(AXES),)
    return jax.shard_map(
        local,
        mesh=mesh,
        in_specs=placed,
        out_specs=(P(AXES, None), P(AXES, None)),
        check_vma=False,
    )
```

```python
import functools

import jax
import jax.numpy as jnp
from jax import lax
from jax.experimental import pallas as pl
from jax.experimental.pallas import tpu as pltpu
from jax.sharding import PartitionSpec as P

HEADS = 16
HEAD_DIM = 128
AXES = ("seq", "head")
TILE = 8
PIECES = 4


def plan(mesh):
    heads_axis = mesh.shape["head"]
    peers = mesh.shape["seq"] * heads_axis // HEADS
    assert mesh.shape["seq"] % peers == 0

    def flat(peer, member):
        return (member // heads_axis * peers + peer) * heads_axis + member % heads_axis

    return peers, flat


def as_tiles(array):
    rows, columns = array.shape
    return array.reshape(rows // TILE, TILE, columns // HEAD_DIM, HEAD_DIM).transpose(0, 2, 1, 3)


def from_tiles(tiles):
    row_tiles, heads = tiles.shape[:2]
    return tiles.transpose(0, 2, 1, 3).reshape(row_tiles * TILE, heads * HEAD_DIM)


def pack_kernel(positions, *refs):
    arrays, (out, sems) = refs[:6], refs[6:]
    row_tiles = arrays[0].shape[0]
    copies = []
    for at, array in enumerate(arrays):
        for half in range(row_tiles):
            slot = at * row_tiles + half
            copies.append(pltpu.make_async_copy(array.at[half], out.at[:, slot], sems.at[slot]))
            copies[-1].start()
    token = lax.broadcasted_iota(jnp.int32, (TILE, HEAD_DIM), 0)
    lane = lax.broadcasted_iota(jnp.int32, (TILE, HEAD_DIM), 1)
    token = token + lane // (HEAD_DIM // row_tiles) * TILE
    place = jnp.zeros((TILE, HEAD_DIM), jnp.int32)
    for t in range(row_tiles * TILE):
        place = jnp.where(token == t, positions[t], place)
    place = lax.shift_right_logical(place, lane % PIECES * 8) & 255
    place = place.astype(jnp.float32).astype(jnp.bfloat16)
    for h in range(HEADS):
        out[h, len(arrays) * row_tiles] = place
    for copy in copies:
        copy.wait()


def pack(positions, arrays):
    tiles = [as_tiles(array) for array in arrays]
    slots = len(tiles) * tiles[0].shape[0] + 1
    return pl.pallas_call(
        pack_kernel,
        out_shape=jax.ShapeDtypeStruct((HEADS, slots, TILE, HEAD_DIM), jnp.bfloat16),
        in_specs=[pl.BlockSpec(memory_space=pltpu.SMEM)]
        + [pl.BlockSpec(memory_space=pltpu.HBM)] * len(tiles),
        out_specs=pl.BlockSpec(memory_space=pltpu.VMEM),
        scratch_shapes=[pltpu.SemaphoreType.DMA((slots - 1,))],
        compiler_params=pltpu.CompilerParams(vmem_limit_bytes=4 * 2**20),
        name="pack",
    )(positions, *tiles)


def dot(a, b, contract):
    return lax.dot_general(a, b, (contract, ((), ())), preferred_element_type=jnp.float32)


def order_of(pair):
    high, low = pair
    return high.astype(jnp.int32) * 65536 + low.astype(jnp.int32)


def attention_kernel(rows, *refs):
    blocks, out = refs[:-1], refs[-1]
    count = HEADS * rows
    scale = HEAD_DIM ** (-0.5)

    def part(ref, at):
        return ref[:, at * rows : (at + 1) * rows, :].reshape(count, HEAD_DIM)

    def places(ref):
        row_tiles = rows // TILE
        packed = ref[:, 6 * rows :, :].astype(jnp.float32)
        lane = lax.broadcasted_iota(jnp.int32, packed.shape, 2)
        span = HEAD_DIM // row_tiles
        split = [jnp.where(lane // span == half, packed, 0.0) for half in range(row_tiles)]
        return jnp.stack(split, axis=1).reshape(count, HEAD_DIM).astype(jnp.bfloat16)

    def weights(shape, axis, first):
        at = lax.broadcasted_iota(jnp.int32, shape, axis) % (HEAD_DIM * TILE // rows)
        chosen = jnp.where(at == first, 1.0, jnp.where(at == first + 1, 256.0, 0.0))
        return chosen.astype(jnp.bfloat16)

    own = blocks[0]
    queries = part(own, 0)
    query_pair = jnp.concatenate([part(own, 3), queries], axis=1)
    own_order = places(own)
    across = (HEAD_DIM, HEAD_DIM)
    query_order = order_of([dot(own_order, weights(across, 0, first), ((1,), (0,))) for first in (2, 0)])
    state = None
    for start in range(0, len(blocks), 2):
        group = blocks[start : start + 2]

        def keyed(at):
            return jnp.concatenate([part(ref, at) for ref in group], axis=0)

        keys, values, key_dot, value_dot = [keyed(at) for at in (1, 2, 4, 5)]
        order = jnp.concatenate([places(ref) for ref in group], axis=0)
        width = keys.shape[0]
        down = (8, HEAD_DIM)
        key_order = order_of([dot(weights(down, 1, first), order, ((1,), (1,))) for first in (2, 0)])
        wide_order = jnp.concatenate([query_order] * (width // HEAD_DIM), axis=1)
        visible = key_order[:1] <= wide_order
        scores = dot(queries, keys, ((1,), (1,))) * scale
        scores = jnp.where(visible, scores, -1e30)
        key_pair = jnp.concatenate([keys, key_dot], axis=1)
        score_tan = dot(query_pair, key_pair, ((1,), (1,))) * scale
        new_max = jnp.max(scores, axis=1, keepdims=True)
        if state is not None:
            new_max = jnp.maximum(new_max, state[0])
        expo = jnp.exp(scores - new_max)
        weighted = expo * score_tan
        total = jnp.sum(expo, axis=1, keepdims=True)
        mass = jnp.sum(weighted, axis=1, keepdims=True)
        expo_low = expo.astype(jnp.bfloat16)
        weighted_low = weighted.astype(jnp.bfloat16)
        mixed = dot(expo_low, values, ((1,), (0,)))
        tangent = dot(
            jnp.concatenate([weighted_low, expo_low], axis=1),
            jnp.concatenate([values, value_dot], axis=0),
            ((1,), (0,)),
        )
        if state is not None:
            shrink = jnp.exp(state[0] - new_max)
            total, mass, mixed, tangent = [
                new + old * shrink for new, old in zip((total, mass, mixed, tangent), state[1:])
            ]
        state = (new_max, total, mass, mixed, tangent)
    _, total, mass, mixed, tangent = state
    inverse = 1.0 / total
    mixed = mixed * inverse
    tangent = tangent * inverse - mass * inverse * mixed
    out[:, :rows, :] = mixed.astype(jnp.bfloat16).reshape(HEADS, rows, HEAD_DIM)
    out[:, rows:, :] = tangent.astype(jnp.bfloat16).reshape(HEADS, rows, HEAD_DIM)


def attention(rows, blocks):
    return pl.pallas_call(
        functools.partial(attention_kernel, rows),
        out_shape=jax.ShapeDtypeStruct((HEADS, 2 * rows, HEAD_DIM), jnp.bfloat16),
        in_specs=[pl.BlockSpec(memory_space=pltpu.VMEM)] * len(blocks),
        out_specs=pl.BlockSpec(memory_space=pltpu.VMEM),
        compiler_params=pltpu.CompilerParams(vmem_limit_bytes=(8 + len(blocks)) * 2**20),
        name="attention",
    )(*blocks)


def unpack_kernel(packed, *refs):
    outs, sems = refs[:2], refs[2]
    row_tiles = outs[0].shape[0]
    copies = []
    for at, out in enumerate(outs):
        for half in range(row_tiles):
            slot = at * row_tiles + half
            copies.append(pltpu.make_async_copy(packed.at[:, slot], out.at[half], sems.at[slot]))
            copies[-1].start()
    for copy in copies:
        copy.wait()


def unpack(packed):
    rows = packed.shape[1] // 2
    tiles = packed.reshape(HEADS, 2 * rows // TILE, TILE, HEAD_DIM)
    shape = jax.ShapeDtypeStruct((rows // TILE, HEADS, TILE, HEAD_DIM), jnp.bfloat16)
    outs = pl.pallas_call(
        unpack_kernel,
        out_shape=(shape, shape),
        in_specs=[pl.BlockSpec(memory_space=pltpu.VMEM)],
        out_specs=[pl.BlockSpec(memory_space=pltpu.HBM)] * 2,
        scratch_shapes=[pltpu.SemaphoreType.DMA((2 * rows // TILE,))],
        compiler_params=pltpu.CompilerParams(vmem_limit_bytes=4 * 2**20),
        name="unpack",
    )(tiles)
    return tuple(from_tiles(out) for out in outs)


def solution(mesh):
    peers, flat = plan(mesh)
    teams = [[flat(peer, member) for member in range(HEADS)] for peer in range(peers)]

    def swap(value):
        return lax.all_to_all(value, AXES, split_axis=0, concat_axis=0, axis_index_groups=teams, tiled=True)

    def from_peer(value, by):
        pairs = [
            (flat(peer, member), flat((peer + by) % peers, member))
            for peer in range(peers)
            for member in range(HEADS)
        ]
        return lax.ppermute(value, AXES, pairs)

    def local(query_main, key_main, value_main, query_tan, key_tan, value_tan, positions):
        rows = query_main.shape[0]
        arrays = (query_main, key_main, value_main, query_tan, key_tan, value_tan)
        here = swap(pack(positions, arrays))
        here = here.reshape(HEADS, -1, HEAD_DIM)
        blocks = [here] + [from_peer(here, by) for by in range(1, peers)]
        return unpack(swap(attention(rows, blocks)))

    placed = (P(AXES, None),) * 6 + (P(AXES),)
    return jax.shard_map(
        local,
        mesh=mesh,
        in_specs=placed,
        out_specs=(P(AXES, None), P(AXES, None)),
        check_vma=False,
    )
```

```python
import functools

import jax
import jax.numpy as jnp
from jax import lax
from jax.experimental import pallas as pl
from jax.experimental.pallas import tpu as pltpu
from jax.sharding import PartitionSpec as P

HEADS = 16
HEAD_DIM = 128
AXES = ("seq", "head")
TILE = 8
PIECES = 4


def plan(mesh):
    heads_axis = mesh.shape["head"]
    peers = mesh.shape["seq"] * heads_axis // HEADS
    assert mesh.shape["seq"] % peers == 0

    def flat(peer, member):
        return (member // heads_axis * peers + peer) * heads_axis + member % heads_axis

    return peers, flat


def as_tiles(array):
    rows, columns = array.shape
    return array.reshape(rows // TILE, TILE, columns // HEAD_DIM, HEAD_DIM).transpose(0, 2, 1, 3)


def from_tiles(tiles):
    row_tiles, heads = tiles.shape[:2]
    return tiles.transpose(0, 2, 1, 3).reshape(row_tiles * TILE, heads * HEAD_DIM)


def pack_kernel(positions, *refs):
    arrays, (out, sems) = refs[:6], refs[6:]
    row_tiles = arrays[0].shape[0]
    copies = []
    for at, array in enumerate(arrays):
        for half in range(row_tiles):
            slot = at * row_tiles + half
            copies.append(pltpu.make_async_copy(array.at[half], out.at[:, slot], sems.at[slot]))
            copies[-1].start()
    token = lax.broadcasted_iota(jnp.int32, (TILE, HEAD_DIM), 0)
    lane = lax.broadcasted_iota(jnp.int32, (TILE, HEAD_DIM), 1)
    token = token + lane // (HEAD_DIM // row_tiles) * TILE
    place = jnp.zeros((TILE, HEAD_DIM), jnp.int32)
    for t in range(row_tiles * TILE):
        place = jnp.where(token == t, positions[t], place)
    place = lax.shift_right_logical(place, lane % PIECES * 8) & 255
    place = place.astype(jnp.float32).astype(jnp.bfloat16)
    for h in range(HEADS):
        out[h, len(arrays) * row_tiles] = place
    for copy in copies:
        copy.wait()


def pack(positions, arrays):
    tiles = [as_tiles(array) for array in arrays]
    slots = len(tiles) * tiles[0].shape[0] + 1
    return pl.pallas_call(
        pack_kernel,
        out_shape=pltpu.VMEM((HEADS, slots, TILE, HEAD_DIM), jnp.bfloat16),
        in_specs=[pl.BlockSpec(memory_space=pltpu.SMEM)]
        + [pl.BlockSpec(memory_space=pltpu.HBM)] * len(tiles),
        out_specs=pl.BlockSpec(memory_space=pltpu.VMEM),
        scratch_shapes=[pltpu.SemaphoreType.DMA((slots - 1,))],
        compiler_params=pltpu.CompilerParams(vmem_limit_bytes=56 * 2**20),
        name="pack",
    )(positions, *tiles)


def dot(a, b, contract):
    return lax.dot_general(a, b, (contract, ((), ())), preferred_element_type=jnp.float32)


def order_of(pair):
    high, low = pair
    return high.astype(jnp.int32) * 65536 + low.astype(jnp.int32)


def attention_kernel(rows, *refs):
    blocks, out = refs[:-1], refs[-1]
    count = HEADS * rows
    scale = HEAD_DIM ** (-0.5)

    def part(ref, at):
        return ref[:, at * rows : (at + 1) * rows, :].reshape(count, HEAD_DIM)

    def places(ref):
        row_tiles = rows // TILE
        packed = ref[:, 6 * rows :, :].astype(jnp.float32)
        lane = lax.broadcasted_iota(jnp.int32, packed.shape, 2)
        span = HEAD_DIM // row_tiles
        split = [jnp.where(lane // span == half, packed, 0.0) for half in range(row_tiles)]
        return jnp.stack(split, axis=1).reshape(count, HEAD_DIM).astype(jnp.bfloat16)

    def weights(shape, axis, first):
        at = lax.broadcasted_iota(jnp.int32, shape, axis) % (HEAD_DIM * TILE // rows)
        chosen = jnp.where(at == first, 1.0, jnp.where(at == first + 1, 256.0, 0.0))
        return chosen.astype(jnp.bfloat16)

    own = blocks[0]
    queries = part(own, 0)
    query_pair = jnp.concatenate([part(own, 3), queries], axis=1)
    own_order = places(own)
    across = (HEAD_DIM, HEAD_DIM)
    query_order = order_of([dot(own_order, weights(across, 0, first), ((1,), (0,))) for first in (2, 0)])
    state = None
    for start in range(0, len(blocks), 2):
        group = blocks[start : start + 2]

        def keyed(at):
            return jnp.concatenate([part(ref, at) for ref in group], axis=0)

        keys, values, key_dot, value_dot = [keyed(at) for at in (1, 2, 4, 5)]
        order = jnp.concatenate([places(ref) for ref in group], axis=0)
        width = keys.shape[0]
        down = (8, HEAD_DIM)
        key_order = order_of([dot(weights(down, 1, first), order, ((1,), (1,))) for first in (2, 0)])
        wide_order = jnp.concatenate([query_order] * (width // HEAD_DIM), axis=1)
        visible = key_order[:1] <= wide_order
        scores = dot(queries, keys, ((1,), (1,))) * scale
        scores = jnp.where(visible, scores, -1e30)
        key_pair = jnp.concatenate([keys, key_dot], axis=1)
        score_tan = dot(query_pair, key_pair, ((1,), (1,))) * scale
        new_max = jnp.max(scores, axis=1, keepdims=True)
        if state is not None:
            new_max = jnp.maximum(new_max, state[0])
        expo = jnp.exp(scores - new_max)
        weighted = expo * score_tan
        total = jnp.sum(expo, axis=1, keepdims=True)
        mass = jnp.sum(weighted, axis=1, keepdims=True)
        expo_low = expo.astype(jnp.bfloat16)
        weighted_low = weighted.astype(jnp.bfloat16)
        mixed = dot(expo_low, values, ((1,), (0,)))
        tangent = dot(
            jnp.concatenate([weighted_low, expo_low], axis=1),
            jnp.concatenate([values, value_dot], axis=0),
            ((1,), (0,)),
        )
        if state is not None:
            shrink = jnp.exp(state[0] - new_max)
            total, mass, mixed, tangent = [
                new + old * shrink for new, old in zip((total, mass, mixed, tangent), state[1:])
            ]
        state = (new_max, total, mass, mixed, tangent)
    _, total, mass, mixed, tangent = state
    inverse = 1.0 / total
    mixed = mixed * inverse
    tangent = tangent * inverse - mass * inverse * mixed
    out[:, :rows, :] = mixed.astype(jnp.bfloat16).reshape(HEADS, rows, HEAD_DIM)
    out[:, rows:, :] = tangent.astype(jnp.bfloat16).reshape(HEADS, rows, HEAD_DIM)


def attention(rows, blocks):
    return pl.pallas_call(
        functools.partial(attention_kernel, rows),
        out_shape=jax.ShapeDtypeStruct((HEADS, 2 * rows, HEAD_DIM), jnp.bfloat16),
        in_specs=[pl.BlockSpec(memory_space=pltpu.VMEM)] * len(blocks),
        out_specs=pl.BlockSpec(memory_space=pltpu.VMEM),
        compiler_params=pltpu.CompilerParams(vmem_limit_bytes=(8 + len(blocks)) * 2**20),
        name="attention",
    )(*blocks)


def unpack_kernel(packed, *refs):
    outs, sems = refs[:2], refs[2]
    row_tiles = outs[0].shape[0]
    copies = []
    for at, out in enumerate(outs):
        for half in range(row_tiles):
            slot = at * row_tiles + half
            copies.append(pltpu.make_async_copy(packed.at[:, slot], out.at[half], sems.at[slot]))
            copies[-1].start()
    for copy in copies:
        copy.wait()


def unpack(packed):
    rows = packed.shape[1] // 2
    tiles = packed.reshape(HEADS, 2 * rows // TILE, TILE, HEAD_DIM)
    shape = jax.ShapeDtypeStruct((rows // TILE, HEADS, TILE, HEAD_DIM), jnp.bfloat16)
    outs = pl.pallas_call(
        unpack_kernel,
        out_shape=(shape, shape),
        in_specs=[pl.BlockSpec(memory_space=pltpu.VMEM)],
        out_specs=[pl.BlockSpec(memory_space=pltpu.HBM)] * 2,
        scratch_shapes=[pltpu.SemaphoreType.DMA((2 * rows // TILE,))],
        compiler_params=pltpu.CompilerParams(vmem_limit_bytes=4 * 2**20),
        name="unpack",
    )(tiles)
    return tuple(from_tiles(out) for out in outs)


def solution(mesh):
    peers, flat = plan(mesh)
    teams = [[flat(peer, member) for member in range(HEADS)] for peer in range(peers)]

    def swap(value):
        return lax.all_to_all(value, AXES, split_axis=0, concat_axis=0, axis_index_groups=teams, tiled=True)

    def from_peer(value, by):
        pairs = [
            (flat(peer, member), flat((peer + by) % peers, member))
            for peer in range(peers)
            for member in range(HEADS)
        ]
        return lax.ppermute(value, AXES, pairs)

    def local(query_main, key_main, value_main, query_tan, key_tan, value_tan, positions):
        rows = query_main.shape[0]
        arrays = (query_main, key_main, value_main, query_tan, key_tan, value_tan)
        here = swap(pack(positions, arrays))
        here = here.reshape(HEADS, -1, HEAD_DIM)
        blocks = [here] + [from_peer(here, by) for by in range(1, peers)]
        return unpack(swap(attention(rows, blocks)))

    placed = (P(AXES, None),) * 6 + (P(AXES),)
    return jax.shard_map(
        local,
        mesh=mesh,
        in_specs=placed,
        out_specs=(P(AXES, None), P(AXES, None)),
        check_vma=False,
    )
```

```python
import functools

import jax
import jax.numpy as jnp
from jax import lax
from jax.experimental import pallas as pl
from jax.experimental.pallas import tpu as pltpu
from jax.sharding import PartitionSpec as P

HEADS = 16
HEAD_DIM = 128
AXES = ("seq", "head")
TILE = 8
PIECES = 4


def plan(mesh, rows):
    heads_axis = mesh.shape["head"]
    peers = mesh.shape["seq"] * heads_axis // HEADS
    assert mesh.shape["seq"] % peers == 0 and rows % TILE == 0
    split = peers if peers == rows // TILE else 1

    def flat(peer, member):
        return (member // heads_axis * peers + peer) * heads_axis + member % heads_axis

    return peers, split, flat


def as_tiles(array, heads_axis):
    rows, columns = array.shape
    tiles = array.reshape(rows // TILE, TILE, columns // HEAD_DIM, HEAD_DIM).transpose(0, 2, 1, 3)
    return tiles.reshape(rows // TILE, -1, heads_axis, TILE, HEAD_DIM)


def from_tiles(tiles):
    tiles = tiles.reshape(tiles.shape[0], -1, TILE, HEAD_DIM)
    row_tiles, heads = tiles.shape[:2]
    return tiles.transpose(0, 2, 1, 3).reshape(row_tiles * TILE, heads * HEAD_DIM)


def slot_of(at, row_tile, row_tiles, split):
    own = row_tiles // split
    return row_tile // own, at * own + row_tile % own


def pack_kernel(positions, *refs):
    arrays, (out, here, sems) = refs[:6], refs[6:]
    row_tiles = arrays[0].shape[0]
    groups, split, heads_axis = out.shape[:3]
    load = pltpu.make_async_copy(positions, here, sems.at[6 * row_tiles])
    load.start()
    copies = []
    for at, array in enumerate(arrays):
        for row_tile in range(row_tiles):
            part, slot = slot_of(at, row_tile, row_tiles, split)
            sem = sems.at[len(copies)]
            copies.append(pltpu.make_async_copy(array.at[row_tile], out.at[:, part, :, slot], sem))
            copies[-1].start()
    own = row_tiles // split
    token = lax.broadcasted_iota(jnp.int32, (TILE, HEAD_DIM), 0)
    lane = lax.broadcasted_iota(jnp.int32, (TILE, HEAD_DIM), 1)
    token = token + lane // (HEAD_DIM // own) * TILE
    load.wait()
    for part in range(split):
        place = jnp.zeros((TILE, HEAD_DIM), jnp.int32)
        for t in range(own * TILE):
            place = jnp.where(token == t, here[part * own * TILE + t], place)
        place = lax.shift_right_logical(place, lane % PIECES * 8) & 255
        place = place.astype(jnp.float32).astype(jnp.bfloat16)
        for group in range(groups):
            for h in range(heads_axis):
                out[group, part, h, 6 * own] = place
    for copy in copies:
        copy.wait()


def pack(positions, arrays, split, heads_axis):
    tiles = [as_tiles(array, heads_axis) for array in arrays]
    row_tiles, groups = tiles[0].shape[:2]
    shape = (groups, split, heads_axis, 6 * row_tiles // split + 1, TILE, HEAD_DIM)
    return pl.pallas_call(
        pack_kernel,
        out_shape=pltpu.VMEM(shape, jnp.bfloat16),
        in_specs=[pl.BlockSpec(memory_space=pltpu.HBM)] * (1 + len(tiles)),
        out_specs=pl.BlockSpec(memory_space=pltpu.VMEM),
        scratch_shapes=[
            pltpu.SMEM(positions.shape, jnp.int32),
            pltpu.SemaphoreType.DMA((6 * row_tiles + 1,)),
        ],
        compiler_params=pltpu.CompilerParams(vmem_limit_bytes=56 * 2**20),
        name="pack",
    )(positions, *tiles)


def dot(a, b, contract):
    return lax.dot_general(a, b, (contract, ((), ())), preferred_element_type=jnp.float32)


def order_of(pair):
    high, low = pair
    return high.astype(jnp.int32) * 65536 + low.astype(jnp.int32)


def attention_kernel(rows, *refs):
    blocks, out = refs[:-1], refs[-1]
    sources = blocks[0].shape[0]
    count = sources * rows
    scale = HEAD_DIM ** (-0.5)

    def part(ref, at):
        return ref[:, at * rows : (at + 1) * rows, :].reshape(count, HEAD_DIM)

    def places(ref):
        row_tiles = rows // TILE
        packed = ref[:, 6 * rows :, :]
        if row_tiles == 1:
            return packed.reshape(count, HEAD_DIM)
        packed = packed.astype(jnp.float32)
        lane = lax.broadcasted_iota(jnp.int32, packed.shape, 2)
        span = HEAD_DIM // row_tiles
        split = [jnp.where(lane // span == half, packed, 0.0) for half in range(row_tiles)]
        return jnp.stack(split, axis=1).reshape(count, HEAD_DIM).astype(jnp.bfloat16)

    def weights(shape, axis, first):
        at = lax.broadcasted_iota(jnp.int32, shape, axis) % (HEAD_DIM * TILE // rows)
        chosen = jnp.where(at == first, 1.0, jnp.where(at == first + 1, 256.0, 0.0))
        return chosen.astype(jnp.bfloat16)

    own = blocks[0]
    queries = part(own, 0)
    query_pair = jnp.concatenate([part(own, 3), queries], axis=1)
    own_order = places(own)
    across = (HEAD_DIM, HEAD_DIM)
    query_order = order_of([dot(own_order, weights(across, 0, first), ((1,), (0,))) for first in (2, 0)])
    state = None
    for start in range(0, len(blocks), 2):
        group = blocks[start : start + 2]

        def keyed(at):
            return jnp.concatenate([part(ref, at) for ref in group], axis=0)

        keys, values, key_dot, value_dot = [keyed(at) for at in (1, 2, 4, 5)]
        order = jnp.concatenate([places(ref) for ref in group], axis=0)
        width = keys.shape[0]
        down = (8, HEAD_DIM)
        key_order = order_of([dot(weights(down, 1, first), order, ((1,), (1,))) for first in (2, 0)])
        wide_order = jnp.concatenate([query_order] * (width // HEAD_DIM), axis=1)
        visible = key_order[:1] <= wide_order
        scores = dot(queries, keys, ((1,), (1,))) * scale
        scores = jnp.where(visible, scores, -1e30)
        key_pair = jnp.concatenate([keys, key_dot], axis=1)
        score_tan = dot(query_pair, key_pair, ((1,), (1,))) * scale
        new_max = jnp.max(scores, axis=1, keepdims=True)
        if state is not None:
            new_max = jnp.maximum(new_max, state[0])
        expo = jnp.exp(scores - new_max)
        weighted = expo * score_tan
        total = jnp.sum(expo, axis=1, keepdims=True)
        mass = jnp.sum(weighted, axis=1, keepdims=True)
        expo_low = expo.astype(jnp.bfloat16)
        weighted_low = weighted.astype(jnp.bfloat16)
        mixed = dot(expo_low, values, ((1,), (0,)))
        tangent = dot(
            jnp.concatenate([weighted_low, expo_low], axis=1),
            jnp.concatenate([values, value_dot], axis=0),
            ((1,), (0,)),
        )
        if state is not None:
            shrink = jnp.exp(state[0] - new_max)
            total, mass, mixed, tangent = [
                new + old * shrink for new, old in zip((total, mass, mixed, tangent), state[1:])
            ]
        state = (new_max, total, mass, mixed, tangent)
    _, total, mass, mixed, tangent = state
    inverse = 1.0 / total
    mixed = mixed * inverse
    tangent = tangent * inverse - mass * inverse * mixed
    out[:, :rows, :] = mixed.astype(jnp.bfloat16).reshape(sources, rows, HEAD_DIM)
    out[:, rows:, :] = tangent.astype(jnp.bfloat16).reshape(sources, rows, HEAD_DIM)


def attention(rows, blocks):
    return pl.pallas_call(
        functools.partial(attention_kernel, rows),
        out_shape=jax.ShapeDtypeStruct((blocks[0].shape[0], 2 * rows, HEAD_DIM), jnp.bfloat16),
        in_specs=[pl.BlockSpec(memory_space=pltpu.VMEM)] * len(blocks),
        out_specs=pl.BlockSpec(memory_space=pltpu.VMEM),
        compiler_params=pltpu.CompilerParams(vmem_limit_bytes=(8 + len(blocks)) * 2**20),
        name="attention",
    )(*blocks)


def unpack_kernel(packed, *refs):
    outs, sems = refs[:2], refs[2]
    row_tiles = outs[0].shape[0]
    copies = []
    for at, out in enumerate(outs):
        for row_tile in range(row_tiles):
            part, slot = slot_of(at, row_tile, row_tiles, packed.shape[1])
            sem = sems.at[len(copies)]
            copies.append(pltpu.make_async_copy(packed.at[:, part, :, slot], out.at[row_tile], sem))
            copies[-1].start()
    for copy in copies:
        copy.wait()


def unpack(packed, split, heads_axis):
    tiles = packed.reshape(HEADS // heads_axis, split, heads_axis, -1, TILE, HEAD_DIM)
    row_tiles = tiles.shape[3] * split // 2
    shape = (row_tiles, HEADS // heads_axis, heads_axis, TILE, HEAD_DIM)
    outs = pl.pallas_call(
        unpack_kernel,
        out_shape=[jax.ShapeDtypeStruct(shape, jnp.bfloat16)] * 2,
        in_specs=[pl.BlockSpec(memory_space=pltpu.VMEM)],
        out_specs=[pl.BlockSpec(memory_space=pltpu.HBM)] * 2,
        scratch_shapes=[pltpu.SemaphoreType.DMA((2 * row_tiles,))],
        compiler_params=pltpu.CompilerParams(vmem_limit_bytes=4 * 2**20),
        name="unpack",
    )(tiles)
    return tuple(from_tiles(out) for out in outs)


def solution(mesh):
    heads_axis = mesh.shape["head"]

    def local(query_main, key_main, value_main, query_tan, key_tan, value_tan, positions):
        rows = query_main.shape[0]
        peers, split, flat = plan(mesh, rows)
        teams = [[flat(peer, member) for member in range(HEADS)] for peer in range(peers)]

        def swap(value):
            groups = teams if split == 1 else None
            return lax.all_to_all(value, AXES, 0, 0, axis_index_groups=groups, tiled=True)

        def from_peer(value, by):
            pairs = [
                (flat(peer, member), flat((peer + by) % peers, member))
                for peer in range(peers)
                for member in range(HEADS)
            ]
            return lax.ppermute(value, AXES, pairs)

        arrays = (query_main, key_main, value_main, query_tan, key_tan, value_tan)
        packed = pack(positions, arrays, split, heads_axis)
        here = swap(packed.reshape(HEADS * split, -1, HEAD_DIM))
        blocks = [here] + [from_peer(here, by) for by in range(1, peers)]
        return unpack(swap(attention(rows // split, blocks)), split, heads_axis)

    placed = (P(AXES, None),) * 6 + (P(AXES),)
    return jax.shard_map(
        local,
        mesh=mesh,
        in_specs=placed,
        out_specs=(P(AXES, None), P(AXES, None)),
        check_vma=False,
    )
```

```python
import functools

import jax
import jax.numpy as jnp
from jax import lax
from jax.experimental import pallas as pl
from jax.experimental.pallas import tpu as pltpu
from jax.sharding import PartitionSpec as P

HEADS = 16
HEAD_DIM = 128
AXES = ("seq", "head")
TILE = 8
PIECES = 4


def plan(mesh, rows):
    heads_axis = mesh.shape["head"]
    peers = mesh.shape["seq"] * heads_axis // HEADS
    assert mesh.shape["seq"] % peers == 0 and rows % TILE == 0
    split = peers if peers == rows // TILE else 1

    def flat(peer, member):
        return (member // heads_axis * peers + peer) * heads_axis + member % heads_axis

    return peers, split, flat


def as_tiles(array, heads_axis):
    rows, columns = array.shape
    tiles = array.reshape(rows // TILE, TILE, columns // HEAD_DIM, HEAD_DIM).transpose(0, 2, 1, 3)
    return tiles.reshape(rows // TILE, -1, heads_axis, TILE, HEAD_DIM)


def from_tiles(tiles):
    tiles = tiles.reshape(tiles.shape[0], -1, TILE, HEAD_DIM)
    row_tiles, heads = tiles.shape[:2]
    return tiles.transpose(0, 2, 1, 3).reshape(row_tiles * TILE, heads * HEAD_DIM)


def slot_of(at, row_tile, row_tiles, split):
    own = row_tiles // split
    return row_tile // own, at * own + row_tile % own


def pack_kernel(positions, *refs):
    arrays, (out, places, here, sems) = refs[:6], refs[6:]
    row_tiles = arrays[0].shape[0]
    load = pltpu.make_async_copy(positions, here, sems.at[6 * row_tiles])
    load.start()
    copies = []
    for at, array in enumerate(arrays):
        for row_tile in range(row_tiles):
            part, slot = slot_of(at, row_tile, row_tiles, out.shape[1])
            sem = sems.at[len(copies)]
            copies.append(pltpu.make_async_copy(array.at[row_tile], out.at[:, part, :, slot], sem))
            copies[-1].start()
    token = lax.broadcasted_iota(jnp.int32, (TILE, HEAD_DIM), 0)
    lane = lax.broadcasted_iota(jnp.int32, (TILE, HEAD_DIM), 1)
    token = token + lane // (HEAD_DIM // row_tiles) * TILE
    place = jnp.zeros((TILE, HEAD_DIM), jnp.int32)
    load.wait()
    for t in range(row_tiles * TILE):
        place = jnp.where(token == t, here[t], place)
    place = lax.shift_right_logical(place, lane % PIECES * 8) & 255
    places[...] = place.astype(jnp.float32).astype(jnp.bfloat16)
    for copy in copies:
        copy.wait()


def pack(positions, arrays, split, heads_axis):
    tiles = [as_tiles(array, heads_axis) for array in arrays]
    row_tiles, groups = tiles[0].shape[:2]
    shape = (groups, split, heads_axis, 6 * row_tiles // split, TILE, HEAD_DIM)
    return pl.pallas_call(
        pack_kernel,
        out_shape=(
            pltpu.VMEM(shape, jnp.bfloat16),
            jax.ShapeDtypeStruct((TILE, HEAD_DIM), jnp.bfloat16),
        ),
        in_specs=[pl.BlockSpec(memory_space=pltpu.HBM)] * (1 + len(tiles)),
        out_specs=[pl.BlockSpec(memory_space=pltpu.VMEM)] * 2,
        scratch_shapes=[
            pltpu.SMEM(positions.shape, jnp.int32),
            pltpu.SemaphoreType.DMA((6 * row_tiles + 1,)),
        ],
        compiler_params=pltpu.CompilerParams(vmem_limit_bytes=56 * 2**20),
        name="pack",
    )(positions, *tiles)


def dot(a, b, contract):
    return lax.dot_general(a, b, (contract, ((), ())), preferred_element_type=jnp.float32)


def order_of(pair):
    high, low = pair
    return high.astype(jnp.int32) * 65536 + low.astype(jnp.int32)


def attention_kernel(rows, split, everyone, *refs):
    blocks, out = refs[:-1], refs[-1]
    peers = len(blocks)
    sources = blocks[0].shape[0]
    count = sources * rows
    scale = HEAD_DIM ** (-0.5)

    def part(ref, at):
        return ref[:, at * rows : (at + 1) * rows, :].reshape(count, HEAD_DIM)

    def places(by):
        peer = lax.rem(lax.axis_index("seq") + by, peers)
        span = HEAD_DIM // (rows * split // TILE)
        if split > 1:
            packed = everyone[...].reshape(count, HEAD_DIM).astype(jnp.float32)
            lane = lax.broadcasted_iota(jnp.int32, packed.shape, 1)
            return jnp.where(lane // span == peer, packed, 0.0).astype(jnp.bfloat16)
        packed = everyone[:, pl.ds(peer, 1)].reshape(sources, TILE, HEAD_DIM).astype(jnp.float32)
        lane = lax.broadcasted_iota(jnp.int32, packed.shape, 2)
        parts = [jnp.where(lane // span == at, packed, 0.0) for at in range(rows // TILE)]
        return jnp.stack(parts, axis=1).reshape(count, HEAD_DIM).astype(jnp.bfloat16)

    def weights(shape, axis, first):
        at = lax.broadcasted_iota(jnp.int32, shape, axis) % (HEAD_DIM * TILE // (rows * split))
        chosen = jnp.where(at == first, 1.0, jnp.where(at == first + 1, 256.0, 0.0))
        return chosen.astype(jnp.bfloat16)

    own = blocks[0]
    queries = part(own, 0)
    query_pair = jnp.concatenate([part(own, 3), queries], axis=1)
    own_order = places(0)
    across = (HEAD_DIM, HEAD_DIM)
    query_order = order_of([dot(own_order, weights(across, 0, first), ((1,), (0,))) for first in (2, 0)])
    state = None
    for start in range(0, len(blocks), 2):
        group = blocks[start : start + 2]

        def keyed(at):
            return jnp.concatenate([part(ref, at) for ref in group], axis=0)

        keys, values, key_dot, value_dot = [keyed(at) for at in (1, 2, 4, 5)]
        order = [places(by) for by in range(start, start + len(group))]
        order = jnp.concatenate(order, axis=0)
        width = keys.shape[0]
        down = (8, HEAD_DIM)
        key_order = order_of([dot(weights(down, 1, first), order, ((1,), (1,))) for first in (2, 0)])
        wide_order = jnp.concatenate([query_order] * (width // HEAD_DIM), axis=1)
        visible = key_order[:1] <= wide_order
        scores = dot(queries, keys, ((1,), (1,))) * scale
        scores = jnp.where(visible, scores, -1e30)
        key_pair = jnp.concatenate([keys, key_dot], axis=1)
        score_tan = dot(query_pair, key_pair, ((1,), (1,))) * scale
        new_max = jnp.max(scores, axis=1, keepdims=True)
        if state is not None:
            new_max = jnp.maximum(new_max, state[0])
        expo = jnp.exp(scores - new_max)
        weighted = expo * score_tan
        total = jnp.sum(expo, axis=1, keepdims=True)
        mass = jnp.sum(weighted, axis=1, keepdims=True)
        expo_low = expo.astype(jnp.bfloat16)
        weighted_low = weighted.astype(jnp.bfloat16)
        mixed = dot(expo_low, values, ((1,), (0,)))
        tangent = dot(
            jnp.concatenate([weighted_low, expo_low], axis=1),
            jnp.concatenate([values, value_dot], axis=0),
            ((1,), (0,)),
        )
        if state is not None:
            shrink = jnp.exp(state[0] - new_max)
            total, mass, mixed, tangent = [
                new + old * shrink for new, old in zip((total, mass, mixed, tangent), state[1:])
            ]
        state = (new_max, total, mass, mixed, tangent)
    _, total, mass, mixed, tangent = state
    inverse = 1.0 / total
    mixed = mixed * inverse
    tangent = tangent * inverse - mass * inverse * mixed
    out[:, :rows, :] = mixed.astype(jnp.bfloat16).reshape(sources, rows, HEAD_DIM)
    out[:, rows:, :] = tangent.astype(jnp.bfloat16).reshape(sources, rows, HEAD_DIM)


def attention(rows, split, everyone, blocks):
    return pl.pallas_call(
        functools.partial(attention_kernel, rows, split),
        out_shape=jax.ShapeDtypeStruct((blocks[0].shape[0], 2 * rows, HEAD_DIM), jnp.bfloat16),
        in_specs=[pl.BlockSpec(memory_space=pltpu.VMEM)] * (1 + len(blocks)),
        out_specs=pl.BlockSpec(memory_space=pltpu.VMEM),
        compiler_params=pltpu.CompilerParams(vmem_limit_bytes=(8 + len(blocks)) * 2**20),
        name="attention",
    )(everyone, *blocks)


def unpack_kernel(packed, *refs):
    outs, sems = refs[:2], refs[2]
    row_tiles = outs[0].shape[0]
    copies = []
    for at, out in enumerate(outs):
        for row_tile in range(row_tiles):
            part, slot = slot_of(at, row_tile, row_tiles, packed.shape[1])
            sem = sems.at[len(copies)]
            copies.append(pltpu.make_async_copy(packed.at[:, part, :, slot], out.at[row_tile], sem))
            copies[-1].start()
    for copy in copies:
        copy.wait()


def unpack(packed, split, heads_axis):
    tiles = packed.reshape(HEADS // heads_axis, split, heads_axis, -1, TILE, HEAD_DIM)
    row_tiles = tiles.shape[3] * split // 2
    shape = (row_tiles, HEADS // heads_axis, heads_axis, TILE, HEAD_DIM)
    outs = pl.pallas_call(
        unpack_kernel,
        out_shape=[jax.ShapeDtypeStruct(shape, jnp.bfloat16)] * 2,
        in_specs=[pl.BlockSpec(memory_space=pltpu.VMEM)],
        out_specs=[pl.BlockSpec(memory_space=pltpu.HBM)] * 2,
        scratch_shapes=[pltpu.SemaphoreType.DMA((2 * row_tiles,))],
        compiler_params=pltpu.CompilerParams(vmem_limit_bytes=4 * 2**20),
        name="unpack",
    )(tiles)
    return tuple(from_tiles(out) for out in outs)


def solution(mesh):
    heads_axis = mesh.shape["head"]

    def local(query_main, key_main, value_main, query_tan, key_tan, value_tan, positions):
        rows = query_main.shape[0]
        peers, split, flat = plan(mesh, rows)
        teams = [[flat(peer, member) for member in range(HEADS)] for peer in range(peers)]

        def swap(value):
            groups = teams if split == 1 else None
            return lax.all_to_all(value, AXES, 0, 0, axis_index_groups=groups, tiled=True)

        def from_peer(value, by):
            pairs = [
                (flat(peer, member), flat((peer + by) % peers, member))
                for peer in range(peers)
                for member in range(HEADS)
            ]
            return lax.ppermute(value, AXES, pairs)

        arrays = (query_main, key_main, value_main, query_tan, key_tan, value_tan)
        packed, places = pack(positions, arrays, split, heads_axis)
        everyone = lax.all_gather(places, AXES)
        everyone = everyone.reshape(HEADS // heads_axis, peers, heads_axis, TILE, HEAD_DIM)
        here = swap(packed.reshape(HEADS * split, -1, HEAD_DIM))
        blocks = [here] + [from_peer(here, by) for by in range(1, peers)]
        return unpack(swap(attention(rows // split, split, everyone, blocks)), split, heads_axis)

    placed = (P(AXES, None),) * 6 + (P(AXES),)
    return jax.shard_map(
        local,
        mesh=mesh,
        in_specs=placed,
        out_specs=(P(AXES, None), P(AXES, None)),
        check_vma=False,
    )
```

```python
import functools
import math

import jax
import jax.numpy as jnp
from jax import lax
from jax.experimental import pallas as pl
from jax.experimental.pallas import tpu as pltpu
from jax.sharding import PartitionSpec as P

HEADS = 16
HEAD_DIM = 128
LOG2_E = math.log2(math.e)
AXES = ("seq", "head")
TILE = 8
PIECES = 4


def plan(mesh, rows):
    heads_axis = mesh.shape["head"]
    peers = mesh.shape["seq"] * heads_axis // HEADS
    assert mesh.shape["seq"] % peers == 0 and rows % TILE == 0
    split = peers if peers == rows // TILE else 1

    def flat(peer, member):
        return (member // heads_axis * peers + peer) * heads_axis + member % heads_axis

    return peers, split, flat


def as_tiles(array):
    rows, columns = array.shape
    return array.reshape(rows // TILE, TILE, columns // HEAD_DIM, HEAD_DIM).transpose(0, 2, 1, 3)


def from_tiles(tiles):
    row_tiles, heads = tiles.shape[:2]
    return tiles.transpose(0, 2, 1, 3).reshape(row_tiles * TILE, heads * HEAD_DIM)


def slot_of(at, row_tile, row_tiles, split):
    own = row_tiles // split
    return row_tile // own, at * own + row_tile % own


def pack_kernel(positions, *refs):
    arrays, (out, here, sems) = refs[:6], refs[6:]
    row_tiles = arrays[0].shape[0]
    split = out.shape[0]
    load = pltpu.make_async_copy(positions, here, sems.at[6 * row_tiles])
    load.start()
    copies = []
    for at, array in enumerate(arrays):
        for row_tile in range(row_tiles):
            part, slot = slot_of(at, row_tile, row_tiles, split)
            sem = sems.at[len(copies)]
            copies.append(pltpu.make_async_copy(array.at[row_tile], out.at[part, :, slot], sem))
            copies[-1].start()
    own = row_tiles // split
    token = lax.broadcasted_iota(jnp.int32, (TILE, HEAD_DIM), 0)
    lane = lax.broadcasted_iota(jnp.int32, (TILE, HEAD_DIM), 1)
    token = token + lane // (HEAD_DIM // own) * TILE
    load.wait()
    for part in range(split):
        place = jnp.zeros((TILE, HEAD_DIM), jnp.int32)
        for t in range(own * TILE):
            place = jnp.where(token == t, here[part * own * TILE + t], place)
        place = lax.shift_right_logical(place, lane % PIECES * 8) & 255
        place = place.astype(jnp.float32).astype(jnp.bfloat16)
        for h in range(HEADS):
            out[part, h, 6 * own] = place
    for copy in copies:
        copy.wait()


def pack(positions, arrays, split):
    tiles = [as_tiles(array) for array in arrays]
    row_tiles = tiles[0].shape[0]
    shape = (split, HEADS, 6 * row_tiles // split + 1, TILE, HEAD_DIM)
    return pl.pallas_call(
        pack_kernel,
        out_shape=pltpu.VMEM(shape, jnp.bfloat16),
        in_specs=[pl.BlockSpec(memory_space=pltpu.HBM)] * (1 + len(tiles)),
        out_specs=pl.BlockSpec(memory_space=pltpu.VMEM),
        scratch_shapes=[
            pltpu.SMEM(positions.shape, jnp.int32),
            pltpu.SemaphoreType.DMA((6 * row_tiles + 1,)),
        ],
        compiler_params=pltpu.CompilerParams(vmem_limit_bytes=56 * 2**20),
        name="pack",
    )(positions, *tiles)


def dot(a, b, contract):
    return lax.dot_general(a, b, (contract, ((), ())), preferred_element_type=jnp.float32)


def order_of(pair):
    high, low = pair
    return high.astype(jnp.int32) * 65536 + low.astype(jnp.int32)


def attention_kernel(rows, *refs):
    blocks, out = refs[:-1], refs[-1]
    sources = blocks[0].shape[0]
    count = sources * rows
    scale = HEAD_DIM ** (-0.5)

    def part(ref, at):
        return ref[:, at * rows : (at + 1) * rows, :].reshape(count, HEAD_DIM)

    def places(ref):
        row_tiles = rows // TILE
        packed = ref[:, 6 * rows :, :]
        if row_tiles == 1:
            return packed.reshape(count, HEAD_DIM)
        packed = packed.astype(jnp.float32)
        lane = lax.broadcasted_iota(jnp.int32, packed.shape, 2)
        span = HEAD_DIM // row_tiles
        split = [jnp.where(lane // span == half, packed, 0.0) for half in range(row_tiles)]
        return jnp.stack(split, axis=1).reshape(count, HEAD_DIM).astype(jnp.bfloat16)

    def weights(shape, axis, first):
        at = lax.broadcasted_iota(jnp.int32, shape, axis) % (HEAD_DIM * TILE // rows)
        chosen = jnp.where(at == first, 1.0, jnp.where(at == first + 1, 256.0, 0.0))
        return chosen.astype(jnp.bfloat16)

    own = blocks[0]
    queries = part(own, 0)
    query_pair = jnp.concatenate([part(own, 3), queries], axis=1)
    own_order = places(own)
    across = (HEAD_DIM, HEAD_DIM)
    query_order = order_of([dot(own_order, weights(across, 0, first), ((1,), (0,))) for first in (2, 0)])
    state = None
    for start in range(0, len(blocks), 2):
        group = blocks[start : start + 2]

        def keyed(at):
            return jnp.concatenate([part(ref, at) for ref in group], axis=0)

        keys, values, key_dot, value_dot = [keyed(at) for at in (1, 2, 4, 5)]
        order = jnp.concatenate([places(ref) for ref in group], axis=0)
        width = keys.shape[0]
        down = (8, HEAD_DIM)
        key_order = order_of([dot(weights(down, 1, first), order, ((1,), (1,))) for first in (2, 0)])
        wide_order = jnp.concatenate([query_order] * (width // HEAD_DIM), axis=1)
        visible = key_order[:1] <= wide_order
        scores = dot(queries, keys, ((1,), (1,)))
        scores = jnp.where(visible, scores, -1e30)
        key_pair = jnp.concatenate([keys, key_dot], axis=1)
        score_tan = dot(query_pair, key_pair, ((1,), (1,)))
        new_max = jnp.max(scores, axis=1, keepdims=True)
        if state is not None:
            new_max = jnp.maximum(new_max, state[0])
        expo = jnp.exp2((scores - new_max) * (scale * LOG2_E))
        weighted = expo * score_tan
        total = jnp.sum(expo, axis=1, keepdims=True)
        mass = jnp.sum(weighted, axis=1, keepdims=True)
        both = dot(expo.astype(jnp.bfloat16), jnp.concatenate([values, value_dot], axis=1), ((1,), (0,)))
        moved = dot(weighted.astype(jnp.bfloat16), values, ((1,), (0,)))
        if state is not None:
            shrink = jnp.exp2((state[0] - new_max) * (scale * LOG2_E))
            total, mass, both, moved = [
                new + old * shrink for new, old in zip((total, mass, both, moved), state[1:])
            ]
        state = (new_max, total, mass, both, moved)
    _, total, mass, both, moved = state
    inverse = 1.0 / total
    mixed = both[:, :HEAD_DIM] * inverse
    tangent = both[:, HEAD_DIM:] * inverse + (moved - mass * mixed) * (inverse * scale)
    out[:, :rows, :] = mixed.astype(jnp.bfloat16).reshape(sources, rows, HEAD_DIM)
    out[:, rows:, :] = tangent.astype(jnp.bfloat16).reshape(sources, rows, HEAD_DIM)


def attention(rows, blocks):
    return pl.pallas_call(
        functools.partial(attention_kernel, rows),
        out_shape=jax.ShapeDtypeStruct((blocks[0].shape[0], 2 * rows, HEAD_DIM), jnp.bfloat16),
        in_specs=[pl.BlockSpec(memory_space=pltpu.VMEM)] * len(blocks),
        out_specs=pl.BlockSpec(memory_space=pltpu.VMEM),
        compiler_params=pltpu.CompilerParams(vmem_limit_bytes=(8 + len(blocks)) * 2**20),
        name="attention",
    )(*blocks)


def unpack_kernel(packed, *refs):
    outs, sems = refs[:2], refs[2]
    row_tiles = outs[0].shape[0]
    copies = []
    for at, out in enumerate(outs):
        for row_tile in range(row_tiles):
            part, slot = slot_of(at, row_tile, row_tiles, packed.shape[0])
            sem = sems.at[len(copies)]
            copies.append(pltpu.make_async_copy(packed.at[part, :, slot], out.at[row_tile], sem))
            copies[-1].start()
    for copy in copies:
        copy.wait()


def unpack(packed, split):
    tiles = packed.reshape(split, HEADS, -1, TILE, HEAD_DIM)
    row_tiles = tiles.shape[2] * split // 2
    shape = (row_tiles, HEADS, TILE, HEAD_DIM)
    outs = pl.pallas_call(
        unpack_kernel,
        out_shape=[jax.ShapeDtypeStruct(shape, jnp.bfloat16)] * 2,
        in_specs=[pl.BlockSpec(memory_space=pltpu.VMEM)],
        out_specs=[pl.BlockSpec(memory_space=pltpu.HBM)] * 2,
        scratch_shapes=[pltpu.SemaphoreType.DMA((2 * row_tiles,))],
        compiler_params=pltpu.CompilerParams(vmem_limit_bytes=4 * 2**20),
        name="unpack",
    )(tiles)
    return tuple(from_tiles(out) for out in outs)


def solution(mesh):
    def local(query_main, key_main, value_main, query_tan, key_tan, value_tan, positions):
        rows = query_main.shape[0]
        peers, split, flat = plan(mesh, rows)
        teams = [[flat(peer, member) for member in range(HEADS)] for peer in range(peers)]
        groups = teams if split == 1 else [sum(teams, [])]

        def swap(value):
            return lax.all_to_all(value, AXES, 0, 0, axis_index_groups=groups, tiled=True)

        def from_peer(value, by):
            pairs = [
                (flat(peer, member), flat((peer + by) % peers, member))
                for peer in range(peers)
                for member in range(HEADS)
            ]
            return lax.ppermute(value, AXES, pairs)

        arrays = (query_main, key_main, value_main, query_tan, key_tan, value_tan)
        packed = pack(positions, arrays, split)
        here = swap(packed.reshape(HEADS * split, -1, HEAD_DIM))
        blocks = [here] + [from_peer(here, by) for by in range(1, peers)]
        return unpack(swap(attention(rows // split, blocks)), split)

    placed = (P(AXES, None),) * 6 + (P(AXES),)
    return jax.shard_map(
        local,
        mesh=mesh,
        in_specs=placed,
        out_specs=(P(AXES, None), P(AXES, None)),
        check_vma=False,
    )
```

```python
import functools
import math

import jax
import jax.numpy as jnp
from jax import lax
from jax.experimental import pallas as pl
from jax.experimental.pallas import tpu as pltpu
from jax.sharding import PartitionSpec as P

HEADS = 16
HEAD_DIM = 128
LOG2_E = math.log2(math.e)
AXES = ("seq", "head")
TILE = 8
PIECES = 4


def plan(mesh, rows):
    heads_axis = mesh.shape["head"]
    peers = mesh.shape["seq"] * heads_axis // HEADS
    assert mesh.shape["seq"] % peers == 0 and rows % TILE == 0
    split = peers if peers == rows // TILE else 1

    def flat(peer, member):
        return (member // heads_axis * peers + peer) * heads_axis + member % heads_axis

    return peers, split, flat


def as_tiles(array):
    rows, columns = array.shape
    return array.reshape(rows // TILE, TILE, columns // HEAD_DIM, HEAD_DIM).transpose(0, 2, 1, 3)


def from_tiles(tiles):
    row_tiles, heads = tiles.shape[:2]
    return tiles.transpose(0, 2, 1, 3).reshape(row_tiles * TILE, heads * HEAD_DIM)


def slot_of(at, row_tile, row_tiles, split):
    own = row_tiles // split
    return row_tile // own, at * own + row_tile % own


def pack_kernel(positions, *refs):
    arrays, (out, here, sems) = refs[:6], refs[6:]
    row_tiles = arrays[0].shape[0]
    split = out.shape[0]
    load = pltpu.make_async_copy(positions, here, sems.at[6 * row_tiles])
    load.start()
    copies = []
    for at, array in enumerate(arrays):
        for row_tile in range(row_tiles):
            part, slot = slot_of(at, row_tile, row_tiles, split)
            sem = sems.at[len(copies)]
            copies.append(pltpu.make_async_copy(array.at[row_tile], out.at[part, :, slot], sem))
            copies[-1].start()
    own = row_tiles // split
    token = lax.broadcasted_iota(jnp.int32, (TILE, HEAD_DIM), 0)
    lane = lax.broadcasted_iota(jnp.int32, (TILE, HEAD_DIM), 1)
    token = token + lane // (HEAD_DIM // own) * TILE
    load.wait()
    for part in range(split):
        place = jnp.zeros((TILE, HEAD_DIM), jnp.int32)
        for t in range(own * TILE):
            place = jnp.where(token == t, here[part * own * TILE + t], place)
        place = lax.shift_right_logical(place, lane % PIECES * 8) & 255
        place = place.astype(jnp.float32).astype(jnp.bfloat16)
        for h in range(HEADS):
            out[part, h, 6 * own] = place
    for copy in copies:
        copy.wait()


def pack(positions, arrays, split):
    tiles = [as_tiles(array) for array in arrays]
    row_tiles = tiles[0].shape[0]
    shape = (split, HEADS, 6 * row_tiles // split + 1, TILE, HEAD_DIM)
    return pl.pallas_call(
        pack_kernel,
        out_shape=pltpu.VMEM(shape, jnp.bfloat16),
        in_specs=[pl.BlockSpec(memory_space=pltpu.HBM)] * (1 + len(tiles)),
        out_specs=pl.BlockSpec(memory_space=pltpu.VMEM),
        scratch_shapes=[
            pltpu.SMEM(positions.shape, jnp.int32),
            pltpu.SemaphoreType.DMA((6 * row_tiles + 1,)),
        ],
        compiler_params=pltpu.CompilerParams(vmem_limit_bytes=56 * 2**20),
        name="pack",
    )(positions, *tiles)


def dot(a, b, contract):
    return lax.dot_general(a, b, (contract, ((), ())), preferred_element_type=jnp.float32)


def order_of(pair):
    high, low = pair
    return high.astype(jnp.int32) * 65536 + low.astype(jnp.int32)


def attention_kernel(rows, *refs):
    blocks, out = refs[:-1], refs[-1]
    sources = blocks[0].shape[0]
    count = sources * rows
    scale = HEAD_DIM ** (-0.5)

    def part(ref, at):
        return ref[:, at * rows : (at + 1) * rows, :].reshape(count, HEAD_DIM)

    def places(ref):
        row_tiles = rows // TILE
        packed = ref[:, 6 * rows :, :]
        if row_tiles == 1:
            return packed.reshape(count, HEAD_DIM)
        packed = packed.astype(jnp.float32)
        lane = lax.broadcasted_iota(jnp.int32, packed.shape, 2)
        span = HEAD_DIM // row_tiles
        split = [jnp.where(lane // span == half, packed, 0.0) for half in range(row_tiles)]
        return jnp.stack(split, axis=1).reshape(count, HEAD_DIM).astype(jnp.bfloat16)

    def weights(shape, axis, first):
        at = lax.broadcasted_iota(jnp.int32, shape, axis) % (HEAD_DIM * TILE // rows)
        chosen = jnp.where(at == first, 1.0, jnp.where(at == first + 1, 256.0, 0.0))
        return chosen.astype(jnp.bfloat16)

    own = blocks[0]
    queries = part(own, 0)
    query_pair = jnp.concatenate([part(own, 3), queries], axis=1)
    own_order = places(own)
    across = (HEAD_DIM, HEAD_DIM)
    query_order = order_of([dot(own_order, weights(across, 0, first), ((1,), (0,))) for first in (2, 0)])
    state = None
    for start in range(0, len(blocks), 2):
        group = blocks[start : start + 2]

        def keyed(at):
            return jnp.concatenate([part(ref, at) for ref in group], axis=0)

        keys, values, key_dot, value_dot = [keyed(at) for at in (1, 2, 4, 5)]
        order = jnp.concatenate([places(ref) for ref in group], axis=0)
        width = keys.shape[0]
        down = (8, HEAD_DIM)
        key_order = order_of([dot(weights(down, 1, first), order, ((1,), (1,))) for first in (2, 0)])
        wide_order = jnp.concatenate([query_order] * (width // HEAD_DIM), axis=1)
        visible = key_order[:1] <= wide_order
        scores = dot(queries, keys, ((1,), (1,)))
        scores = jnp.where(visible, scores, -1e30)
        key_pair = jnp.concatenate([keys, key_dot], axis=1)
        score_tan = dot(query_pair, key_pair, ((1,), (1,)))
        new_max = jnp.max(scores, axis=1, keepdims=True)
        if state is not None:
            new_max = jnp.maximum(new_max, state[0])
        expo = jnp.exp2((scores - new_max) * (scale * LOG2_E))
        weighted = expo * score_tan
        total = jnp.sum(expo, axis=1, keepdims=True)
        mass = jnp.sum(weighted, axis=1, keepdims=True)
        both = dot(expo.astype(jnp.bfloat16), jnp.concatenate([values, value_dot], axis=1), ((1,), (0,)))
        moved = dot(weighted.astype(jnp.bfloat16), values, ((1,), (0,)))
        if state is not None:
            shrink = jnp.exp2((state[0] - new_max) * (scale * LOG2_E))
            total, mass, both, moved = [
                new + old * shrink for new, old in zip((total, mass, both, moved), state[1:])
            ]
        state = (new_max, total, mass, both, moved)
    _, total, mass, both, moved = state
    inverse = 1.0 / total
    mixed = both[:, :HEAD_DIM] * inverse
    tangent = both[:, HEAD_DIM:] * inverse + (moved - mass * mixed) * (inverse * scale)
    out[:, :rows, :] = mixed.astype(jnp.bfloat16).reshape(sources, rows, HEAD_DIM)
    out[:, rows:, :] = tangent.astype(jnp.bfloat16).reshape(sources, rows, HEAD_DIM)


def attention(rows, blocks):
    return pl.pallas_call(
        functools.partial(attention_kernel, rows),
        out_shape=jax.ShapeDtypeStruct((blocks[0].shape[0], 2 * rows, HEAD_DIM), jnp.bfloat16),
        in_specs=[pl.BlockSpec(memory_space=pltpu.VMEM)] * len(blocks),
        out_specs=pl.BlockSpec(memory_space=pltpu.VMEM),
        compiler_params=pltpu.CompilerParams(vmem_limit_bytes=(8 + len(blocks)) * 2**20),
        name="attention",
    )(*blocks)


def unpack_kernel(packed, *refs):
    outs, sems = refs[:2], refs[2]
    row_tiles = outs[0].shape[0]
    copies = []
    for at, out in enumerate(outs):
        for row_tile in range(row_tiles):
            part, slot = slot_of(at, row_tile, row_tiles, packed.shape[0])
            sem = sems.at[len(copies)]
            copies.append(pltpu.make_async_copy(packed.at[part, :, slot], out.at[row_tile], sem))
            copies[-1].start()
    for copy in copies:
        copy.wait()


def unpack(packed, split):
    tiles = packed.reshape(split, HEADS, -1, TILE, HEAD_DIM)
    row_tiles = tiles.shape[2] * split // 2
    shape = (row_tiles, HEADS, TILE, HEAD_DIM)
    outs = pl.pallas_call(
        unpack_kernel,
        out_shape=[jax.ShapeDtypeStruct(shape, jnp.bfloat16)] * 2,
        in_specs=[pl.BlockSpec(memory_space=pltpu.VMEM)],
        out_specs=[pl.BlockSpec(memory_space=pltpu.HBM)] * 2,
        scratch_shapes=[pltpu.SemaphoreType.DMA((2 * row_tiles,))],
        compiler_params=pltpu.CompilerParams(vmem_limit_bytes=4 * 2**20),
        name="unpack",
    )(tiles)
    return tuple(from_tiles(out) for out in outs)


def solution(mesh):
    def local(query_main, key_main, value_main, query_tan, key_tan, value_tan, positions):
        rows = query_main.shape[0]
        peers, split, flat = plan(mesh, rows)
        bits = HEADS.bit_length() - 1
        order = [int(f"{head:0{bits}b}"[::-1], 2) for head in range(HEADS)]
        teams = [[flat(peer, member) for member in order] for peer in range(peers)]
        groups = teams if split == 1 else [sum(teams, [])]

        def swap(value):
            return lax.all_to_all(value, AXES, 0, 0, axis_index_groups=groups, tiled=True)

        def from_peer(value, by):
            pairs = [
                (flat(peer, member), flat((peer + by) % peers, member))
                for peer in range(peers)
                for member in range(HEADS)
            ]
            return lax.ppermute(value, AXES, pairs)

        arrays = (query_main, key_main, value_main, query_tan, key_tan, value_tan)
        packed = pack(positions, arrays, split)
        here = swap(packed.reshape(HEADS * split, -1, HEAD_DIM))
        blocks = [here] + [from_peer(here, by) for by in range(1, peers)]
        return unpack(swap(attention(rows // split, blocks)), split)

    placed = (P(AXES, None),) * 6 + (P(AXES),)
    return jax.shard_map(
        local,
        mesh=mesh,
        in_specs=placed,
        out_specs=(P(AXES, None), P(AXES, None)),
        check_vma=False,
    )
```

```python
import functools
import math

import jax
import jax.numpy as jnp
from jax import lax
from jax.experimental import pallas as pl
from jax.experimental.pallas import tpu as pltpu
from jax.sharding import PartitionSpec as P

HEADS = 16
HEAD_DIM = 128
LOG2_E = math.log2(math.e)
AXES = ("seq", "head")
TILE = 8
PIECES = 4


def as_tiles(array):
    rows, columns = array.shape
    return array.reshape(rows // TILE, TILE, columns // HEAD_DIM, HEAD_DIM).transpose(0, 2, 1, 3)


def from_tiles(tiles):
    row_tiles, heads = tiles.shape[:2]
    return tiles.transpose(0, 2, 1, 3).reshape(row_tiles * TILE, heads * HEAD_DIM)


def pack_kernel(positions, *refs):
    arrays, (own, other, here, sems) = refs[:6], refs[6:]
    row_tiles = arrays[0].shape[0]
    load = pltpu.make_async_copy(positions, here, sems.at[0])
    load.start()
    copies = []
    for out, held in ((other, 4), (own, 6)):
        for at, array in enumerate(arrays[:held]):
            for row_tile in range(row_tiles):
                sem = sems.at[1 + len(copies)]
                slot = at * row_tiles + row_tile
                copies.append(pltpu.make_async_copy(array.at[row_tile], out.at[:, slot], sem))
                copies[-1].start()
    token = lax.broadcasted_iota(jnp.int32, (TILE, HEAD_DIM), 0)
    lane = lax.broadcasted_iota(jnp.int32, (TILE, HEAD_DIM), 1)
    token = token + lane // (HEAD_DIM // row_tiles) * TILE
    place = jnp.zeros((TILE, HEAD_DIM), jnp.int32)
    load.wait()
    for t in range(row_tiles * TILE):
        place = jnp.where(token == t, here[t], place)
    place = lax.shift_right_logical(place, lane % PIECES * 8) & 255
    place = place.astype(jnp.float32).astype(jnp.bfloat16)
    for h in range(HEADS):
        own[h, 6 * row_tiles] = place
        other[h, 4 * row_tiles] = place
    for copy in copies:
        copy.wait()


def pack(positions, arrays):
    tiles = [as_tiles(array) for array in arrays]
    row_tiles = tiles[0].shape[0]
    shapes = [(HEADS, held * row_tiles + 1, TILE, HEAD_DIM) for held in (6, 4)]
    return pl.pallas_call(
        pack_kernel,
        out_shape=[pltpu.VMEM(shape, jnp.bfloat16) for shape in shapes],
        in_specs=[pl.BlockSpec(memory_space=pltpu.HBM)] * (1 + len(tiles)),
        out_specs=[pl.BlockSpec(memory_space=pltpu.VMEM)] * 2,
        scratch_shapes=[
            pltpu.SMEM(positions.shape, jnp.int32),
            pltpu.SemaphoreType.DMA((10 * row_tiles + 1,)),
        ],
        compiler_params=pltpu.CompilerParams(vmem_limit_bytes=56 * 2**20),
        name="pack",
    )(positions, *tiles)


def dot(a, b, contract):
    return lax.dot_general(a, b, (contract, ((), ())), preferred_element_type=jnp.float32)


def order_of(pair):
    high, low = pair
    return high.astype(jnp.int32) * 65536 + low.astype(jnp.int32)


def attention_kernel(rows, *refs):
    blocks, out = refs[:-1], refs[-1]
    count = HEADS * rows
    scale = HEAD_DIM ** (-0.5)

    def part(ref, at):
        return ref[:, at * rows : (at + 1) * rows, :].reshape(count, HEAD_DIM)

    def places(ref):
        row_tiles = rows // TILE
        packed = ref[:, ref.shape[1] - TILE :, :]
        packed = packed.astype(jnp.float32)
        lane = lax.broadcasted_iota(jnp.int32, packed.shape, 2)
        span = HEAD_DIM // row_tiles
        split = [jnp.where(lane // span == half, packed, 0.0) for half in range(row_tiles)]
        return jnp.stack(split, axis=1).reshape(count, HEAD_DIM).astype(jnp.bfloat16)

    def weights(shape, axis, first):
        at = lax.broadcasted_iota(jnp.int32, shape, axis) % (HEAD_DIM * TILE // rows)
        chosen = jnp.where(at == first, 1.0, jnp.where(at == first + 1, 256.0, 0.0))
        return chosen.astype(jnp.bfloat16)

    own = blocks[0]
    queries = part(own, 4)
    query_pair = jnp.concatenate([part(own, 5), queries], axis=1)
    own_order = places(own)
    across = (HEAD_DIM, HEAD_DIM)
    query_order = order_of([dot(own_order, weights(across, 0, first), ((1,), (0,))) for first in (2, 0)])
    state = None
    for start in range(0, len(blocks), 2):
        group = blocks[start : start + 2]

        def keyed(at):
            return jnp.concatenate([part(ref, at) for ref in group], axis=0)

        keys, values, key_dot, value_dot = [keyed(at) for at in range(4)]
        order = jnp.concatenate([places(ref) for ref in group], axis=0)
        width = keys.shape[0]
        down = (8, HEAD_DIM)
        key_order = order_of([dot(weights(down, 1, first), order, ((1,), (1,))) for first in (2, 0)])
        wide_order = jnp.concatenate([query_order] * (width // HEAD_DIM), axis=1)
        visible = key_order[:1] <= wide_order
        scores = dot(queries, keys, ((1,), (1,)))
        scores = jnp.where(visible, scores, -1e30)
        key_pair = jnp.concatenate([keys, key_dot], axis=1)
        score_tan = dot(query_pair, key_pair, ((1,), (1,)))
        new_max = jnp.max(scores, axis=1, keepdims=True)
        if state is not None:
            new_max = jnp.maximum(new_max, state[0])
        expo = jnp.exp2((scores - new_max) * (scale * LOG2_E))
        weighted = expo * score_tan
        total = jnp.sum(expo, axis=1, keepdims=True)
        mass = jnp.sum(weighted, axis=1, keepdims=True)
        both = dot(expo.astype(jnp.bfloat16), jnp.concatenate([values, value_dot], axis=1), ((1,), (0,)))
        moved = dot(weighted.astype(jnp.bfloat16), values, ((1,), (0,)))
        if state is not None:
            shrink = jnp.exp2((state[0] - new_max) * (scale * LOG2_E))
            total, mass, both, moved = [
                new + old * shrink for new, old in zip((total, mass, both, moved), state[1:])
            ]
        state = (new_max, total, mass, both, moved)
    _, total, mass, both, moved = state
    inverse = 1.0 / total
    mixed = both[:, :HEAD_DIM] * inverse
    tangent = both[:, HEAD_DIM:] * inverse + (moved - mass * mixed) * (inverse * scale)
    out[:, :rows, :] = mixed.astype(jnp.bfloat16).reshape(HEADS, rows, HEAD_DIM)
    out[:, rows:, :] = tangent.astype(jnp.bfloat16).reshape(HEADS, rows, HEAD_DIM)


def attention(rows, blocks):
    return pl.pallas_call(
        functools.partial(attention_kernel, rows),
        out_shape=jax.ShapeDtypeStruct((HEADS, 2 * rows, HEAD_DIM), jnp.bfloat16),
        in_specs=[pl.BlockSpec(memory_space=pltpu.VMEM)] * len(blocks),
        out_specs=pl.BlockSpec(memory_space=pltpu.VMEM),
        compiler_params=pltpu.CompilerParams(vmem_limit_bytes=(8 + len(blocks)) * 2**20),
        name="attention",
    )(*blocks)


def unpack_kernel(packed, *refs):
    outs, sems = refs[:2], refs[2]
    row_tiles = outs[0].shape[0]
    copies = []
    for at, out in enumerate(outs):
        for row_tile in range(row_tiles):
            slot = at * row_tiles + row_tile
            copies.append(pltpu.make_async_copy(packed.at[:, slot], out.at[row_tile], sems.at[slot]))
            copies[-1].start()
    for copy in copies:
        copy.wait()


def unpack(packed):
    row_tiles = packed.shape[1] // TILE // 2
    shape = (row_tiles, HEADS, TILE, HEAD_DIM)
    outs = pl.pallas_call(
        unpack_kernel,
        out_shape=[jax.ShapeDtypeStruct(shape, jnp.bfloat16)] * 2,
        in_specs=[pl.BlockSpec(memory_space=pltpu.VMEM)],
        out_specs=[pl.BlockSpec(memory_space=pltpu.HBM)] * 2,
        scratch_shapes=[pltpu.SemaphoreType.DMA((2 * row_tiles,))],
        compiler_params=pltpu.CompilerParams(vmem_limit_bytes=4 * 2**20),
        name="unpack",
    )(packed.reshape(HEADS, 2 * row_tiles, TILE, HEAD_DIM))
    return tuple(from_tiles(out) for out in outs)


def solution(mesh):
    devices = mesh.shape["seq"] * mesh.shape["head"]
    assert devices % HEADS == 0
    groups = [list(range(first, first + HEADS)) for first in range(0, devices, HEADS)]

    def swap(value):
        value = value.reshape(HEADS, -1, HEAD_DIM)
        return lax.all_to_all(value, AXES, 0, 0, axis_index_groups=groups, tiled=True)

    def from_group(value, by):
        pairs = [(device, (device + by * HEADS) % devices) for device in range(devices)]
        return lax.ppermute(value, AXES, pairs)

    def local(query_main, key_main, value_main, query_tan, key_tan, value_tan, positions):
        rows = query_main.shape[0]
        arrays = (key_main, value_main, key_tan, value_tan, query_main, query_tan)
        own, other = pack(positions, arrays)
        others = [from_group(other, by) for by in range(1, len(groups))]
        blocks = [swap(own)] + [swap(each) for each in others]
        return unpack(swap(attention(rows, blocks)))

    placed = (P(AXES, None),) * 6 + (P(AXES),)
    return jax.shard_map(
        local,
        mesh=mesh,
        in_specs=placed,
        out_specs=(P(AXES, None), P(AXES, None)),
        check_vma=False,
    )
```

```python
import functools
import math

import jax
import jax.numpy as jnp
from jax import lax
from jax.experimental import pallas as pl
from jax.experimental.pallas import tpu as pltpu
from jax.sharding import PartitionSpec as P

HEADS = 16
HEAD_DIM = 128
LOG2_E = math.log2(math.e)
AXES = ("seq", "head")
TILE = 8
PIECES = 4


def plan(mesh, rows):
    heads_axis = mesh.shape["head"]
    peers = mesh.shape["seq"] * heads_axis // HEADS
    assert mesh.shape["seq"] % peers == 0 and rows % TILE == 0
    split = peers if peers == rows // TILE else 1

    def flat(peer, member):
        return (member // heads_axis * peers + peer) * heads_axis + member % heads_axis

    return peers, split, flat


def as_tiles(array):
    rows, columns = array.shape
    return array.reshape(rows // TILE, TILE, columns // HEAD_DIM, HEAD_DIM).transpose(0, 2, 1, 3)


def from_tiles(tiles):
    row_tiles, heads = tiles.shape[:2]
    return tiles.transpose(0, 2, 1, 3).reshape(row_tiles * TILE, heads * HEAD_DIM)


def slot_of(at, row_tile, row_tiles, split):
    own = row_tiles // split
    return row_tile // own, at * own + row_tile % own


def copy_tiles(arrays, out, sems):
    row_tiles = arrays[0].shape[0]
    copies = []
    for at, array in enumerate(arrays):
        for row_tile in range(row_tiles):
            part, slot = slot_of(at, row_tile, row_tiles, out.shape[0])
            sem = sems.at[len(copies)]
            copies.append(pltpu.make_async_copy(array.at[row_tile], out.at[part, :, slot], sem))
            copies[-1].start()
    return copies


def pack_kernel(*refs):
    arrays, (out, sems) = refs[:-2], refs[-2:]
    for copy in copy_tiles(arrays, out, sems):
        copy.wait()


def pack_places_kernel(positions, *refs):
    arrays, (out, sems, here) = refs[:-3], refs[-3:]
    row_tiles = arrays[0].shape[0]
    split = out.shape[0]
    load = pltpu.make_async_copy(positions, here, sems.at[len(arrays) * row_tiles])
    load.start()
    copies = copy_tiles(arrays, out, sems)
    own = row_tiles // split
    token = lax.broadcasted_iota(jnp.int32, (TILE, HEAD_DIM), 0)
    lane = lax.broadcasted_iota(jnp.int32, (TILE, HEAD_DIM), 1)
    token = token + lane // (HEAD_DIM // own) * TILE
    load.wait()
    for part in range(split):
        place = jnp.zeros((TILE, HEAD_DIM), jnp.int32)
        for t in range(own * TILE):
            place = jnp.where(token == t, here[part * own * TILE + t], place)
        place = lax.shift_right_logical(place, lane % PIECES * 8) & 255
        place = place.astype(jnp.float32).astype(jnp.bfloat16)
        for h in range(HEADS):
            out[part, h, len(arrays) * own] = place
    for copy in copies:
        copy.wait()


def pack(arrays, split, positions=None):
    tiles = [as_tiles(array) for array in arrays]
    row_tiles = tiles[0].shape[0]
    slots = len(tiles) * row_tiles // split
    kernel, first, scratch = pack_kernel, (), []
    if positions is not None:
        kernel, first, scratch = pack_places_kernel, (positions,), [pltpu.SMEM(positions.shape, jnp.int32)]
    packed = pl.pallas_call(
        kernel,
        out_shape=pltpu.VMEM((split, HEADS, slots + len(first), TILE, HEAD_DIM), jnp.bfloat16),
        in_specs=[pl.BlockSpec(memory_space=pltpu.HBM)] * (len(first) + len(tiles)),
        out_specs=pl.BlockSpec(memory_space=pltpu.VMEM),
        scratch_shapes=[pltpu.SemaphoreType.DMA((len(tiles) * row_tiles + 1,))] + scratch,
        compiler_params=pltpu.CompilerParams(vmem_limit_bytes=56 * 2**20),
        name="pack",
    )(*first, *tiles)
    return packed.reshape(HEADS * split, -1, HEAD_DIM)


def dot(a, b, contract):
    return lax.dot_general(a, b, (contract, ((), ())), preferred_element_type=jnp.float32)


def order_of(pair):
    high, low = pair
    return high.astype(jnp.int32) * 65536 + low.astype(jnp.int32)


def part_of(ref, at, rows):
    return ref[:, at * rows : (at + 1) * rows, :].reshape(-1, HEAD_DIM)


def softmax_kernel(rows, *refs):
    blocks, (expo_out, weighted_out, total_out, mass_out) = refs[:-4], refs[-4:]
    count = blocks[0].shape[0] * rows
    scale = HEAD_DIM ** (-0.5)

    def places(ref):
        row_tiles = rows // TILE
        packed = ref[:, 4 * rows :, :]
        if row_tiles == 1:
            return packed.reshape(count, HEAD_DIM)
        packed = packed.astype(jnp.float32)
        lane = lax.broadcasted_iota(jnp.int32, packed.shape, 2)
        span = HEAD_DIM // row_tiles
        split = [jnp.where(lane // span == half, packed, 0.0) for half in range(row_tiles)]
        return jnp.stack(split, axis=1).reshape(count, HEAD_DIM).astype(jnp.bfloat16)

    def weights(shape, axis, first):
        at = lax.broadcasted_iota(jnp.int32, shape, axis) % (HEAD_DIM * TILE // rows)
        chosen = jnp.where(at == first, 1.0, jnp.where(at == first + 1, 256.0, 0.0))
        return chosen.astype(jnp.bfloat16)

    own = blocks[0]
    queries = part_of(own, 2, rows)
    query_pair = jnp.concatenate([part_of(own, 3, rows), queries], axis=1)
    own_order = places(own)
    across, down = (HEAD_DIM, HEAD_DIM), (8, HEAD_DIM)
    query_order = order_of([dot(own_order, weights(across, 0, first), ((1,), (0,))) for first in (2, 0)])
    wide_order = jnp.concatenate([query_order] * (count // HEAD_DIM), axis=1)
    masked = []
    for ref in blocks:
        key_order = order_of([dot(weights(down, 1, first), places(ref), ((1,), (1,))) for first in (2, 0)])
        scores = dot(queries, part_of(ref, 0, rows), ((1,), (1,)))
        masked.append(jnp.where(key_order[:1] <= wide_order, scores, -1e30))
    tops = [jnp.max(scores, axis=1, keepdims=True) for scores in masked]
    top = functools.reduce(jnp.maximum, tops)
    total, mass = 0.0, 0.0
    for at, (ref, scores) in enumerate(zip(blocks, masked)):
        key_pair = jnp.concatenate([part_of(ref, 0, rows), part_of(ref, 1, rows)], axis=1)
        score_tan = dot(query_pair, key_pair, ((1,), (1,)))
        expo = jnp.exp2((scores - top) * (scale * LOG2_E))
        weighted = expo * score_tan
        total += jnp.sum(expo, axis=1, keepdims=True)
        mass += jnp.sum(weighted, axis=1, keepdims=True)
        expo_out[at] = expo.astype(jnp.bfloat16)
        weighted_out[at] = weighted.astype(jnp.bfloat16)
    total_out[...] = jnp.broadcast_to(total, total_out.shape)
    mass_out[...] = jnp.broadcast_to(mass, mass_out.shape)


def mix_kernel(rows, expo, weighted, total, mass, *refs):
    blocks, out = refs[:-1], refs[-1]
    scale = HEAD_DIM ** (-0.5)
    both, moved = 0.0, 0.0
    for at, ref in enumerate(blocks):
        values = part_of(ref, 0, rows)
        pair = jnp.concatenate([values, part_of(ref, 1, rows)], axis=1)
        both += dot(expo[at], pair, ((1,), (0,)))
        moved += dot(weighted[at], values, ((1,), (0,)))
    inverse = 1.0 / total[...]
    mixed = both[:, :HEAD_DIM] * inverse
    tangent = both[:, HEAD_DIM:] * inverse + (moved - mass[...] * mixed) * (inverse * scale)
    out[:, :rows, :] = mixed.astype(jnp.bfloat16).reshape(-1, rows, HEAD_DIM)
    out[:, rows:, :] = tangent.astype(jnp.bfloat16).reshape(-1, rows, HEAD_DIM)


def softmax(rows, blocks):
    count = blocks[0].shape[0] * rows
    low = jax.ShapeDtypeStruct((len(blocks), count, count), jnp.bfloat16)
    wide = jax.ShapeDtypeStruct((count, HEAD_DIM), jnp.float32)
    return pl.pallas_call(
        functools.partial(softmax_kernel, rows),
        out_shape=(low, low, wide, wide),
        in_specs=[pl.BlockSpec(memory_space=pltpu.VMEM)] * len(blocks),
        out_specs=[pl.BlockSpec(memory_space=pltpu.VMEM)] * 4,
        compiler_params=pltpu.CompilerParams(vmem_limit_bytes=(8 + len(blocks)) * 2**20),
        name="softmax",
    )(*blocks)


def mix(rows, soft, blocks):
    return pl.pallas_call(
        functools.partial(mix_kernel, rows),
        out_shape=jax.ShapeDtypeStruct((blocks[0].shape[0], 2 * rows, HEAD_DIM), jnp.bfloat16),
        in_specs=[pl.BlockSpec(memory_space=pltpu.VMEM)] * (len(soft) + len(blocks)),
        out_specs=pl.BlockSpec(memory_space=pltpu.VMEM),
        compiler_params=pltpu.CompilerParams(vmem_limit_bytes=(8 + len(blocks)) * 2**20),
        name="mix",
    )(*soft, *blocks)


def unpack_kernel(packed, *refs):
    outs, sems = refs[:2], refs[2]
    row_tiles = outs[0].shape[0]
    copies = []
    for at, out in enumerate(outs):
        for row_tile in range(row_tiles):
            part, slot = slot_of(at, row_tile, row_tiles, packed.shape[0])
            sem = sems.at[len(copies)]
            copies.append(pltpu.make_async_copy(packed.at[part, :, slot], out.at[row_tile], sem))
            copies[-1].start()
    for copy in copies:
        copy.wait()


def unpack(packed, split):
    tiles = packed.reshape(split, HEADS, -1, TILE, HEAD_DIM)
    row_tiles = tiles.shape[2] * split // 2
    shape = (row_tiles, HEADS, TILE, HEAD_DIM)
    outs = pl.pallas_call(
        unpack_kernel,
        out_shape=[jax.ShapeDtypeStruct(shape, jnp.bfloat16)] * 2,
        in_specs=[pl.BlockSpec(memory_space=pltpu.VMEM)],
        out_specs=[pl.BlockSpec(memory_space=pltpu.HBM)] * 2,
        scratch_shapes=[pltpu.SemaphoreType.DMA((2 * row_tiles,))],
        compiler_params=pltpu.CompilerParams(vmem_limit_bytes=4 * 2**20),
        name="unpack",
    )(tiles)
    return tuple(from_tiles(out) for out in outs)


def solution(mesh):
    def local(query_main, key_main, value_main, query_tan, key_tan, value_tan, positions):
        rows = query_main.shape[0]
        peers, split, flat = plan(mesh, rows)
        teams = [[flat(peer, member) for member in range(HEADS)] for peer in range(peers)]
        groups = teams if split == 1 else [sum(teams, [])]

        def swap(value):
            return lax.all_to_all(value, AXES, 0, 0, axis_index_groups=groups, tiled=True)

        def from_peer(value, by):
            pairs = [
                (flat(peer, member), flat((peer + by) % peers, member))
                for peer in range(peers)
                for member in range(HEADS)
            ]
            return lax.ppermute(value, AXES, pairs)

        def gather(packed):
            here = swap(packed)
            return [here] + [from_peer(here, by) for by in range(1, peers)]

        scored = pack((key_main, key_tan, query_main, query_tan), split, positions)
        valued = pack((value_main, value_tan), split)
        soft = softmax(rows // split, gather(scored))
        return unpack(swap(mix(rows // split, soft, gather(valued))), split)

    placed = (P(AXES, None),) * 6 + (P(AXES),)
    return jax.shard_map(
        local,
        mesh=mesh,
        in_specs=placed,
        out_specs=(P(AXES, None), P(AXES, None)),
        check_vma=False,
    )
```

```python
import functools
import math

import jax
import jax.numpy as jnp
from jax import lax
from jax.experimental import pallas as pl
from jax.experimental.pallas import tpu as pltpu
from jax.sharding import PartitionSpec as P

HEADS = 16
HEAD_DIM = 128
LOG2_E = math.log2(math.e)
STATE = 5
AXES = ("seq", "head")
TILE = 8
PIECES = 4


def plan(mesh, rows):
    heads_axis = mesh.shape["head"]
    peers = mesh.shape["seq"] * heads_axis // HEADS
    assert mesh.shape["seq"] % peers == 0 and rows % TILE == 0
    split = peers if peers == rows // TILE else 1

    def flat(peer, member):
        return (member // heads_axis * peers + peer) * heads_axis + member % heads_axis

    return peers, split, flat


def as_tiles(array):
    rows, columns = array.shape
    return array.reshape(rows // TILE, TILE, columns // HEAD_DIM, HEAD_DIM).transpose(0, 2, 1, 3)


def from_tiles(tiles):
    row_tiles, heads = tiles.shape[:2]
    return tiles.transpose(0, 2, 1, 3).reshape(row_tiles * TILE, heads * HEAD_DIM)


def tile_slots(messages, at, array):
    split = messages.shape[0]
    row_tiles = array.shape[0]
    own = row_tiles // split
    if own == 1:
        return [(slice(None), messages.at[:, :, at])]
    return [(tile, messages.at[tile // own, :, at * own + tile % own]) for tile in range(row_tiles)]


def copy_tiles(pairs, sems, out=False):
    copies = []
    for array, slots in pairs:
        for tile, slot in slots:
            ends = (slot, array.at[tile]) if out else (array.at[tile], slot)
            copies.append(pltpu.make_async_copy(*ends, sems.at[len(copies)]))
            copies[-1].start()
    return copies


def pack_kernel(positions, *refs):
    arrays, (out, here, sems) = refs[:6], refs[6:]
    row_tiles = arrays[0].shape[0]
    split = out.shape[0]
    load = pltpu.make_async_copy(positions, here, sems.at[6 * row_tiles])
    load.start()
    copies = copy_tiles([(array, tile_slots(out, at, array)) for at, array in enumerate(arrays)], sems)
    own = row_tiles // split
    token = lax.broadcasted_iota(jnp.int32, (TILE, HEAD_DIM), 0)
    lane = lax.broadcasted_iota(jnp.int32, (TILE, HEAD_DIM), 1)
    token = token + lane // (HEAD_DIM // own) * TILE
    load.wait()
    for part in range(split):
        place = jnp.zeros((TILE, HEAD_DIM), jnp.int32)
        for t in range(own * TILE):
            place = jnp.where(token == t, here[part * own * TILE + t], place)
        place = lax.shift_right_logical(place, lane % PIECES * 8) & 255
        place = place.astype(jnp.float32).astype(jnp.bfloat16)
        for h in range(HEADS):
            out[part, h, 6 * own] = place
    for copy in copies:
        copy.wait()


def pack(positions, arrays, split):
    tiles = [as_tiles(array) for array in arrays]
    row_tiles = tiles[0].shape[0]
    shape = (split, HEADS, 6 * row_tiles // split + 1, TILE, HEAD_DIM)
    return pl.pallas_call(
        pack_kernel,
        out_shape=pltpu.VMEM(shape, jnp.bfloat16),
        in_specs=[pl.BlockSpec(memory_space=pltpu.HBM)] * (1 + len(tiles)),
        out_specs=pl.BlockSpec(memory_space=pltpu.VMEM),
        scratch_shapes=[
            pltpu.SMEM(positions.shape, jnp.int32),
            pltpu.SemaphoreType.DMA((6 * row_tiles + 1,)),
        ],
        compiler_params=pltpu.CompilerParams(vmem_limit_bytes=56 * 2**20),
        name="pack",
    )(positions, *tiles)


def dot(a, b, contract):
    return lax.dot_general(a, b, (contract, ((), ())), preferred_element_type=jnp.float32)


def order_of(pair):
    high, low = pair
    return high.astype(jnp.int32) * 65536 + low.astype(jnp.int32)


def attention_kernel(rows, held, last, *refs):
    own, state, refs = refs[0], refs[1 : 1 + held], refs[1 + held :]
    blocks, outs = (refs[:-1], refs[-1:]) if last else (refs[:-STATE], refs[-STATE:])
    blocks = blocks if held else (own,) + blocks
    count = own.shape[0] * rows
    scale = HEAD_DIM ** (-0.5)

    def part(ref, at):
        return ref[:, at * rows : (at + 1) * rows, :].reshape(count, HEAD_DIM)

    def places(ref):
        row_tiles = rows // TILE
        packed = ref[:, 6 * rows :, :]
        if row_tiles == 1:
            return packed.reshape(count, HEAD_DIM)
        packed = packed.astype(jnp.float32)
        lane = lax.broadcasted_iota(jnp.int32, packed.shape, 2)
        span = HEAD_DIM // row_tiles
        split = [jnp.where(lane // span == half, packed, 0.0) for half in range(row_tiles)]
        return jnp.stack(split, axis=1).reshape(count, HEAD_DIM).astype(jnp.bfloat16)

    def weights(shape, axis, first):
        at = lax.broadcasted_iota(jnp.int32, shape, axis) % (HEAD_DIM * TILE // rows)
        chosen = jnp.where(at == first, 1.0, jnp.where(at == first + 1, 256.0, 0.0))
        return chosen.astype(jnp.bfloat16)

    queries = part(own, 0)
    query_pair = jnp.concatenate([part(own, 3), queries], axis=1)
    own_order = places(own)
    across, down = (HEAD_DIM, HEAD_DIM), (8, HEAD_DIM)
    query_order = order_of([dot(own_order, weights(across, 0, first), ((1,), (0,))) for first in (2, 0)])
    wide_order = jnp.concatenate([query_order] * (count // HEAD_DIM), axis=1)
    if held:
        top, total, mass, both, moved = [ref[...] for ref in state]
        top, total, mass = top[:, :1], total[:, :1], mass[:, :1]
    for at, ref in enumerate(blocks):
        keys, values, key_dot, value_dot = [part(ref, slot) for slot in (1, 2, 4, 5)]
        key_order = order_of([dot(weights(down, 1, first), places(ref), ((1,), (1,))) for first in (2, 0)])
        scores = dot(queries, keys, ((1,), (1,)))
        scores = jnp.where(key_order[:1] <= wide_order, scores, -1e30)
        key_pair = jnp.concatenate([keys, key_dot], axis=1)
        score_tan = dot(query_pair, key_pair, ((1,), (1,)))
        first = at == 0 and not held
        new_top = jnp.max(scores, axis=1, keepdims=True)
        if not first:
            new_top = jnp.maximum(new_top, top)
        expo = jnp.exp2((scores - new_top) * (scale * LOG2_E))
        weighted = expo * score_tan
        new = [
            jnp.sum(expo, axis=1, keepdims=True),
            jnp.sum(weighted, axis=1, keepdims=True),
            dot(expo.astype(jnp.bfloat16), jnp.concatenate([values, value_dot], axis=1), ((1,), (0,))),
            dot(weighted.astype(jnp.bfloat16), values, ((1,), (0,))),
        ]
        if not first:
            shrink = jnp.exp2((top - new_top) * (scale * LOG2_E))
            new = [now + old * shrink for now, old in zip(new, (total, mass, both, moved))]
        top, (total, mass, both, moved) = new_top, new
    if not last:
        for out, value in zip(outs, (top, total, mass, both, moved)):
            out[...] = jnp.broadcast_to(value, out.shape)
        return
    inverse = 1.0 / total
    mixed = both[:, :HEAD_DIM] * inverse
    tangent = both[:, HEAD_DIM:] * inverse + (moved - mass * mixed) * (inverse * scale)
    outs[0][:, :rows, :] = mixed.astype(jnp.bfloat16).reshape(-1, rows, HEAD_DIM)
    outs[0][:, rows:, :] = tangent.astype(jnp.bfloat16).reshape(-1, rows, HEAD_DIM)


def attention(rows, own, state, blocks, last):
    sources = own.shape[0]
    if last:
        out_shape = [jax.ShapeDtypeStruct((sources, 2 * rows, HEAD_DIM), jnp.bfloat16)]
    else:
        widths = [HEAD_DIM] * 3 + [2 * HEAD_DIM, HEAD_DIM]
        out_shape = [jax.ShapeDtypeStruct((sources * rows, width), jnp.float32) for width in widths]
    operands = (own, *state, *blocks)
    flops = 14 * (sources * rows) ** 2 * HEAD_DIM * max(len(blocks), 1)
    return pl.pallas_call(
        functools.partial(attention_kernel, rows, len(state), last),
        out_shape=out_shape,
        in_specs=[pl.BlockSpec(memory_space=pltpu.VMEM)] * len(operands),
        out_specs=[pl.BlockSpec(memory_space=pltpu.VMEM)] * len(out_shape),
        compiler_params=pltpu.CompilerParams(vmem_limit_bytes=(8 + len(operands)) * 2**20),
        cost_estimate=pl.CostEstimate(flops=flops, bytes_accessed=2**20, transcendentals=2**16),
        name="attention",
    )(*operands)


def unpack_kernel(packed, *refs):
    outs, sems = refs[:2], refs[2]
    pairs = [(out, tile_slots(packed, at, out)) for at, out in enumerate(outs)]
    for copy in copy_tiles(pairs, sems, out=True):
        copy.wait()


def unpack(packed, split):
    tiles = packed.reshape(split, HEADS, -1, TILE, HEAD_DIM)
    row_tiles = tiles.shape[2] * split // 2
    shape = (row_tiles, HEADS, TILE, HEAD_DIM)
    outs = pl.pallas_call(
        unpack_kernel,
        out_shape=[jax.ShapeDtypeStruct(shape, jnp.bfloat16)] * 2,
        in_specs=[pl.BlockSpec(memory_space=pltpu.VMEM)],
        out_specs=[pl.BlockSpec(memory_space=pltpu.HBM)] * 2,
        scratch_shapes=[pltpu.SemaphoreType.DMA((2 * row_tiles,))],
        compiler_params=pltpu.CompilerParams(vmem_limit_bytes=4 * 2**20),
        name="unpack",
    )(tiles)
    return tuple(from_tiles(out) for out in outs)


def solution(mesh):
    def local(query_main, key_main, value_main, query_tan, key_tan, value_tan, positions):
        rows = query_main.shape[0]
        peers, split, flat = plan(mesh, rows)
        teams = [[flat(peer, member) for member in range(HEADS)] for peer in range(peers)]
        groups = teams if split == 1 else [sum(teams, [])]

        def swap(value):
            return lax.all_to_all(value, AXES, 0, 0, axis_index_groups=groups, tiled=True)

        def from_peer(value, by):
            pairs = [
                (flat(peer, member), flat((peer + by) % peers, member))
                for peer in range(peers)
                for member in range(HEADS)
            ]
            return lax.ppermute(value, AXES, pairs)

        arrays = (query_main, key_main, value_main, query_tan, key_tan, value_tan)
        packed = pack(positions, arrays, split)
        here = swap(packed.reshape(HEADS * split, -1, HEAD_DIM))
        others = [from_peer(here, by) for by in range(1, peers)]
        state = attention(rows // split, here, (), (), last=False)
        (mixed,) = attention(rows // split, here, state, others, last=True)
        return unpack(swap(mixed), split)

    placed = (P(AXES, None),) * 6 + (P(AXES),)
    return jax.shard_map(
        local,
        mesh=mesh,
        in_specs=placed,
        out_specs=(P(AXES, None), P(AXES, None)),
        check_vma=False,
    )
```

```python
import functools
import math

import jax
import jax.numpy as jnp
from jax import lax
from jax.experimental import pallas as pl
from jax.experimental.pallas import tpu as pltpu
from jax.sharding import PartitionSpec as P

HEADS = 16
HEAD_DIM = 128
LOG2_E = math.log2(math.e)
AXES = ("seq", "head")
TILE = 8
PIECES = 4


def plan(mesh, rows):
    heads_axis = mesh.shape["head"]
    peers = mesh.shape["seq"] * heads_axis // HEADS
    assert mesh.shape["seq"] % peers == 0 and rows % TILE == 0

    def flat(team, member):
        peer = (team + member.bit_count()) % peers
        return (member // heads_axis * peers + peer) * heads_axis + member % heads_axis

    return peers, 1, flat


def as_tiles(array):
    rows, columns = array.shape
    return array.reshape(rows // TILE, TILE, columns // HEAD_DIM, HEAD_DIM).transpose(0, 2, 1, 3)


def from_tiles(tiles):
    row_tiles, heads = tiles.shape[:2]
    return tiles.transpose(0, 2, 1, 3).reshape(row_tiles * TILE, heads * HEAD_DIM)


def slot_of(at, row_tile, row_tiles, split):
    own = row_tiles // split
    return row_tile // own, at * own + row_tile % own


def pack_kernel(positions, *refs):
    arrays, (out, here, sems) = refs[:6], refs[6:]
    row_tiles = arrays[0].shape[0]
    split = out.shape[0]
    load = pltpu.make_async_copy(positions, here, sems.at[6 * row_tiles])
    load.start()
    copies = []
    for at, array in enumerate(arrays):
        for row_tile in range(row_tiles):
            part, slot = slot_of(at, row_tile, row_tiles, split)
            sem = sems.at[len(copies)]
            copies.append(pltpu.make_async_copy(array.at[row_tile], out.at[part, :, slot], sem))
            copies[-1].start()
    own = row_tiles // split
    token = lax.broadcasted_iota(jnp.int32, (TILE, HEAD_DIM), 0)
    lane = lax.broadcasted_iota(jnp.int32, (TILE, HEAD_DIM), 1)
    token = token + lane // (HEAD_DIM // own) * TILE
    load.wait()
    for part in range(split):
        place = jnp.zeros((TILE, HEAD_DIM), jnp.int32)
        for t in range(own * TILE):
            place = jnp.where(token == t, here[part * own * TILE + t], place)
        place = lax.shift_right_logical(place, lane % PIECES * 8) & 255
        place = place.astype(jnp.float32).astype(jnp.bfloat16)
        for h in range(HEADS):
            out[part, h, 6 * own] = place
    for copy in copies:
        copy.wait()


def pack(positions, arrays, split):
    tiles = [as_tiles(array) for array in arrays]
    row_tiles = tiles[0].shape[0]
    shape = (split, HEADS, 6 * row_tiles // split + 1, TILE, HEAD_DIM)
    return pl.pallas_call(
        pack_kernel,
        out_shape=pltpu.VMEM(shape, jnp.bfloat16),
        in_specs=[pl.BlockSpec(memory_space=pltpu.HBM)] * (1 + len(tiles)),
        out_specs=pl.BlockSpec(memory_space=pltpu.VMEM),
        scratch_shapes=[
            pltpu.SMEM(positions.shape, jnp.int32),
            pltpu.SemaphoreType.DMA((6 * row_tiles + 1,)),
        ],
        compiler_params=pltpu.CompilerParams(vmem_limit_bytes=56 * 2**20),
        name="pack",
    )(positions, *tiles)


def dot(a, b, contract):
    return lax.dot_general(a, b, (contract, ((), ())), preferred_element_type=jnp.float32)


def order_of(pair):
    high, low = pair
    return high.astype(jnp.int32) * 65536 + low.astype(jnp.int32)


def attention_kernel(rows, *refs):
    blocks, out = refs[:-1], refs[-1]
    sources = blocks[0].shape[0]
    count = sources * rows
    scale = HEAD_DIM ** (-0.5)

    def part(ref, at):
        return ref[:, at * rows : (at + 1) * rows, :].reshape(count, HEAD_DIM)

    def places(ref):
        row_tiles = rows // TILE
        packed = ref[:, 6 * rows :, :]
        if row_tiles == 1:
            return packed.reshape(count, HEAD_DIM)
        packed = packed.astype(jnp.float32)
        lane = lax.broadcasted_iota(jnp.int32, packed.shape, 2)
        span = HEAD_DIM // row_tiles
        split = [jnp.where(lane // span == half, packed, 0.0) for half in range(row_tiles)]
        return jnp.stack(split, axis=1).reshape(count, HEAD_DIM).astype(jnp.bfloat16)

    def weights(shape, axis, first):
        at = lax.broadcasted_iota(jnp.int32, shape, axis) % (HEAD_DIM * TILE // rows)
        chosen = jnp.where(at == first, 1.0, jnp.where(at == first + 1, 256.0, 0.0))
        return chosen.astype(jnp.bfloat16)

    own = blocks[0]
    queries = part(own, 0)
    query_pair = jnp.concatenate([part(own, 3), queries], axis=1)
    own_order = places(own)
    across = (HEAD_DIM, HEAD_DIM)
    query_order = order_of([dot(own_order, weights(across, 0, first), ((1,), (0,))) for first in (2, 0)])
    state = None
    for start in range(0, len(blocks), 2):
        group = blocks[start : start + 2]

        def keyed(at):
            return jnp.concatenate([part(ref, at) for ref in group], axis=0)

        keys, values, key_dot, value_dot = [keyed(at) for at in (1, 2, 4, 5)]
        order = jnp.concatenate([places(ref) for ref in group], axis=0)
        width = keys.shape[0]
        down = (8, HEAD_DIM)
        key_order = order_of([dot(weights(down, 1, first), order, ((1,), (1,))) for first in (2, 0)])
        wide_order = jnp.concatenate([query_order] * (width // HEAD_DIM), axis=1)
        visible = key_order[:1] <= wide_order
        scores = dot(queries, keys, ((1,), (1,)))
        scores = jnp.where(visible, scores, -1e30)
        key_pair = jnp.concatenate([keys, key_dot], axis=1)
        score_tan = dot(query_pair, key_pair, ((1,), (1,)))
        new_max = jnp.max(scores, axis=1, keepdims=True)
        if state is not None:
            new_max = jnp.maximum(new_max, state[0])
        expo = jnp.exp2((scores - new_max) * (scale * LOG2_E))
        weighted = expo * score_tan
        total = jnp.sum(expo, axis=1, keepdims=True)
        mass = jnp.sum(weighted, axis=1, keepdims=True)
        both = dot(expo.astype(jnp.bfloat16), jnp.concatenate([values, value_dot], axis=1), ((1,), (0,)))
        moved = dot(weighted.astype(jnp.bfloat16), values, ((1,), (0,)))
        if state is not None:
            shrink = jnp.exp2((state[0] - new_max) * (scale * LOG2_E))
            total, mass, both, moved = [
                new + old * shrink for new, old in zip((total, mass, both, moved), state[1:])
            ]
        state = (new_max, total, mass, both, moved)
    _, total, mass, both, moved = state
    inverse = 1.0 / total
    mixed = both[:, :HEAD_DIM] * inverse
    tangent = both[:, HEAD_DIM:] * inverse + (moved - mass * mixed) * (inverse * scale)
    out[:, :rows, :] = mixed.astype(jnp.bfloat16).reshape(sources, rows, HEAD_DIM)
    out[:, rows:, :] = tangent.astype(jnp.bfloat16).reshape(sources, rows, HEAD_DIM)


def attention(rows, blocks):
    return pl.pallas_call(
        functools.partial(attention_kernel, rows),
        out_shape=jax.ShapeDtypeStruct((blocks[0].shape[0], 2 * rows, HEAD_DIM), jnp.bfloat16),
        in_specs=[pl.BlockSpec(memory_space=pltpu.VMEM)] * len(blocks),
        out_specs=pl.BlockSpec(memory_space=pltpu.VMEM),
        compiler_params=pltpu.CompilerParams(vmem_limit_bytes=(8 + len(blocks)) * 2**20),
        name="attention",
    )(*blocks)


def unpack_kernel(packed, *refs):
    outs, sems = refs[:2], refs[2]
    row_tiles = outs[0].shape[0]
    copies = []
    for at, out in enumerate(outs):
        for row_tile in range(row_tiles):
            part, slot = slot_of(at, row_tile, row_tiles, packed.shape[0])
            sem = sems.at[len(copies)]
            copies.append(pltpu.make_async_copy(packed.at[part, :, slot], out.at[row_tile], sem))
            copies[-1].start()
    for copy in copies:
        copy.wait()


def unpack(packed, split):
    tiles = packed.reshape(split, HEADS, -1, TILE, HEAD_DIM)
    row_tiles = tiles.shape[2] * split // 2
    shape = (row_tiles, HEADS, TILE, HEAD_DIM)
    outs = pl.pallas_call(
        unpack_kernel,
        out_shape=[jax.ShapeDtypeStruct(shape, jnp.bfloat16)] * 2,
        in_specs=[pl.BlockSpec(memory_space=pltpu.VMEM)],
        out_specs=[pl.BlockSpec(memory_space=pltpu.HBM)] * 2,
        scratch_shapes=[pltpu.SemaphoreType.DMA((2 * row_tiles,))],
        compiler_params=pltpu.CompilerParams(vmem_limit_bytes=4 * 2**20),
        name="unpack",
    )(tiles)
    return tuple(from_tiles(out) for out in outs)


def solution(mesh):
    def local(query_main, key_main, value_main, query_tan, key_tan, value_tan, positions):
        rows = query_main.shape[0]
        peers, split, flat = plan(mesh, rows)
        teams = [[flat(peer, member) for member in range(HEADS)] for peer in range(peers)]
        groups = teams if split == 1 else [sum(teams, [])]

        def swap(value):
            return lax.all_to_all(value, AXES, 0, 0, axis_index_groups=groups, tiled=True)

        def from_peer(value, by):
            pairs = [
                (flat(peer, member), flat((peer + by) % peers, member))
                for peer in range(peers)
                for member in range(HEADS)
            ]
            return lax.ppermute(value, AXES, pairs)

        arrays = (query_main, key_main, value_main, query_tan, key_tan, value_tan)
        packed = pack(positions, arrays, split)
        here = swap(packed.reshape(HEADS * split, -1, HEAD_DIM))
        blocks = [here] + [from_peer(here, by) for by in range(1, peers)]
        return unpack(swap(attention(rows // split, blocks)), split)

    placed = (P(AXES, None),) * 6 + (P(AXES),)
    return jax.shard_map(
        local,
        mesh=mesh,
        in_specs=placed,
        out_specs=(P(AXES, None), P(AXES, None)),
        check_vma=False,
    )
```

```python
import functools
import math

import jax
import jax.numpy as jnp
from jax import lax
from jax.experimental import pallas as pl
from jax.experimental.pallas import tpu as pltpu
from jax.sharding import PartitionSpec as P

HEADS = 16
HEAD_DIM = 128
LOG2_E = math.log2(math.e)
AXES = ("seq", "head")
TILE = 8
PIECES = 4


def plan(mesh, rows):
    heads_axis = mesh.shape["head"]
    peers = mesh.shape["seq"] * heads_axis // HEADS
    assert mesh.shape["seq"] % peers == 0 and rows % TILE == 0

    def flat(peer, member):
        return (member // heads_axis * peers + peer) * heads_axis + member % heads_axis

    return peers, 1, flat


def as_tiles(array):
    rows, columns = array.shape
    return array.reshape(rows // TILE, TILE, columns // HEAD_DIM, HEAD_DIM).transpose(0, 2, 1, 3)


def from_tiles(tiles):
    row_tiles, heads = tiles.shape[:2]
    return tiles.transpose(0, 2, 1, 3).reshape(row_tiles * TILE, heads * HEAD_DIM)


def slot_of(at, row_tile, row_tiles, split):
    own = row_tiles // split
    return row_tile // own, at * own + row_tile % own


def pack_kernel(positions, *refs):
    arrays, (out, here, sems) = refs[:6], refs[6:]
    row_tiles = arrays[0].shape[0]
    split = out.shape[0]
    load = pltpu.make_async_copy(positions, here, sems.at[6 * row_tiles])
    load.start()
    copies = []
    for at, array in enumerate(arrays):
        for row_tile in range(row_tiles):
            part, slot = slot_of(at, row_tile, row_tiles, split)
            sem = sems.at[len(copies)]
            copies.append(pltpu.make_async_copy(array.at[row_tile], out.at[part, :, slot], sem))
            copies[-1].start()
    own = row_tiles // split
    token = lax.broadcasted_iota(jnp.int32, (TILE, HEAD_DIM), 0)
    lane = lax.broadcasted_iota(jnp.int32, (TILE, HEAD_DIM), 1)
    token = token + lane // (HEAD_DIM // own) * TILE
    load.wait()
    for part in range(split):
        place = jnp.zeros((TILE, HEAD_DIM), jnp.int32)
        for t in range(own * TILE):
            place = jnp.where(token == t, here[part * own * TILE + t], place)
        place = lax.shift_right_logical(place, lane % PIECES * 8) & 255
        place = place.astype(jnp.float32).astype(jnp.bfloat16)
        for h in range(HEADS):
            out[part, h, 6 * own] = place
    for copy in copies:
        copy.wait()


def pack(positions, arrays, split):
    tiles = [as_tiles(array) for array in arrays]
    row_tiles = tiles[0].shape[0]
    shape = (split, HEADS, 6 * row_tiles // split + 1, TILE, HEAD_DIM)
    return pl.pallas_call(
        pack_kernel,
        out_shape=pltpu.VMEM(shape, jnp.bfloat16),
        in_specs=[pl.BlockSpec(memory_space=pltpu.HBM)] * (1 + len(tiles)),
        out_specs=pl.BlockSpec(memory_space=pltpu.VMEM),
        scratch_shapes=[
            pltpu.SMEM(positions.shape, jnp.int32),
            pltpu.SemaphoreType.DMA((6 * row_tiles + 1,)),
        ],
        compiler_params=pltpu.CompilerParams(vmem_limit_bytes=56 * 2**20),
        name="pack",
    )(positions, *tiles)


def dot(a, b, contract):
    return lax.dot_general(a, b, (contract, ((), ())), preferred_element_type=jnp.float32)


def order_of(pair):
    high, low = pair
    return high.astype(jnp.int32) * 65536 + low.astype(jnp.int32)


def attention_kernel(rows, *refs):
    blocks, out = refs[:-1], refs[-1]
    sources = blocks[0].shape[0]
    count = sources * rows
    scale = HEAD_DIM ** (-0.5)

    def part(ref, at):
        return ref[:, at * rows : (at + 1) * rows, :].reshape(count, HEAD_DIM)

    def places(ref):
        row_tiles = rows // TILE
        packed = ref[:, 6 * rows :, :]
        if row_tiles == 1:
            return packed.reshape(count, HEAD_DIM)
        packed = packed.astype(jnp.float32)
        lane = lax.broadcasted_iota(jnp.int32, packed.shape, 2)
        span = HEAD_DIM // row_tiles
        split = [jnp.where(lane // span == half, packed, 0.0) for half in range(row_tiles)]
        return jnp.stack(split, axis=1).reshape(count, HEAD_DIM).astype(jnp.bfloat16)

    def weights(shape, axis, first):
        at = lax.broadcasted_iota(jnp.int32, shape, axis) % (HEAD_DIM * TILE // rows)
        chosen = jnp.where(at == first, 1.0, jnp.where(at == first + 1, 256.0, 0.0))
        return chosen.astype(jnp.bfloat16)

    own = blocks[0]
    queries = part(own, 0)
    query_pair = jnp.concatenate([part(own, 3), queries], axis=1)
    own_order = places(own)
    across = (HEAD_DIM, HEAD_DIM)
    query_order = order_of([dot(own_order, weights(across, 0, first), ((1,), (0,))) for first in (2, 0)])
    state = None
    for start in range(0, len(blocks), 2):
        group = blocks[start : start + 2]

        def keyed(at):
            return jnp.concatenate([part(ref, at) for ref in group], axis=0)

        keys, values, key_dot, value_dot = [keyed(at) for at in (1, 2, 4, 5)]
        order = jnp.concatenate([places(ref) for ref in group], axis=0)
        width = keys.shape[0]
        down = (8, HEAD_DIM)
        key_order = order_of([dot(weights(down, 1, first), order, ((1,), (1,))) for first in (2, 0)])
        wide_order = jnp.concatenate([query_order] * (width // HEAD_DIM), axis=1)
        visible = key_order[:1] <= wide_order
        scores = dot(queries, keys, ((1,), (1,)))
        scores = jnp.where(visible, scores, -1e30)
        key_pair = jnp.concatenate([keys, key_dot], axis=1)
        score_tan = dot(query_pair, key_pair, ((1,), (1,)))
        new_max = jnp.max(scores, axis=1, keepdims=True)
        if state is not None:
            new_max = jnp.maximum(new_max, state[0])
        expo = jnp.exp2((scores - new_max) * (scale * LOG2_E))
        weighted = expo * score_tan
        total = jnp.sum(expo, axis=1, keepdims=True)
        mass = jnp.sum(weighted, axis=1, keepdims=True)
        both = dot(expo.astype(jnp.bfloat16), jnp.concatenate([values, value_dot], axis=1), ((1,), (0,)))
        moved = dot(weighted.astype(jnp.bfloat16), values, ((1,), (0,)))
        if state is not None:
            shrink = jnp.exp2((state[0] - new_max) * (scale * LOG2_E))
            total, mass, both, moved = [
                new + old * shrink for new, old in zip((total, mass, both, moved), state[1:])
            ]
        state = (new_max, total, mass, both, moved)
    _, total, mass, both, moved = state
    inverse = 1.0 / total
    mixed = both[:, :HEAD_DIM] * inverse
    tangent = both[:, HEAD_DIM:] * inverse + (moved - mass * mixed) * (inverse * scale)
    out[:, :rows, :] = mixed.astype(jnp.bfloat16).reshape(sources, rows, HEAD_DIM)
    out[:, rows:, :] = tangent.astype(jnp.bfloat16).reshape(sources, rows, HEAD_DIM)


def attention(rows, blocks):
    return pl.pallas_call(
        functools.partial(attention_kernel, rows),
        out_shape=jax.ShapeDtypeStruct((blocks[0].shape[0], 2 * rows, HEAD_DIM), jnp.bfloat16),
        in_specs=[pl.BlockSpec(memory_space=pltpu.VMEM)] * len(blocks),
        out_specs=pl.BlockSpec(memory_space=pltpu.VMEM),
        compiler_params=pltpu.CompilerParams(vmem_limit_bytes=(8 + len(blocks)) * 2**20),
        name="attention",
    )(*blocks)


def unpack_kernel(packed, *refs):
    outs, sems = refs[:2], refs[2]
    row_tiles = outs[0].shape[0]
    copies = []
    for at, out in enumerate(outs):
        for row_tile in range(row_tiles):
            part, slot = slot_of(at, row_tile, row_tiles, packed.shape[0])
            sem = sems.at[len(copies)]
            copies.append(pltpu.make_async_copy(packed.at[part, :, slot], out.at[row_tile], sem))
            copies[-1].start()
    for copy in copies:
        copy.wait()


def unpack(packed, split):
    tiles = packed.reshape(split, HEADS, -1, TILE, HEAD_DIM)
    row_tiles = tiles.shape[2] * split // 2
    shape = (row_tiles, HEADS, TILE, HEAD_DIM)
    outs = pl.pallas_call(
        unpack_kernel,
        out_shape=[jax.ShapeDtypeStruct(shape, jnp.bfloat16)] * 2,
        in_specs=[pl.BlockSpec(memory_space=pltpu.VMEM)],
        out_specs=[pl.BlockSpec(memory_space=pltpu.HBM)] * 2,
        scratch_shapes=[pltpu.SemaphoreType.DMA((2 * row_tiles,))],
        compiler_params=pltpu.CompilerParams(vmem_limit_bytes=4 * 2**20),
        name="unpack",
    )(tiles)
    return tuple(from_tiles(out) for out in outs)


def solution(mesh):
    def local(query_main, key_main, value_main, query_tan, key_tan, value_tan, positions):
        rows = query_main.shape[0]
        peers, split, flat = plan(mesh, rows)
        teams = [[flat(peer, at ^ HEADS // 4) for at in range(HEADS)] for peer in range(peers)]
        groups = teams if split == 1 else [sum(teams, [])]

        def swap(value):
            return lax.all_to_all(value, AXES, 0, 0, axis_index_groups=groups, tiled=True)

        def from_peer(value, by):
            pairs = [
                (flat(peer, member), flat((peer + by) % peers, member))
                for peer in range(peers)
                for member in range(HEADS)
            ]
            return lax.ppermute(value, AXES, pairs)

        arrays = (query_main, key_main, value_main, query_tan, key_tan, value_tan)
        packed = pack(positions, arrays, split)
        here = swap(packed.reshape(HEADS * split, -1, HEAD_DIM))
        blocks = [here] + [from_peer(here, by) for by in range(1, peers)]
        return unpack(swap(attention(rows // split, blocks)), split)

    placed = (P(AXES, None),) * 6 + (P(AXES),)
    return jax.shard_map(
        local,
        mesh=mesh,
        in_specs=placed,
        out_specs=(P(AXES, None), P(AXES, None)),
        check_vma=False,
    )
```

```python
import functools
import math

import jax
import jax.numpy as jnp
from jax import lax
from jax.experimental import pallas as pl
from jax.experimental.pallas import tpu as pltpu
from jax.sharding import PartitionSpec as P

HEADS = 16
HEAD_DIM = 128
LOG2_E = math.log2(math.e)
AXES = ("seq", "head")
TILE = 8
PIECES = 4


def plan(mesh, rows):
    heads_axis = mesh.shape["head"]
    peers = mesh.shape["seq"] * heads_axis // HEADS
    assert mesh.shape["seq"] % peers == 0 and rows % TILE == 0

    def flat(peer, member):
        return (member // heads_axis * peers + peer) * heads_axis + member % heads_axis

    return peers, 1, flat


def as_tiles(array):
    rows, columns = array.shape
    return array.reshape(rows // TILE, TILE, columns // HEAD_DIM, HEAD_DIM).transpose(0, 2, 1, 3)


def from_tiles(tiles):
    row_tiles, heads = tiles.shape[:2]
    return tiles.transpose(0, 2, 1, 3).reshape(row_tiles * TILE, heads * HEAD_DIM)


def slot_of(at, row_tile, row_tiles, split):
    own = row_tiles // split
    return row_tile // own, at * own + row_tile % own


def pack_kernel(positions, *refs):
    arrays, (out, here, sems) = refs[:6], refs[6:]
    row_tiles = arrays[0].shape[0]
    split = out.shape[0]
    load = pltpu.make_async_copy(positions, here, sems.at[6 * row_tiles])
    load.start()
    copies = []
    for at, array in enumerate(arrays):
        for row_tile in range(row_tiles):
            part, slot = slot_of(at, row_tile, row_tiles, split)
            sem = sems.at[len(copies)]
            copies.append(pltpu.make_async_copy(array.at[row_tile], out.at[part, :, slot], sem))
            copies[-1].start()
    own = row_tiles // split
    token = lax.broadcasted_iota(jnp.int32, (TILE, HEAD_DIM), 0)
    lane = lax.broadcasted_iota(jnp.int32, (TILE, HEAD_DIM), 1)
    token = token + lane // (HEAD_DIM // own) * TILE
    load.wait()
    for part in range(split):
        place = jnp.zeros((TILE, HEAD_DIM), jnp.int32)
        for t in range(own * TILE):
            place = jnp.where(token == t, here[part * own * TILE + t], place)
        place = lax.shift_right_logical(place, lane % PIECES * 8) & 255
        place = place.astype(jnp.float32).astype(jnp.bfloat16)
        for h in range(HEADS):
            out[part, h, 6 * own] = place
    for copy in copies:
        copy.wait()


def pack(positions, arrays, split):
    tiles = [as_tiles(array) for array in arrays]
    row_tiles = tiles[0].shape[0]
    shape = (split, HEADS, 6 * row_tiles // split + 1, TILE, HEAD_DIM)
    return pl.pallas_call(
        pack_kernel,
        out_shape=pltpu.VMEM(shape, jnp.bfloat16),
        in_specs=[pl.BlockSpec(memory_space=pltpu.HBM)] * (1 + len(tiles)),
        out_specs=pl.BlockSpec(memory_space=pltpu.VMEM),
        scratch_shapes=[
            pltpu.SMEM(positions.shape, jnp.int32),
            pltpu.SemaphoreType.DMA((6 * row_tiles + 1,)),
        ],
        compiler_params=pltpu.CompilerParams(vmem_limit_bytes=56 * 2**20),
        name="pack",
    )(positions, *tiles)


def dot(a, b, contract):
    return lax.dot_general(a, b, (contract, ((), ())), preferred_element_type=jnp.float32)


def order_of(pair):
    high, low = pair
    return high.astype(jnp.int32) * 65536 + low.astype(jnp.int32)


def attention_kernel(rows, *refs):
    blocks, out = refs[:-1], refs[-1]
    sources = blocks[0].shape[0]
    count = sources * rows
    scale = HEAD_DIM ** (-0.5)

    def part(ref, at):
        return ref[:, at * rows : (at + 1) * rows, :].reshape(count, HEAD_DIM)

    def places(ref):
        row_tiles = rows // TILE
        packed = ref[:, 6 * rows :, :]
        if row_tiles == 1:
            return packed.reshape(count, HEAD_DIM)
        packed = packed.astype(jnp.float32)
        lane = lax.broadcasted_iota(jnp.int32, packed.shape, 2)
        span = HEAD_DIM // row_tiles
        split = [jnp.where(lane // span == half, packed, 0.0) for half in range(row_tiles)]
        return jnp.stack(split, axis=1).reshape(count, HEAD_DIM).astype(jnp.bfloat16)

    def weights(shape, axis, first):
        at = lax.broadcasted_iota(jnp.int32, shape, axis) % (HEAD_DIM * TILE // rows)
        chosen = jnp.where(at == first, 1.0, jnp.where(at == first + 1, 256.0, 0.0))
        return chosen.astype(jnp.bfloat16)

    own = blocks[0]
    queries = part(own, 0)
    query_pair = jnp.concatenate([part(own, 3), queries], axis=1)
    own_order = places(own)
    across = (HEAD_DIM, HEAD_DIM)
    query_order = order_of([dot(own_order, weights(across, 0, first), ((1,), (0,))) for first in (2, 0)])
    state = None
    for start in range(0, len(blocks), 2):
        group = blocks[start : start + 2]

        def keyed(at):
            return jnp.concatenate([part(ref, at) for ref in group], axis=0)

        keys, values, key_dot, value_dot = [keyed(at) for at in (1, 2, 4, 5)]
        order = jnp.concatenate([places(ref) for ref in group], axis=0)
        width = keys.shape[0]
        down = (8, HEAD_DIM)
        key_order = order_of([dot(weights(down, 1, first), order, ((1,), (1,))) for first in (2, 0)])
        wide_order = jnp.concatenate([query_order] * (width // HEAD_DIM), axis=1)
        visible = key_order[:1] <= wide_order
        scores = dot(queries, keys, ((1,), (1,)))
        scores = jnp.where(visible, scores, -1e30)
        key_pair = jnp.concatenate([keys, key_dot], axis=1)
        score_tan = dot(query_pair, key_pair, ((1,), (1,)))
        new_max = jnp.max(scores, axis=1, keepdims=True)
        if state is not None:
            new_max = jnp.maximum(new_max, state[0])
        expo = jnp.exp2((scores - new_max) * (scale * LOG2_E))
        weighted = expo * score_tan
        total = jnp.sum(expo, axis=1, keepdims=True)
        mass = jnp.sum(weighted, axis=1, keepdims=True)
        both = dot(expo.astype(jnp.bfloat16), jnp.concatenate([values, value_dot], axis=1), ((1,), (0,)))
        moved = dot(weighted.astype(jnp.bfloat16), values, ((1,), (0,)))
        if state is not None:
            shrink = jnp.exp2((state[0] - new_max) * (scale * LOG2_E))
            total, mass, both, moved = [
                new + old * shrink for new, old in zip((total, mass, both, moved), state[1:])
            ]
        state = (new_max, total, mass, both, moved)
    _, total, mass, both, moved = state
    inverse = 1.0 / total
    mixed = both[:, :HEAD_DIM] * inverse
    tangent = both[:, HEAD_DIM:] * inverse + (moved - mass * mixed) * (inverse * scale)
    out[:, :rows, :] = mixed.astype(jnp.bfloat16).reshape(sources, rows, HEAD_DIM)
    out[:, rows:, :] = tangent.astype(jnp.bfloat16).reshape(sources, rows, HEAD_DIM)


def attention(rows, blocks):
    return pl.pallas_call(
        functools.partial(attention_kernel, rows),
        out_shape=jax.ShapeDtypeStruct((blocks[0].shape[0], 2 * rows, HEAD_DIM), jnp.bfloat16),
        in_specs=[pl.BlockSpec(memory_space=pltpu.VMEM)] * len(blocks),
        out_specs=pl.BlockSpec(memory_space=pltpu.VMEM),
        compiler_params=pltpu.CompilerParams(vmem_limit_bytes=(8 + len(blocks)) * 2**20),
        name="attention",
    )(*blocks)


def unpack_kernel(packed, *refs):
    outs, sems = refs[:2], refs[2]
    row_tiles = outs[0].shape[0]
    copies = []
    for at, out in enumerate(outs):
        for row_tile in range(row_tiles):
            part, slot = slot_of(at, row_tile, row_tiles, packed.shape[0])
            sem = sems.at[len(copies)]
            copies.append(pltpu.make_async_copy(packed.at[part, :, slot], out.at[row_tile], sem))
            copies[-1].start()
    for copy in copies:
        copy.wait()


def unpack(packed, split):
    tiles = packed.reshape(split, HEADS, -1, TILE, HEAD_DIM)
    row_tiles = tiles.shape[2] * split // 2
    shape = (row_tiles, HEADS, TILE, HEAD_DIM)
    outs = pl.pallas_call(
        unpack_kernel,
        out_shape=[jax.ShapeDtypeStruct(shape, jnp.bfloat16)] * 2,
        in_specs=[pl.BlockSpec(memory_space=pltpu.VMEM)],
        out_specs=[pl.BlockSpec(memory_space=pltpu.HBM)] * 2,
        scratch_shapes=[pltpu.SemaphoreType.DMA((2 * row_tiles,))],
        compiler_params=pltpu.CompilerParams(vmem_limit_bytes=4 * 2**20),
        name="unpack",
    )(tiles)
    return tuple(from_tiles(out) for out in outs)


def solution(mesh):
    def local(query_main, key_main, value_main, query_tan, key_tan, value_tan, positions):
        rows = query_main.shape[0]
        peers, split, flat = plan(mesh, rows)
        teams = [[flat(peer, at ^ 11) for at in range(HEADS)] for peer in reversed(range(peers))]
        groups = teams if split == 1 else [sum(teams, [])]

        def swap(value):
            return lax.all_to_all(value, AXES, 0, 0, axis_index_groups=groups, tiled=True)

        def from_peer(value, by):
            pairs = [
                (flat(peer, member), flat((peer + by) % peers, member))
                for peer in range(peers)
                for member in range(HEADS)
            ]
            return lax.ppermute(value, AXES, pairs)

        arrays = (query_main, key_main, value_main, query_tan, key_tan, value_tan)
        packed = pack(positions, arrays, split)
        here = swap(packed.reshape(HEADS * split, -1, HEAD_DIM))
        blocks = [here] + [from_peer(here, by) for by in range(1, peers)]
        return unpack(swap(attention(rows // split, blocks)), split)

    placed = (P(AXES, None),) * 6 + (P(AXES),)
    return jax.shard_map(
        local,
        mesh=mesh,
        in_specs=placed,
        out_specs=(P(AXES, None), P(AXES, None)),
        check_vma=False,
    )
```

```python
import functools
import math

import jax
import jax.numpy as jnp
from jax import lax
from jax.experimental import pallas as pl
from jax.experimental.pallas import tpu as pltpu
from jax.sharding import PartitionSpec as P

HEADS = 16
HEAD_DIM = 128
LOG2_E = math.log2(math.e)
AXES = ("seq", "head")
TILE = 8
PIECES = 4


def plan(mesh, rows):
    heads_axis = mesh.shape["head"]
    peers = mesh.shape["seq"] * heads_axis // HEADS
    assert mesh.shape["seq"] % peers == 0 and rows % TILE == 0

    def flat(peer, member):
        return (member // heads_axis * peers + peer) * heads_axis + member % heads_axis

    return peers, 1, flat


def as_tiles(array):
    rows, columns = array.shape
    return array.reshape(rows // TILE, TILE, columns // HEAD_DIM, HEAD_DIM).transpose(0, 2, 1, 3)


def from_tiles(tiles):
    row_tiles, heads = tiles.shape[:2]
    return tiles.transpose(0, 2, 1, 3).reshape(row_tiles * TILE, heads * HEAD_DIM)


def slot_of(at, row_tile, row_tiles, split):
    own = row_tiles // split
    return row_tile // own, at * own + row_tile % own


def pack_kernel(positions, *refs):
    arrays, (out, here, sems) = refs[:6], refs[6:]
    row_tiles = arrays[0].shape[0]
    split = out.shape[0]
    load = pltpu.make_async_copy(positions, here, sems.at[6 * row_tiles])
    load.start()
    copies = []
    for at, array in enumerate(arrays):
        for row_tile in range(row_tiles):
            part, slot = slot_of(at, row_tile, row_tiles, split)
            sem = sems.at[len(copies)]
            copies.append(pltpu.make_async_copy(array.at[row_tile], out.at[part, :, slot], sem))
            copies[-1].start()
    own = row_tiles // split
    token = lax.broadcasted_iota(jnp.int32, (TILE, HEAD_DIM), 0)
    lane = lax.broadcasted_iota(jnp.int32, (TILE, HEAD_DIM), 1)
    token = token + lane // (HEAD_DIM // own) * TILE
    load.wait()
    for part in range(split):
        place = jnp.zeros((TILE, HEAD_DIM), jnp.int32)
        for t in range(own * TILE):
            place = jnp.where(token == t, here[part * own * TILE + t], place)
        place = lax.shift_right_logical(place, lane % PIECES * 8) & 255
        place = place.astype(jnp.float32).astype(jnp.bfloat16)
        for h in range(HEADS):
            out[part, h, 6 * own] = place
    for copy in copies:
        copy.wait()


def pack(positions, arrays, split):
    tiles = [as_tiles(array) for array in arrays]
    row_tiles = tiles[0].shape[0]
    shape = (split, HEADS, 6 * row_tiles // split + 1, TILE, HEAD_DIM)
    return pl.pallas_call(
        pack_kernel,
        out_shape=pltpu.VMEM(shape, jnp.bfloat16),
        in_specs=[pl.BlockSpec(memory_space=pltpu.HBM)] * (1 + len(tiles)),
        out_specs=pl.BlockSpec(memory_space=pltpu.VMEM),
        scratch_shapes=[
            pltpu.SMEM(positions.shape, jnp.int32),
            pltpu.SemaphoreType.DMA((6 * row_tiles + 1,)),
        ],
        compiler_params=pltpu.CompilerParams(vmem_limit_bytes=56 * 2**20),
        name="pack",
    )(positions, *tiles)


def dot(a, b, contract):
    return lax.dot_general(a, b, (contract, ((), ())), preferred_element_type=jnp.float32)


def order_of(pair):
    high, low = pair
    return high.astype(jnp.int32) * 65536 + low.astype(jnp.int32)


def attention_kernel(rows, *refs):
    blocks, out = refs[:-1], refs[-1]
    sources = blocks[0].shape[0]
    count = sources * rows
    scale = HEAD_DIM ** (-0.5)

    def part(ref, at):
        return ref[:, at * rows : (at + 1) * rows, :].reshape(count, HEAD_DIM)

    def places(ref):
        row_tiles = rows // TILE
        packed = ref[:, 6 * rows :, :]
        if row_tiles == 1:
            return packed.reshape(count, HEAD_DIM)
        packed = packed.astype(jnp.float32)
        lane = lax.broadcasted_iota(jnp.int32, packed.shape, 2)
        span = HEAD_DIM // row_tiles
        split = [jnp.where(lane // span == half, packed, 0.0) for half in range(row_tiles)]
        return jnp.stack(split, axis=1).reshape(count, HEAD_DIM).astype(jnp.bfloat16)

    def weights(shape, axis, first):
        at = lax.broadcasted_iota(jnp.int32, shape, axis) % (HEAD_DIM * TILE // rows)
        chosen = jnp.where(at == first, 1.0, jnp.where(at == first + 1, 256.0, 0.0))
        return chosen.astype(jnp.bfloat16)

    own = blocks[0]
    queries = part(own, 0)
    query_pair = jnp.concatenate([part(own, 3), queries], axis=1)
    own_order = places(own)
    across = (HEAD_DIM, HEAD_DIM)
    query_order = order_of([dot(own_order, weights(across, 0, first), ((1,), (0,))) for first in (2, 0)])
    state = None
    for start in range(0, len(blocks), 2):
        group = blocks[start : start + 2]

        def keyed(at):
            return jnp.concatenate([part(ref, at) for ref in group], axis=0)

        keys, values, key_dot, value_dot = [keyed(at) for at in (1, 2, 4, 5)]
        order = jnp.concatenate([places(ref) for ref in group], axis=0)
        width = keys.shape[0]
        down = (8, HEAD_DIM)
        key_order = order_of([dot(weights(down, 1, first), order, ((1,), (1,))) for first in (2, 0)])
        wide_order = jnp.concatenate([query_order] * (width // HEAD_DIM), axis=1)
        visible = key_order[:1] <= wide_order
        scores = dot(queries, keys, ((1,), (1,)))
        scores = jnp.where(visible, scores, -1e30)
        key_pair = jnp.concatenate([keys, key_dot], axis=1)
        score_tan = dot(query_pair, key_pair, ((1,), (1,)))
        new_max = jnp.max(scores, axis=1, keepdims=True)
        if state is not None:
            new_max = jnp.maximum(new_max, state[0])
        expo = jnp.exp2((scores - new_max) * (scale * LOG2_E))
        weighted = expo * score_tan
        total = jnp.sum(expo, axis=1, keepdims=True)
        mass = jnp.sum(weighted, axis=1, keepdims=True)
        both = dot(expo.astype(jnp.bfloat16), jnp.concatenate([values, value_dot], axis=1), ((1,), (0,)))
        moved = dot(weighted.astype(jnp.bfloat16), values, ((1,), (0,)))
        if state is not None:
            shrink = jnp.exp2((state[0] - new_max) * (scale * LOG2_E))
            total, mass, both, moved = [
                new + old * shrink for new, old in zip((total, mass, both, moved), state[1:])
            ]
        state = (new_max, total, mass, both, moved)
    _, total, mass, both, moved = state
    inverse = 1.0 / total
    mixed = both[:, :HEAD_DIM] * inverse
    tangent = both[:, HEAD_DIM:] * inverse + (moved - mass * mixed) * (inverse * scale)
    out[:, :rows, :] = mixed.astype(jnp.bfloat16).reshape(sources, rows, HEAD_DIM)
    out[:, rows:, :] = tangent.astype(jnp.bfloat16).reshape(sources, rows, HEAD_DIM)


def attention(rows, blocks):
    return pl.pallas_call(
        functools.partial(attention_kernel, rows),
        out_shape=jax.ShapeDtypeStruct((blocks[0].shape[0], 2 * rows, HEAD_DIM), jnp.bfloat16),
        in_specs=[pl.BlockSpec(memory_space=pltpu.VMEM)] * len(blocks),
        out_specs=pl.BlockSpec(memory_space=pltpu.VMEM),
        compiler_params=pltpu.CompilerParams(vmem_limit_bytes=(8 + len(blocks)) * 2**20),
        name="attention",
    )(*blocks)


def unpack_kernel(packed, *refs):
    outs, sems = refs[:2], refs[2]
    row_tiles = outs[0].shape[0]
    copies = []
    for at, out in enumerate(outs):
        for row_tile in range(row_tiles):
            part, slot = slot_of(at, row_tile, row_tiles, packed.shape[0])
            sem = sems.at[len(copies)]
            copies.append(pltpu.make_async_copy(packed.at[part, :, slot], out.at[row_tile], sem))
            copies[-1].start()
    for copy in copies:
        copy.wait()


def unpack(packed, split):
    tiles = packed.reshape(split, HEADS, -1, TILE, HEAD_DIM)
    row_tiles = tiles.shape[2] * split // 2
    shape = (row_tiles, HEADS, TILE, HEAD_DIM)
    outs = pl.pallas_call(
        unpack_kernel,
        out_shape=[jax.ShapeDtypeStruct(shape, jnp.bfloat16)] * 2,
        in_specs=[pl.BlockSpec(memory_space=pltpu.VMEM)],
        out_specs=[pl.BlockSpec(memory_space=pltpu.HBM)] * 2,
        scratch_shapes=[pltpu.SemaphoreType.DMA((2 * row_tiles,))],
        compiler_params=pltpu.CompilerParams(vmem_limit_bytes=4 * 2**20),
        name="unpack",
    )(tiles)
    return tuple(from_tiles(out) for out in outs)


def solution(mesh):
    def local(query_main, key_main, value_main, query_tan, key_tan, value_tan, positions):
        rows = query_main.shape[0]
        peers, split, flat = plan(mesh, rows)
        bits = HEADS.bit_length() - 1
        order = [int(f"{head:0{bits}b}"[::-1], 2) ^ 11 for head in range(HEADS)]
        teams = [[flat(peer, member) for member in order] for peer in range(peers)]
        groups = teams if split == 1 else [sum(teams, [])]

        def swap(value):
            return lax.all_to_all(value, AXES, 0, 0, axis_index_groups=groups, tiled=True)

        def from_peer(value, by):
            pairs = [
                (flat(peer, member), flat((peer + by) % peers, member))
                for peer in range(peers)
                for member in range(HEADS)
            ]
            return lax.ppermute(value, AXES, pairs)

        arrays = (query_main, key_main, value_main, query_tan, key_tan, value_tan)
        packed = pack(positions, arrays, split)
        here = swap(packed.reshape(HEADS * split, -1, HEAD_DIM))
        blocks = [here] + [from_peer(here, by) for by in range(1, peers)]
        return unpack(swap(attention(rows // split, blocks)), split)

    placed = (P(AXES, None),) * 6 + (P(AXES),)
    return jax.shard_map(
        local,
        mesh=mesh,
        in_specs=placed,
        out_specs=(P(AXES, None), P(AXES, None)),
        check_vma=False,
    )
```

```python
import functools
import math

import jax
import jax.numpy as jnp
from jax import lax
from jax.experimental import pallas as pl
from jax.experimental.pallas import tpu as pltpu
from jax.sharding import PartitionSpec as P

HEADS = 16
HEAD_DIM = 128
LOG2_E = math.log2(math.e)
AXES = ("seq", "head")
TILE = 8
MIDDLE = 11
ARRAYS = 6
PIECES = 4


def plan(mesh):
    heads_axis = mesh.shape["head"]
    peers = mesh.shape["seq"] * heads_axis // HEADS
    assert mesh.shape["seq"] % peers == 0

    def flat(peer, head):
        member = head ^ MIDDLE
        return (member // heads_axis * peers + peer) * heads_axis + member % heads_axis

    return [[flat(peer, head) for head in range(HEADS)] for peer in range(peers)]


def as_tiles(array):
    rows, columns = array.shape
    return array.reshape(rows // TILE, TILE, columns // HEAD_DIM, HEAD_DIM).transpose(0, 2, 1, 3)


def from_tiles(tiles):
    row_tiles, heads = tiles.shape[:2]
    return tiles.transpose(0, 2, 1, 3).reshape(row_tiles * TILE, heads * HEAD_DIM)


def pack_kernel(positions, *refs):
    arrays, (out, here, sems) = refs[:ARRAYS], refs[ARRAYS:]
    row_tiles = arrays[0].shape[0]
    last = ARRAYS * row_tiles
    load = pltpu.make_async_copy(positions, here, sems.at[last])
    load.start()
    copies = []
    for at, array in enumerate(arrays):
        for tile in range(row_tiles):
            slot = at * row_tiles + tile
            copies.append(pltpu.make_async_copy(array.at[tile], out.at[:, slot], sems.at[slot]))
            copies[-1].start()
    token = lax.broadcasted_iota(jnp.int32, (TILE, HEAD_DIM), 0)
    lane = lax.broadcasted_iota(jnp.int32, (TILE, HEAD_DIM), 1)
    token = token + lane // (HEAD_DIM // row_tiles) * TILE
    place = jnp.zeros((TILE, HEAD_DIM), jnp.int32)
    load.wait()
    for t in range(row_tiles * TILE):
        place = jnp.where(token == t, here[t], place)
    place = lax.shift_right_logical(place, lane % PIECES * 8) & 255
    place = place.astype(jnp.float32).astype(jnp.bfloat16)
    for head in range(HEADS):
        out[head, last] = place
    for copy in copies:
        copy.wait()


def pack(positions, arrays):
    tiles = [as_tiles(array) for array in arrays]
    slots = ARRAYS * tiles[0].shape[0] + 1
    packed = pl.pallas_call(
        pack_kernel,
        out_shape=pltpu.VMEM((HEADS, slots, TILE, HEAD_DIM), jnp.bfloat16),
        in_specs=[pl.BlockSpec(memory_space=pltpu.HBM)] * (1 + ARRAYS),
        out_specs=pl.BlockSpec(memory_space=pltpu.VMEM),
        scratch_shapes=[
            pltpu.SMEM(positions.shape, jnp.int32),
            pltpu.SemaphoreType.DMA((slots,)),
        ],
        compiler_params=pltpu.CompilerParams(vmem_limit_bytes=56 * 2**20),
        name="pack",
    )(positions, *tiles)
    return packed.reshape(HEADS, slots * TILE, HEAD_DIM)


def dot(a, b, contract):
    return lax.dot_general(a, b, (contract, ((), ())), preferred_element_type=jnp.float32)


def order_of(pair):
    high, low = pair
    return high.astype(jnp.int32) * 65536 + low.astype(jnp.int32)


def attention_kernel(rows, *refs):
    blocks, out = refs[:-1], refs[-1]
    count = HEADS * rows
    scale = HEAD_DIM ** (-0.5)
    lanes = HEAD_DIM * TILE // rows

    def part(ref, at):
        return ref[:, at * rows : (at + 1) * rows, :].reshape(count, HEAD_DIM)

    def places(ref):
        packed = ref[:, ARRAYS * rows :, :].astype(jnp.float32)
        lane = lax.broadcasted_iota(jnp.int32, packed.shape, 2)
        parts = [jnp.where(lane // lanes == at, packed, 0.0) for at in range(rows // TILE)]
        return jnp.stack(parts, axis=1).reshape(count, HEAD_DIM).astype(jnp.bfloat16)

    def weights(shape, axis, first):
        at = lax.broadcasted_iota(jnp.int32, shape, axis) % lanes
        chosen = jnp.where(at == first, 1.0, jnp.where(at == first + 1, 256.0, 0.0))
        return chosen.astype(jnp.bfloat16)

    own = blocks[0]
    queries = part(own, 0)
    query_pair = jnp.concatenate([part(own, 3), queries], axis=1)
    own_order = places(own)
    across = (HEAD_DIM, HEAD_DIM)
    query_order = order_of([dot(own_order, weights(across, 0, first), ((1,), (0,))) for first in (2, 0)])
    state = None
    for start in range(0, len(blocks), 2):
        group = blocks[start : start + 2]

        def keyed(at):
            return jnp.concatenate([part(ref, at) for ref in group], axis=0)

        keys, values, key_dot, value_dot = [keyed(at) for at in (1, 2, 4, 5)]
        order = jnp.concatenate([places(ref) for ref in group], axis=0)
        width = keys.shape[0]
        down = (8, HEAD_DIM)
        key_order = order_of([dot(weights(down, 1, first), order, ((1,), (1,))) for first in (2, 0)])
        wide_order = jnp.concatenate([query_order] * (width // HEAD_DIM), axis=1)
        visible = key_order[:1] <= wide_order
        scores = dot(queries, keys, ((1,), (1,)))
        scores = jnp.where(visible, scores, -1e30)
        key_pair = jnp.concatenate([keys, key_dot], axis=1)
        score_tan = dot(query_pair, key_pair, ((1,), (1,)))
        new_max = jnp.max(scores, axis=1, keepdims=True)
        if state is not None:
            new_max = jnp.maximum(new_max, state[0])
        expo = jnp.exp2((scores - new_max) * (scale * LOG2_E))
        total = jnp.sum(expo, axis=1, keepdims=True)
        both = dot(expo.astype(jnp.bfloat16), jnp.concatenate([values, value_dot], axis=1), ((1,), (0,)))
        summed = jnp.concatenate([values, jnp.ones_like(values)], axis=1)
        moved = dot((expo * score_tan).astype(jnp.bfloat16), summed, ((1,), (0,)))
        if state is not None:
            shrink = jnp.exp2((state[0] - new_max) * (scale * LOG2_E))
            total, both, moved = [new + old * shrink for new, old in zip((total, both, moved), state[1:])]
        state = (new_max, total, both, moved)
    _, total, both, moved = state
    inverse = 1.0 / total
    mixed = both[:, :HEAD_DIM] * inverse
    weighted, mass = moved[:, :HEAD_DIM], moved[:, HEAD_DIM:]
    tangent = both[:, HEAD_DIM:] * inverse + (weighted - mass * mixed) * (inverse * scale)
    out[:, :rows, :] = mixed.astype(jnp.bfloat16).reshape(HEADS, rows, HEAD_DIM)
    out[:, rows:, :] = tangent.astype(jnp.bfloat16).reshape(HEADS, rows, HEAD_DIM)


def attention(rows, blocks):
    return pl.pallas_call(
        functools.partial(attention_kernel, rows),
        out_shape=jax.ShapeDtypeStruct((HEADS, 2 * rows, HEAD_DIM), jnp.bfloat16),
        in_specs=[pl.BlockSpec(memory_space=pltpu.VMEM)] * len(blocks),
        out_specs=pl.BlockSpec(memory_space=pltpu.VMEM),
        compiler_params=pltpu.CompilerParams(vmem_limit_bytes=(8 + len(blocks)) * 2**20),
        name="attention",
    )(*blocks)


def unpack_kernel(packed, *refs):
    outs, sems = refs[:2], refs[2]
    row_tiles = outs[0].shape[0]
    copies = []
    for at, out in enumerate(outs):
        for tile in range(row_tiles):
            slot = at * row_tiles + tile
            copies.append(pltpu.make_async_copy(packed.at[:, slot], out.at[tile], sems.at[slot]))
            copies[-1].start()
    for copy in copies:
        copy.wait()


def unpack(packed):
    slots = packed.shape[1] // TILE
    shape = (slots // 2, HEADS, TILE, HEAD_DIM)
    outs = pl.pallas_call(
        unpack_kernel,
        out_shape=[jax.ShapeDtypeStruct(shape, jnp.bfloat16)] * 2,
        in_specs=[pl.BlockSpec(memory_space=pltpu.VMEM)],
        out_specs=[pl.BlockSpec(memory_space=pltpu.HBM)] * 2,
        scratch_shapes=[pltpu.SemaphoreType.DMA((slots,))],
        compiler_params=pltpu.CompilerParams(vmem_limit_bytes=4 * 2**20),
        name="unpack",
    )(packed.reshape(HEADS, slots, TILE, HEAD_DIM))
    return tuple(from_tiles(out) for out in outs)


def solution(mesh):
    teams = plan(mesh)

    def swap(value):
        return lax.all_to_all(value, AXES, 0, 0, axis_index_groups=teams, tiled=True)

    def from_peer(value, by):
        pairs = [pair for at, team in enumerate(teams) for pair in zip(team, teams[(at + by) % len(teams)])]
        return lax.ppermute(value, AXES, pairs)

    def local(query_main, key_main, value_main, query_tan, key_tan, value_tan, positions):
        rows = query_main.shape[0]
        arrays = (query_main, key_main, value_main, query_tan, key_tan, value_tan)
        here = swap(pack(positions, arrays))
        blocks = [here] + [from_peer(here, by) for by in range(1, len(teams))]
        return unpack(swap(attention(rows, blocks)))

    placed = (P(AXES, None),) * 6 + (P(AXES),)
    return jax.shard_map(
        local,
        mesh=mesh,
        in_specs=placed,
        out_specs=(P(AXES, None), P(AXES, None)),
        check_vma=False,
    )
```

```python
import functools
import math

import jax
import jax.numpy as jnp
from jax import lax
from jax.experimental import pallas as pl
from jax.experimental.pallas import tpu as pltpu
from jax.sharding import PartitionSpec as P

HEADS = 16
HEAD_DIM = 128
LOG2_E = math.log2(math.e)
AXES = ("seq", "head")
TILE = 8
MIDDLE = 15
ARRAYS = 6
PIECES = 4


def plan(mesh):
    heads_axis = mesh.shape["head"]
    peers = mesh.shape["seq"] * heads_axis // HEADS
    assert mesh.shape["seq"] % peers == 0

    def flat(peer, head):
        member = head ^ MIDDLE
        return (member // heads_axis * peers + peer) * heads_axis + member % heads_axis

    return [[flat(peer, head) for head in range(HEADS)] for peer in range(peers)]


def as_tiles(array):
    rows, columns = array.shape
    return array.reshape(rows // TILE, TILE, columns // HEAD_DIM, HEAD_DIM).transpose(0, 2, 1, 3)


def from_tiles(tiles):
    row_tiles, heads = tiles.shape[:2]
    return tiles.transpose(0, 2, 1, 3).reshape(row_tiles * TILE, heads * HEAD_DIM)


def pack_kernel(positions, *refs):
    arrays, (out, here, sems) = refs[:ARRAYS], refs[ARRAYS:]
    row_tiles = arrays[0].shape[0]
    last = ARRAYS * row_tiles
    load = pltpu.make_async_copy(positions, here, sems.at[last])
    load.start()
    copies = []
    for at, array in enumerate(arrays):
        for tile in range(row_tiles):
            slot = at * row_tiles + tile
            copies.append(pltpu.make_async_copy(array.at[tile], out.at[:, slot], sems.at[slot]))
            copies[-1].start()
    token = lax.broadcasted_iota(jnp.int32, (TILE, HEAD_DIM), 0)
    lane = lax.broadcasted_iota(jnp.int32, (TILE, HEAD_DIM), 1)
    token = token + lane // (HEAD_DIM // row_tiles) * TILE
    place = jnp.zeros((TILE, HEAD_DIM), jnp.int32)
    load.wait()
    for t in range(row_tiles * TILE):
        place = jnp.where(token == t, here[t], place)
    place = lax.shift_right_logical(place, lane % PIECES * 8) & 255
    place = place.astype(jnp.float32).astype(jnp.bfloat16)
    for head in range(HEADS):
        out[head, last] = place
    for copy in copies:
        copy.wait()


def pack(positions, arrays):
    tiles = [as_tiles(array) for array in arrays]
    slots = ARRAYS * tiles[0].shape[0] + 1
    packed = pl.pallas_call(
        pack_kernel,
        out_shape=pltpu.VMEM((HEADS, slots, TILE, HEAD_DIM), jnp.bfloat16),
        in_specs=[pl.BlockSpec(memory_space=pltpu.HBM)] * (1 + ARRAYS),
        out_specs=pl.BlockSpec(memory_space=pltpu.VMEM),
        scratch_shapes=[
            pltpu.SMEM(positions.shape, jnp.int32),
            pltpu.SemaphoreType.DMA((slots,)),
        ],
        compiler_params=pltpu.CompilerParams(vmem_limit_bytes=56 * 2**20),
        name="pack",
    )(positions, *tiles)
    return packed.reshape(HEADS, slots * TILE, HEAD_DIM)


def dot(a, b, contract):
    return lax.dot_general(a, b, (contract, ((), ())), preferred_element_type=jnp.float32)


def order_of(pair):
    high, low = pair
    return high.astype(jnp.int32) * 65536 + low.astype(jnp.int32)


def attention_kernel(rows, *refs):
    blocks, out = refs[:-1], refs[-1]
    count = HEADS * rows
    scale = HEAD_DIM ** (-0.5)
    lanes = HEAD_DIM * TILE // rows

    def part(ref, at):
        return ref[:, at * rows : (at + 1) * rows, :].reshape(count, HEAD_DIM)

    def places(ref):
        packed = ref[:, ARRAYS * rows :, :].astype(jnp.float32)
        lane = lax.broadcasted_iota(jnp.int32, packed.shape, 2)
        parts = [jnp.where(lane // lanes == at, packed, 0.0) for at in range(rows // TILE)]
        return jnp.stack(parts, axis=1).reshape(count, HEAD_DIM).astype(jnp.bfloat16)

    def weights(shape, axis, first):
        at = lax.broadcasted_iota(jnp.int32, shape, axis) % lanes
        chosen = jnp.where(at == first, 1.0, jnp.where(at == first + 1, 256.0, 0.0))
        return chosen.astype(jnp.bfloat16)

    own = blocks[0]
    queries = part(own, 0)
    query_pair = jnp.concatenate([part(own, 3), queries], axis=1)
    own_order = places(own)
    across = (HEAD_DIM, HEAD_DIM)
    query_order = order_of([dot(own_order, weights(across, 0, first), ((1,), (0,))) for first in (2, 0)])
    state = None
    for start in range(0, len(blocks), 2):
        group = blocks[start : start + 2]

        def keyed(at):
            return jnp.concatenate([part(ref, at) for ref in group], axis=0)

        keys, values, key_dot, value_dot = [keyed(at) for at in (1, 2, 4, 5)]
        order = jnp.concatenate([places(ref) for ref in group], axis=0)
        width = keys.shape[0]
        down = (8, HEAD_DIM)
        key_order = order_of([dot(weights(down, 1, first), order, ((1,), (1,))) for first in (2, 0)])
        wide_order = jnp.concatenate([query_order] * (width // HEAD_DIM), axis=1)
        visible = key_order[:1] <= wide_order
        scores = dot(queries, keys, ((1,), (1,)))
        scores = jnp.where(visible, scores, -1e30)
        key_pair = jnp.concatenate([keys, key_dot], axis=1)
        score_tan = dot(query_pair, key_pair, ((1,), (1,)))
        new_max = jnp.max(scores, axis=1, keepdims=True)
        if state is not None:
            new_max = jnp.maximum(new_max, state[0])
        expo = jnp.exp2((scores - new_max) * (scale * LOG2_E))
        total = jnp.sum(expo, axis=1, keepdims=True)
        both = dot(expo.astype(jnp.bfloat16), jnp.concatenate([values, value_dot], axis=1), ((1,), (0,)))
        summed = jnp.concatenate([values, jnp.ones_like(values)], axis=1)
        moved = dot((expo * score_tan).astype(jnp.bfloat16), summed, ((1,), (0,)))
        if state is not None:
            shrink = jnp.exp2((state[0] - new_max) * (scale * LOG2_E))
            total, both, moved = [new + old * shrink for new, old in zip((total, both, moved), state[1:])]
        state = (new_max, total, both, moved)
    _, total, both, moved = state
    inverse = 1.0 / total
    mixed = both[:, :HEAD_DIM] * inverse
    weighted, mass = moved[:, :HEAD_DIM], moved[:, HEAD_DIM:]
    tangent = both[:, HEAD_DIM:] * inverse + (weighted - mass * mixed) * (inverse * scale)
    out[:, :rows, :] = mixed.astype(jnp.bfloat16).reshape(HEADS, rows, HEAD_DIM)
    out[:, rows:, :] = tangent.astype(jnp.bfloat16).reshape(HEADS, rows, HEAD_DIM)


def attention(rows, blocks):
    return pl.pallas_call(
        functools.partial(attention_kernel, rows),
        out_shape=jax.ShapeDtypeStruct((HEADS, 2 * rows, HEAD_DIM), jnp.bfloat16),
        in_specs=[pl.BlockSpec(memory_space=pltpu.VMEM)] * len(blocks),
        out_specs=pl.BlockSpec(memory_space=pltpu.VMEM),
        compiler_params=pltpu.CompilerParams(vmem_limit_bytes=(8 + len(blocks)) * 2**20),
        name="attention",
    )(*blocks)


def unpack_kernel(packed, *refs):
    outs, sems = refs[:2], refs[2]
    row_tiles = outs[0].shape[0]
    copies = []
    for at, out in enumerate(outs):
        for tile in range(row_tiles):
            slot = at * row_tiles + tile
            copies.append(pltpu.make_async_copy(packed.at[:, slot], out.at[tile], sems.at[slot]))
            copies[-1].start()
    for copy in copies:
        copy.wait()


def unpack(packed):
    slots = packed.shape[1] // TILE
    shape = (slots // 2, HEADS, TILE, HEAD_DIM)
    outs = pl.pallas_call(
        unpack_kernel,
        out_shape=[jax.ShapeDtypeStruct(shape, jnp.bfloat16)] * 2,
        in_specs=[pl.BlockSpec(memory_space=pltpu.VMEM)],
        out_specs=[pl.BlockSpec(memory_space=pltpu.HBM)] * 2,
        scratch_shapes=[pltpu.SemaphoreType.DMA((slots,))],
        compiler_params=pltpu.CompilerParams(vmem_limit_bytes=4 * 2**20),
        name="unpack",
    )(packed.reshape(HEADS, slots, TILE, HEAD_DIM))
    return tuple(from_tiles(out) for out in outs)


def solution(mesh):
    teams = plan(mesh)

    def swap(value):
        return lax.all_to_all(value, AXES, 0, 0, axis_index_groups=teams, tiled=True)

    def from_peer(value, by):
        pairs = [pair for at, team in enumerate(teams) for pair in zip(team, teams[(at + by) % len(teams)])]
        return lax.ppermute(value, AXES, pairs)

    def local(query_main, key_main, value_main, query_tan, key_tan, value_tan, positions):
        rows = query_main.shape[0]
        arrays = (query_main, key_main, value_main, query_tan, key_tan, value_tan)
        here = swap(pack(positions, arrays))
        blocks = [here] + [from_peer(here, by) for by in range(1, len(teams))]
        return unpack(swap(attention(rows, blocks)))

    placed = (P(AXES, None),) * 6 + (P(AXES),)
    return jax.shard_map(
        local,
        mesh=mesh,
        in_specs=placed,
        out_specs=(P(AXES, None), P(AXES, None)),
        check_vma=False,
    )
```

```python
import functools
import math

import jax
import jax.numpy as jnp
from jax import lax
from jax.experimental import pallas as pl
from jax.experimental.pallas import tpu as pltpu
from jax.sharding import PartitionSpec as P

HEADS = 16
HEAD_DIM = 128
LOG2_E = math.log2(math.e)
AXES = ("seq", "head")
TILE = 8
MIDDLE = 11
ARRAYS = 6
BLOCK = 128
PIECES = 4


def plan(mesh):
    heads_axis = mesh.shape["head"]
    peers = mesh.shape["seq"] * heads_axis // HEADS
    assert mesh.shape["seq"] % peers == 0

    def flat(peer, head):
        member = head ^ MIDDLE
        return (member // heads_axis * peers + peer) * heads_axis + member % heads_axis

    return [[flat(peer, head) for head in range(HEADS)] for peer in range(peers)]


def as_tiles(array):
    rows, columns = array.shape
    return array.reshape(rows // TILE, TILE, columns // HEAD_DIM, HEAD_DIM).transpose(0, 2, 1, 3)


def from_tiles(tiles):
    row_tiles, heads = tiles.shape[:2]
    return tiles.transpose(0, 2, 1, 3).reshape(row_tiles * TILE, heads * HEAD_DIM)


def pack_kernel(positions, *refs):
    arrays, (out, here, sems) = refs[:ARRAYS], refs[ARRAYS:]
    row_tiles = arrays[0].shape[0]
    last = ARRAYS * row_tiles
    load = pltpu.make_async_copy(positions, here, sems.at[last])
    load.start()
    copies = []
    for at, array in enumerate(arrays):
        for tile in range(row_tiles):
            slot = at * row_tiles + tile
            copies.append(pltpu.make_async_copy(array.at[tile], out.at[:, slot], sems.at[slot]))
            copies[-1].start()
    token = lax.broadcasted_iota(jnp.int32, (TILE, HEAD_DIM), 0)
    lane = lax.broadcasted_iota(jnp.int32, (TILE, HEAD_DIM), 1)
    token = token + lane // (HEAD_DIM // row_tiles) * TILE
    place = jnp.zeros((TILE, HEAD_DIM), jnp.int32)
    load.wait()
    for t in range(row_tiles * TILE):
        place = jnp.where(token == t, here[t], place)
    place = lax.shift_right_logical(place, lane % PIECES * 8) & 255
    place = place.astype(jnp.float32).astype(jnp.bfloat16)
    for head in range(HEADS):
        out[head, last] = place
    for copy in copies:
        copy.wait()


def pack(positions, arrays):
    tiles = [as_tiles(array) for array in arrays]
    slots = ARRAYS * tiles[0].shape[0] + 1
    packed = pl.pallas_call(
        pack_kernel,
        out_shape=pltpu.VMEM((HEADS, slots, TILE, HEAD_DIM), jnp.bfloat16),
        in_specs=[pl.BlockSpec(memory_space=pltpu.HBM)] * (1 + ARRAYS),
        out_specs=pl.BlockSpec(memory_space=pltpu.VMEM),
        scratch_shapes=[
            pltpu.SMEM(positions.shape, jnp.int32),
            pltpu.SemaphoreType.DMA((slots,)),
        ],
        compiler_params=pltpu.CompilerParams(vmem_limit_bytes=56 * 2**20),
        name="pack",
    )(positions, *tiles)
    return packed.reshape(HEADS, slots * TILE, HEAD_DIM)


def dot(a, b, contract):
    return lax.dot_general(a, b, (contract, ((), ())), preferred_element_type=jnp.float32)


def order_of(pair):
    high, low = pair
    return high.astype(jnp.int32) * 65536 + low.astype(jnp.int32)


def attention_kernel(rows, *refs):
    blocks, out = refs[:-1], refs[-1]
    count = HEADS * rows
    scale = HEAD_DIM ** (-0.5)
    lanes = HEAD_DIM * TILE // rows

    def part(ref, at):
        return ref[:, at * rows : (at + 1) * rows, :].reshape(count, HEAD_DIM)

    def places(ref):
        packed = ref[:, ARRAYS * rows :, :].astype(jnp.float32)
        lane = lax.broadcasted_iota(jnp.int32, packed.shape, 2)
        parts = [jnp.where(lane // lanes == at, packed, 0.0) for at in range(rows // TILE)]
        return jnp.stack(parts, axis=1).reshape(count, HEAD_DIM).astype(jnp.bfloat16)

    def weights(shape, axis, first):
        at = lax.broadcasted_iota(jnp.int32, shape, axis) % lanes
        chosen = jnp.where(at == first, 1.0, jnp.where(at == first + 1, 256.0, 0.0))
        return chosen.astype(jnp.bfloat16)

    own = blocks[0]
    all_queries, all_query_dot, own_order = part(own, 0), part(own, 3), places(own)
    across, down = (HEAD_DIM, HEAD_DIM), (8, HEAD_DIM)
    query_order = order_of([dot(own_order, weights(across, 0, first), ((1,), (0,))) for first in (2, 0)])
    groups = [blocks[start : start + 2] for start in range(0, len(blocks), 2)]
    keyed = []
    for group in groups:
        keys, values, key_dot, value_dot, order = [
            jnp.concatenate(each, axis=0)
            for each in zip(*[[part(ref, at) for at in (1, 2, 4, 5)] + [places(ref)] for ref in group])
        ]
        key_order = order_of([dot(weights(down, 1, first), order, ((1,), (1,))) for first in (2, 0)])
        key_pair = jnp.concatenate([keys, key_dot], axis=1)
        value_pair = jnp.concatenate([values, value_dot], axis=1)
        summed = jnp.concatenate([values, jnp.ones_like(values)], axis=1)
        keyed.append((keys, key_pair, value_pair, summed, key_order[:1]))
    for block in range(count // BLOCK):
        here = slice(block * BLOCK, (block + 1) * BLOCK)
        queries = all_queries[here]
        query_pair = jnp.concatenate([all_query_dot[here], queries], axis=1)
        state = None
        for keys, key_pair, value_pair, summed, key_order in keyed:
            wide_order = jnp.concatenate([query_order[here]] * (keys.shape[0] // HEAD_DIM), axis=1)
            scores = dot(queries, keys, ((1,), (1,)))
            scores = jnp.where(key_order <= wide_order, scores, -1e30)
            score_tan = dot(query_pair, key_pair, ((1,), (1,)))
            new_max = jnp.max(scores, axis=1, keepdims=True)
            if state is not None:
                new_max = jnp.maximum(new_max, state[0])
            expo = jnp.exp2((scores - new_max) * (scale * LOG2_E))
            total = jnp.sum(expo, axis=1, keepdims=True)
            both = dot(expo.astype(jnp.bfloat16), value_pair, ((1,), (0,)))
            moved = dot((expo * score_tan).astype(jnp.bfloat16), summed, ((1,), (0,)))
            if state is not None:
                shrink = jnp.exp2((state[0] - new_max) * (scale * LOG2_E))
                total, both, moved = [new + old * shrink for new, old in zip((total, both, moved), state[1:])]
            state = (new_max, total, both, moved)
        _, total, both, moved = state
        inverse = 1.0 / total
        mixed = both[:, :HEAD_DIM] * inverse
        weighted, mass = moved[:, :HEAD_DIM], moved[:, HEAD_DIM:]
        tangent = both[:, HEAD_DIM:] * inverse + (weighted - mass * mixed) * (inverse * scale)
        sources = slice(block * BLOCK // rows, (block + 1) * BLOCK // rows)
        out[sources, :rows, :] = mixed.astype(jnp.bfloat16).reshape(-1, rows, HEAD_DIM)
        out[sources, rows:, :] = tangent.astype(jnp.bfloat16).reshape(-1, rows, HEAD_DIM)


def attention(rows, blocks):
    return pl.pallas_call(
        functools.partial(attention_kernel, rows),
        out_shape=jax.ShapeDtypeStruct((HEADS, 2 * rows, HEAD_DIM), jnp.bfloat16),
        in_specs=[pl.BlockSpec(memory_space=pltpu.VMEM)] * len(blocks),
        out_specs=pl.BlockSpec(memory_space=pltpu.VMEM),
        compiler_params=pltpu.CompilerParams(vmem_limit_bytes=(8 + len(blocks)) * 2**20),
        name="attention",
    )(*blocks)


def unpack_kernel(packed, *refs):
    outs, sems = refs[:2], refs[2]
    row_tiles = outs[0].shape[0]
    copies = []
    for at, out in enumerate(outs):
        for tile in range(row_tiles):
            slot = at * row_tiles + tile
            copies.append(pltpu.make_async_copy(packed.at[:, slot], out.at[tile], sems.at[slot]))
            copies[-1].start()
    for copy in copies:
        copy.wait()


def unpack(packed):
    slots = packed.shape[1] // TILE
    shape = (slots // 2, HEADS, TILE, HEAD_DIM)
    outs = pl.pallas_call(
        unpack_kernel,
        out_shape=[jax.ShapeDtypeStruct(shape, jnp.bfloat16)] * 2,
        in_specs=[pl.BlockSpec(memory_space=pltpu.VMEM)],
        out_specs=[pl.BlockSpec(memory_space=pltpu.HBM)] * 2,
        scratch_shapes=[pltpu.SemaphoreType.DMA((slots,))],
        compiler_params=pltpu.CompilerParams(vmem_limit_bytes=4 * 2**20),
        name="unpack",
    )(packed.reshape(HEADS, slots, TILE, HEAD_DIM))
    return tuple(from_tiles(out) for out in outs)


def solution(mesh):
    teams = plan(mesh)

    def swap(value):
        return lax.all_to_all(value, AXES, 0, 0, axis_index_groups=teams, tiled=True)

    def from_peer(value, by):
        pairs = [pair for at, team in enumerate(teams) for pair in zip(team, teams[(at + by) % len(teams)])]
        return lax.ppermute(value, AXES, pairs)

    def local(query_main, key_main, value_main, query_tan, key_tan, value_tan, positions):
        rows = query_main.shape[0]
        arrays = (query_main, key_main, value_main, query_tan, key_tan, value_tan)
        here = swap(pack(positions, arrays))
        blocks = [here] + [from_peer(here, by) for by in range(1, len(teams))]
        return unpack(swap(attention(rows, blocks)))

    placed = (P(AXES, None),) * 6 + (P(AXES),)
    return jax.shard_map(
        local,
        mesh=mesh,
        in_specs=placed,
        out_specs=(P(AXES, None), P(AXES, None)),
        check_vma=False,
    )
```

```python
import functools
import math

import jax
import jax.numpy as jnp
from jax import lax
from jax.experimental import pallas as pl
from jax.experimental.pallas import tpu as pltpu
from jax.sharding import PartitionSpec as P

HEADS = 16
HEAD_DIM = 128
LOG2_E = math.log2(math.e)
AXES = ("seq", "head")
TILE = 8
MIDDLE = 11
TURN = 4
ARRAYS = 6
PIECES = 4


def plan(mesh, first):
    heads_axis = mesh.shape["head"]
    peers = mesh.shape["seq"] * heads_axis // HEADS
    assert mesh.shape["seq"] % peers == 0

    def flat(peer, head):
        member = head ^ first
        return (member // heads_axis * peers + peer) * heads_axis + member % heads_axis

    return [[flat(peer, head) for head in range(HEADS)] for peer in range(peers)]


def as_tiles(array):
    rows, columns = array.shape
    return array.reshape(rows // TILE, TILE, columns // HEAD_DIM, HEAD_DIM).transpose(0, 2, 1, 3)


def from_tiles(tiles):
    row_tiles, heads = tiles.shape[:2]
    return tiles.transpose(0, 2, 1, 3).reshape(row_tiles * TILE, heads * HEAD_DIM)


def pack_kernel(positions, *refs):
    arrays, (out, here, sems) = refs[:ARRAYS], refs[ARRAYS:]
    row_tiles = arrays[0].shape[0]
    last = ARRAYS * row_tiles
    load = pltpu.make_async_copy(positions, here, sems.at[last])
    load.start()
    copies = []
    for at, array in enumerate(arrays):
        for tile in range(row_tiles):
            slot = at * row_tiles + tile
            copies.append(pltpu.make_async_copy(array.at[tile], out.at[:, slot], sems.at[slot]))
            copies[-1].start()
    token = lax.broadcasted_iota(jnp.int32, (TILE, HEAD_DIM), 0)
    lane = lax.broadcasted_iota(jnp.int32, (TILE, HEAD_DIM), 1)
    token = token + lane // (HEAD_DIM // row_tiles) * TILE
    place = jnp.zeros((TILE, HEAD_DIM), jnp.int32)
    load.wait()
    for t in range(row_tiles * TILE):
        place = jnp.where(token == t, here[t], place)
    place = lax.shift_right_logical(place, lane % PIECES * 8) & 255
    place = place.astype(jnp.float32).astype(jnp.bfloat16)
    for head in range(HEADS):
        out[head, last] = place
    for copy in copies:
        copy.wait()


def pack(positions, arrays):
    tiles = [as_tiles(array) for array in arrays]
    slots = ARRAYS * tiles[0].shape[0] + 1
    packed = pl.pallas_call(
        pack_kernel,
        out_shape=pltpu.VMEM((HEADS, slots, TILE, HEAD_DIM), jnp.bfloat16),
        in_specs=[pl.BlockSpec(memory_space=pltpu.HBM)] * (1 + ARRAYS),
        out_specs=pl.BlockSpec(memory_space=pltpu.VMEM),
        scratch_shapes=[
            pltpu.SMEM(positions.shape, jnp.int32),
            pltpu.SemaphoreType.DMA((slots,)),
        ],
        compiler_params=pltpu.CompilerParams(vmem_limit_bytes=56 * 2**20),
        name="pack",
    )(positions, *tiles)
    return packed.reshape(HEADS, slots * TILE, HEAD_DIM)


def dot(a, b, contract):
    return lax.dot_general(a, b, (contract, ((), ())), preferred_element_type=jnp.float32)


def order_of(pair):
    high, low = pair
    return high.astype(jnp.int32) * 65536 + low.astype(jnp.int32)


def attention_kernel(rows, *refs):
    blocks, out = refs[:-1], refs[-1]
    count = HEADS * rows
    scale = HEAD_DIM ** (-0.5)
    lanes = HEAD_DIM * TILE // rows

    def part(ref, at):
        return ref[:, at * rows : (at + 1) * rows, :].reshape(count, HEAD_DIM)

    def places(ref):
        packed = ref[:, ARRAYS * rows :, :].astype(jnp.float32)
        lane = lax.broadcasted_iota(jnp.int32, packed.shape, 2)
        parts = [jnp.where(lane // lanes == at, packed, 0.0) for at in range(rows // TILE)]
        return jnp.stack(parts, axis=1).reshape(count, HEAD_DIM).astype(jnp.bfloat16)

    def weights(shape, axis, first):
        at = lax.broadcasted_iota(jnp.int32, shape, axis) % lanes
        chosen = jnp.where(at == first, 1.0, jnp.where(at == first + 1, 256.0, 0.0))
        return chosen.astype(jnp.bfloat16)

    own = blocks[0]
    queries = part(own, 0)
    query_pair = jnp.concatenate([part(own, 3), queries], axis=1)
    own_order = places(own)
    across = (HEAD_DIM, HEAD_DIM)
    query_order = order_of([dot(own_order, weights(across, 0, first), ((1,), (0,))) for first in (2, 0)])
    state = None
    for start in range(0, len(blocks), 2):
        group = blocks[start : start + 2]

        def keyed(at):
            return jnp.concatenate([part(ref, at) for ref in group], axis=0)

        keys, values, key_dot, value_dot = [keyed(at) for at in (1, 2, 4, 5)]
        order = jnp.concatenate([places(ref) for ref in group], axis=0)
        width = keys.shape[0]
        down = (8, HEAD_DIM)
        key_order = order_of([dot(weights(down, 1, first), order, ((1,), (1,))) for first in (2, 0)])
        wide_order = jnp.concatenate([query_order] * (width // HEAD_DIM), axis=1)
        visible = key_order[:1] <= wide_order
        scores = dot(queries, keys, ((1,), (1,)))
        scores = jnp.where(visible, scores, -1e30)
        key_pair = jnp.concatenate([keys, key_dot], axis=1)
        score_tan = dot(query_pair, key_pair, ((1,), (1,)))
        new_max = jnp.max(scores, axis=1, keepdims=True)
        if state is not None:
            new_max = jnp.maximum(new_max, state[0])
        expo = jnp.exp2((scores - new_max) * (scale * LOG2_E))
        total = jnp.sum(expo, axis=1, keepdims=True)
        both = dot(expo.astype(jnp.bfloat16), jnp.concatenate([values, value_dot], axis=1), ((1,), (0,)))
        summed = jnp.concatenate([values, jnp.ones_like(values)], axis=1)
        moved = dot((expo * score_tan).astype(jnp.bfloat16), summed, ((1,), (0,)))
        if state is not None:
            shrink = jnp.exp2((state[0] - new_max) * (scale * LOG2_E))
            total, both, moved = [new + old * shrink for new, old in zip((total, both, moved), state[1:])]
        state = (new_max, total, both, moved)
    _, total, both, moved = state
    inverse = 1.0 / total
    mixed = both[:, :HEAD_DIM] * inverse
    weighted, mass = moved[:, :HEAD_DIM], moved[:, HEAD_DIM:]
    tangent = both[:, HEAD_DIM:] * inverse + (weighted - mass * mixed) * (inverse * scale)
    mixed = mixed.astype(jnp.bfloat16).reshape(HEADS, rows, HEAD_DIM)
    tangent = tangent.astype(jnp.bfloat16).reshape(HEADS, rows, HEAD_DIM)
    for source, block in runs():
        out[block : block + TURN, :rows, :] = mixed[source : source + TURN]
        out[block : block + TURN, rows:, :] = tangent[source : source + TURN]


def attention(rows, blocks):
    return pl.pallas_call(
        functools.partial(attention_kernel, rows),
        out_shape=jax.ShapeDtypeStruct((HEADS, 2 * rows, HEAD_DIM), jnp.bfloat16),
        in_specs=[pl.BlockSpec(memory_space=pltpu.VMEM)] * len(blocks),
        out_specs=pl.BlockSpec(memory_space=pltpu.VMEM),
        compiler_params=pltpu.CompilerParams(vmem_limit_bytes=(8 + len(blocks)) * 2**20),
        name="attention",
    )(*blocks)


def runs():
    return [(head, head ^ TURN) for head in range(0, HEADS, TURN)]


def unpack_kernel(packed, *refs):
    outs, sems = refs[:2], refs[2]
    row_tiles = outs[0].shape[0]
    copies = []
    for at, out in enumerate(outs):
        for tile in range(row_tiles):
            slot = at * row_tiles + tile
            for head, block in runs():
                source = packed.at[block : block + TURN, slot]
                target = out.at[tile, head : head + TURN]
                copies.append(pltpu.make_async_copy(source, target, sems.at[len(copies)]))
                copies[-1].start()
    for copy in copies:
        copy.wait()


def unpack(packed):
    slots = packed.shape[1] // TILE
    shape = (slots // 2, HEADS, TILE, HEAD_DIM)
    outs = pl.pallas_call(
        unpack_kernel,
        out_shape=[jax.ShapeDtypeStruct(shape, jnp.bfloat16)] * 2,
        in_specs=[pl.BlockSpec(memory_space=pltpu.VMEM)],
        out_specs=[pl.BlockSpec(memory_space=pltpu.HBM)] * 2,
        scratch_shapes=[pltpu.SemaphoreType.DMA((slots * len(runs()),))],
        compiler_params=pltpu.CompilerParams(vmem_limit_bytes=4 * 2**20),
        name="unpack",
    )(packed.reshape(HEADS, slots, TILE, HEAD_DIM))
    return tuple(from_tiles(out) for out in outs)


def solution(mesh):
    teams = plan(mesh, MIDDLE)

    def swap(value, first):
        return lax.all_to_all(value, AXES, 0, 0, axis_index_groups=plan(mesh, first), tiled=True)

    def from_peer(value, by):
        pairs = [pair for at, team in enumerate(teams) for pair in zip(team, teams[(at + by) % len(teams)])]
        return lax.ppermute(value, AXES, pairs)

    def local(query_main, key_main, value_main, query_tan, key_tan, value_tan, positions):
        rows = query_main.shape[0]
        arrays = (query_main, key_main, value_main, query_tan, key_tan, value_tan)
        here = swap(pack(positions, arrays), MIDDLE)
        blocks = [here] + [from_peer(here, by) for by in range(1, len(teams))]
        return unpack(swap(attention(rows, blocks), MIDDLE ^ TURN))

    placed = (P(AXES, None),) * 6 + (P(AXES),)
    return jax.shard_map(
        local,
        mesh=mesh,
        in_specs=placed,
        out_specs=(P(AXES, None), P(AXES, None)),
        check_vma=False,
    )
```

```python
import functools
import math

import jax
import jax.numpy as jnp
from jax import lax
from jax.experimental import pallas as pl
from jax.experimental.pallas import tpu as pltpu
from jax.sharding import PartitionSpec as P

HEADS = 16
HEAD_DIM = 128
LOG2_E = math.log2(math.e)
AXES = ("seq", "head")
TILE = 8
MIDDLE = 10
ARRAYS = 6
PIECES = 4


def plan(mesh):
    heads_axis = mesh.shape["head"]
    peers = mesh.shape["seq"] * heads_axis // HEADS
    assert mesh.shape["seq"] % peers == 0

    def flat(peer, head):
        member = head ^ MIDDLE
        return (member // heads_axis * peers + peer) * heads_axis + member % heads_axis

    return [[flat(peer, head) for head in range(HEADS)] for peer in range(peers)]


def as_tiles(array):
    rows, columns = array.shape
    return array.reshape(rows // TILE, TILE, columns // HEAD_DIM, HEAD_DIM).transpose(0, 2, 1, 3)


def from_tiles(tiles):
    row_tiles, heads = tiles.shape[:2]
    return tiles.transpose(0, 2, 1, 3).reshape(row_tiles * TILE, heads * HEAD_DIM)


def pack_kernel(positions, *refs):
    arrays, (out, here, sems) = refs[:ARRAYS], refs[ARRAYS:]
    row_tiles = arrays[0].shape[0]
    last = ARRAYS * row_tiles
    load = pltpu.make_async_copy(positions, here, sems.at[last])
    load.start()
    copies = []
    for at, array in enumerate(arrays):
        for tile in range(row_tiles):
            slot = at * row_tiles + tile
            copies.append(pltpu.make_async_copy(array.at[tile], out.at[:, slot], sems.at[slot]))
            copies[-1].start()
    token = lax.broadcasted_iota(jnp.int32, (TILE, HEAD_DIM), 0)
    lane = lax.broadcasted_iota(jnp.int32, (TILE, HEAD_DIM), 1)
    token = token + lane // (HEAD_DIM // row_tiles) * TILE
    place = jnp.zeros((TILE, HEAD_DIM), jnp.int32)
    load.wait()
    for t in range(row_tiles * TILE):
        place = jnp.where(token == t, here[t], place)
    place = lax.shift_right_logical(place, lane % PIECES * 8) & 255
    place = place.astype(jnp.float32).astype(jnp.bfloat16)
    for head in range(HEADS):
        out[head, last] = place
    for copy in copies:
        copy.wait()


def pack(positions, arrays):
    tiles = [as_tiles(array) for array in arrays]
    slots = ARRAYS * tiles[0].shape[0] + 1
    packed = pl.pallas_call(
        pack_kernel,
        out_shape=pltpu.VMEM((HEADS, slots, TILE, HEAD_DIM), jnp.bfloat16),
        in_specs=[pl.BlockSpec(memory_space=pltpu.HBM)] * (1 + ARRAYS),
        out_specs=pl.BlockSpec(memory_space=pltpu.VMEM),
        scratch_shapes=[
            pltpu.SMEM(positions.shape, jnp.int32),
            pltpu.SemaphoreType.DMA((slots,)),
        ],
        compiler_params=pltpu.CompilerParams(vmem_limit_bytes=56 * 2**20),
        name="pack",
    )(positions, *tiles)
    return packed.reshape(HEADS, slots * TILE, HEAD_DIM)


def dot(a, b, contract):
    return lax.dot_general(a, b, (contract, ((), ())), preferred_element_type=jnp.float32)


def order_of(pair):
    high, low = pair
    return high.astype(jnp.int32) * 65536 + low.astype(jnp.int32)


def attention_kernel(rows, *refs):
    blocks, out = refs[:-1], refs[-1]
    count = HEADS * rows
    scale = HEAD_DIM ** (-0.5)
    lanes = HEAD_DIM * TILE // rows

    def part(ref, at):
        return ref[:, at * rows : (at + 1) * rows, :].reshape(count, HEAD_DIM)

    def places(ref):
        packed = ref[:, ARRAYS * rows :, :].astype(jnp.float32)
        lane = lax.broadcasted_iota(jnp.int32, packed.shape, 2)
        parts = [jnp.where(lane // lanes == at, packed, 0.0) for at in range(rows // TILE)]
        return jnp.stack(parts, axis=1).reshape(count, HEAD_DIM).astype(jnp.bfloat16)

    def weights(shape, axis, first):
        at = lax.broadcasted_iota(jnp.int32, shape, axis) % lanes
        chosen = jnp.where(at == first, 1.0, jnp.where(at == first + 1, 256.0, 0.0))
        return chosen.astype(jnp.bfloat16)

    own = blocks[0]
    queries = part(own, 0)
    query_pair = jnp.concatenate([part(own, 3), queries], axis=1)
    own_order = places(own)
    across = (HEAD_DIM, HEAD_DIM)
    query_order = order_of([dot(own_order, weights(across, 0, first), ((1,), (0,))) for first in (2, 0)])
    state = None
    for start in range(0, len(blocks), 2):
        group = blocks[start : start + 2]

        def keyed(at):
            return jnp.concatenate([part(ref, at) for ref in group], axis=0)

        keys, values, key_dot, value_dot = [keyed(at) for at in (1, 2, 4, 5)]
        order = jnp.concatenate([places(ref) for ref in group], axis=0)
        width = keys.shape[0]
        down = (8, HEAD_DIM)
        key_order = order_of([dot(weights(down, 1, first), order, ((1,), (1,))) for first in (2, 0)])
        wide_order = jnp.concatenate([query_order] * (width // HEAD_DIM), axis=1)
        visible = key_order[:1] <= wide_order
        scores = dot(queries, keys, ((1,), (1,)))
        scores = jnp.where(visible, scores, -1e30)
        key_pair = jnp.concatenate([keys, key_dot], axis=1)
        score_tan = dot(query_pair, key_pair, ((1,), (1,)))
        new_max = jnp.max(scores, axis=1, keepdims=True)
        if state is not None:
            new_max = jnp.maximum(new_max, state[0])
        expo = jnp.exp2((scores - new_max) * (scale * LOG2_E))
        total = jnp.sum(expo, axis=1, keepdims=True)
        both = dot(expo.astype(jnp.bfloat16), jnp.concatenate([values, value_dot], axis=1), ((1,), (0,)))
        summed = jnp.concatenate([values, jnp.ones_like(values)], axis=1)
        moved = dot((expo * score_tan).astype(jnp.bfloat16), summed, ((1,), (0,)))
        if state is not None:
            shrink = jnp.exp2((state[0] - new_max) * (scale * LOG2_E))
            total, both, moved = [new + old * shrink for new, old in zip((total, both, moved), state[1:])]
        state = (new_max, total, both, moved)
    _, total, both, moved = state
    inverse = 1.0 / total
    mixed = both[:, :HEAD_DIM] * inverse
    weighted, mass = moved[:, :HEAD_DIM], moved[:, HEAD_DIM:]
    tangent = both[:, HEAD_DIM:] * inverse + (weighted - mass * mixed) * (inverse * scale)
    out[:, :rows, :] = mixed.astype(jnp.bfloat16).reshape(HEADS, rows, HEAD_DIM)
    out[:, rows:, :] = tangent.astype(jnp.bfloat16).reshape(HEADS, rows, HEAD_DIM)


def attention(rows, blocks):
    return pl.pallas_call(
        functools.partial(attention_kernel, rows),
        out_shape=jax.ShapeDtypeStruct((HEADS, 2 * rows, HEAD_DIM), jnp.bfloat16),
        in_specs=[pl.BlockSpec(memory_space=pltpu.VMEM)] * len(blocks),
        out_specs=pl.BlockSpec(memory_space=pltpu.VMEM),
        compiler_params=pltpu.CompilerParams(vmem_limit_bytes=(8 + len(blocks)) * 2**20),
        name="attention",
    )(*blocks)


def unpack_kernel(packed, *refs):
    outs, sems = refs[:2], refs[2]
    row_tiles = outs[0].shape[0]
    copies = []
    for at, out in enumerate(outs):
        for tile in range(row_tiles):
            slot = at * row_tiles + tile
            copies.append(pltpu.make_async_copy(packed.at[:, slot], out.at[tile], sems.at[slot]))
            copies[-1].start()
    for copy in copies:
        copy.wait()


def unpack(packed):
    slots = packed.shape[1] // TILE
    shape = (slots // 2, HEADS, TILE, HEAD_DIM)
    outs = pl.pallas_call(
        unpack_kernel,
        out_shape=[jax.ShapeDtypeStruct(shape, jnp.bfloat16)] * 2,
        in_specs=[pl.BlockSpec(memory_space=pltpu.VMEM)],
        out_specs=[pl.BlockSpec(memory_space=pltpu.HBM)] * 2,
        scratch_shapes=[pltpu.SemaphoreType.DMA((slots,))],
        compiler_params=pltpu.CompilerParams(vmem_limit_bytes=4 * 2**20),
        name="unpack",
    )(packed.reshape(HEADS, slots, TILE, HEAD_DIM))
    return tuple(from_tiles(out) for out in outs)


def solution(mesh):
    teams = plan(mesh)

    def swap(value):
        return lax.all_to_all(value, AXES, 0, 0, axis_index_groups=teams, tiled=True)

    def from_peer(value, by):
        pairs = [pair for at, team in enumerate(teams) for pair in zip(team, teams[(at + by) % len(teams)])]
        return lax.ppermute(value, AXES, pairs)

    def local(query_main, key_main, value_main, query_tan, key_tan, value_tan, positions):
        rows = query_main.shape[0]
        arrays = (query_main, key_main, value_main, query_tan, key_tan, value_tan)
        here = swap(pack(positions, arrays))
        blocks = [here] + [from_peer(here, by) for by in range(1, len(teams))]
        return unpack(swap(attention(rows, blocks)))

    placed = (P(AXES, None),) * 6 + (P(AXES),)
    return jax.shard_map(
        local,
        mesh=mesh,
        in_specs=placed,
        out_specs=(P(AXES, None), P(AXES, None)),
        check_vma=False,
    )
```

```python
import functools
import math

import jax
import jax.numpy as jnp
from jax import lax
from jax.experimental import pallas as pl
from jax.experimental.pallas import tpu as pltpu
from jax.sharding import PartitionSpec as P

HEADS = 16
HEAD_DIM = 128
LOG2_E = math.log2(math.e)
AXES = ("seq", "head")
TILE = 8
MIDDLE = 11
ARRAYS = 6
PIECES = 4


def plan(mesh):
    heads_axis = mesh.shape["head"]
    peers = mesh.shape["seq"] * heads_axis // HEADS
    assert mesh.shape["seq"] % peers == 0

    def flat(peer, head):
        member = head ^ MIDDLE
        peer = (peer + 1) % peers if head == 0 else peer
        return (member // heads_axis * peers + peer) * heads_axis + member % heads_axis

    return [[flat(peer, head) for head in range(HEADS)] for peer in range(peers)]


def as_tiles(array):
    rows, columns = array.shape
    return array.reshape(rows // TILE, TILE, columns // HEAD_DIM, HEAD_DIM).transpose(0, 2, 1, 3)


def from_tiles(tiles):
    row_tiles, heads = tiles.shape[:2]
    return tiles.transpose(0, 2, 1, 3).reshape(row_tiles * TILE, heads * HEAD_DIM)


def pack_kernel(positions, *refs):
    arrays, (out, here, sems) = refs[:ARRAYS], refs[ARRAYS:]
    row_tiles = arrays[0].shape[0]
    last = ARRAYS * row_tiles
    load = pltpu.make_async_copy(positions, here, sems.at[last])
    load.start()
    copies = []
    for at, array in enumerate(arrays):
        for tile in range(row_tiles):
            slot = at * row_tiles + tile
            copies.append(pltpu.make_async_copy(array.at[tile], out.at[:, slot], sems.at[slot]))
            copies[-1].start()
    token = lax.broadcasted_iota(jnp.int32, (TILE, HEAD_DIM), 0)
    lane = lax.broadcasted_iota(jnp.int32, (TILE, HEAD_DIM), 1)
    token = token + lane // (HEAD_DIM // row_tiles) * TILE
    place = jnp.zeros((TILE, HEAD_DIM), jnp.int32)
    load.wait()
    for t in range(row_tiles * TILE):
        place = jnp.where(token == t, here[t], place)
    place = lax.shift_right_logical(place, lane % PIECES * 8) & 255
    place = place.astype(jnp.float32).astype(jnp.bfloat16)
    for head in range(HEADS):
        out[head, last] = place
    for copy in copies:
        copy.wait()


def pack(positions, arrays):
    tiles = [as_tiles(array) for array in arrays]
    slots = ARRAYS * tiles[0].shape[0] + 1
    packed = pl.pallas_call(
        pack_kernel,
        out_shape=pltpu.VMEM((HEADS, slots, TILE, HEAD_DIM), jnp.bfloat16),
        in_specs=[pl.BlockSpec(memory_space=pltpu.HBM)] * (1 + ARRAYS),
        out_specs=pl.BlockSpec(memory_space=pltpu.VMEM),
        scratch_shapes=[
            pltpu.SMEM(positions.shape, jnp.int32),
            pltpu.SemaphoreType.DMA((slots,)),
        ],
        compiler_params=pltpu.CompilerParams(vmem_limit_bytes=56 * 2**20),
        name="pack",
    )(positions, *tiles)
    return packed.reshape(HEADS, slots * TILE, HEAD_DIM)


def dot(a, b, contract):
    return lax.dot_general(a, b, (contract, ((), ())), preferred_element_type=jnp.float32)


def order_of(pair):
    high, low = pair
    return high.astype(jnp.int32) * 65536 + low.astype(jnp.int32)


def attention_kernel(rows, *refs):
    blocks, out = refs[:-1], refs[-1]
    count = HEADS * rows
    scale = HEAD_DIM ** (-0.5)
    lanes = HEAD_DIM * TILE // rows

    def part(ref, at):
        return ref[:, at * rows : (at + 1) * rows, :].reshape(count, HEAD_DIM)

    def places(ref):
        packed = ref[:, ARRAYS * rows :, :].astype(jnp.float32)
        lane = lax.broadcasted_iota(jnp.int32, packed.shape, 2)
        parts = [jnp.where(lane // lanes == at, packed, 0.0) for at in range(rows // TILE)]
        return jnp.stack(parts, axis=1).reshape(count, HEAD_DIM).astype(jnp.bfloat16)

    def weights(shape, axis, first):
        at = lax.broadcasted_iota(jnp.int32, shape, axis) % lanes
        chosen = jnp.where(at == first, 1.0, jnp.where(at == first + 1, 256.0, 0.0))
        return chosen.astype(jnp.bfloat16)

    own = blocks[0]
    queries = part(own, 0)
    query_pair = jnp.concatenate([part(own, 3), queries], axis=1)
    own_order = places(own)
    across = (HEAD_DIM, HEAD_DIM)
    query_order = order_of([dot(own_order, weights(across, 0, first), ((1,), (0,))) for first in (2, 0)])
    state = None
    for start in range(0, len(blocks), 2):
        group = blocks[start : start + 2]

        def keyed(at):
            return jnp.concatenate([part(ref, at) for ref in group], axis=0)

        keys, values, key_dot, value_dot = [keyed(at) for at in (1, 2, 4, 5)]
        order = jnp.concatenate([places(ref) for ref in group], axis=0)
        width = keys.shape[0]
        down = (8, HEAD_DIM)
        key_order = order_of([dot(weights(down, 1, first), order, ((1,), (1,))) for first in (2, 0)])
        wide_order = jnp.concatenate([query_order] * (width // HEAD_DIM), axis=1)
        visible = key_order[:1] <= wide_order
        scores = dot(queries, keys, ((1,), (1,)))
        scores = jnp.where(visible, scores, -1e30)
        key_pair = jnp.concatenate([keys, key_dot], axis=1)
        score_tan = dot(query_pair, key_pair, ((1,), (1,)))
        new_max = jnp.max(scores, axis=1, keepdims=True)
        if state is not None:
            new_max = jnp.maximum(new_max, state[0])
        expo = jnp.exp2((scores - new_max) * (scale * LOG2_E))
        total = jnp.sum(expo, axis=1, keepdims=True)
        both = dot(expo.astype(jnp.bfloat16), jnp.concatenate([values, value_dot], axis=1), ((1,), (0,)))
        summed = jnp.concatenate([values, jnp.ones_like(values)], axis=1)
        moved = dot((expo * score_tan).astype(jnp.bfloat16), summed, ((1,), (0,)))
        if state is not None:
            shrink = jnp.exp2((state[0] - new_max) * (scale * LOG2_E))
            total, both, moved = [new + old * shrink for new, old in zip((total, both, moved), state[1:])]
        state = (new_max, total, both, moved)
    _, total, both, moved = state
    inverse = 1.0 / total
    mixed = both[:, :HEAD_DIM] * inverse
    weighted, mass = moved[:, :HEAD_DIM], moved[:, HEAD_DIM:]
    tangent = both[:, HEAD_DIM:] * inverse + (weighted - mass * mixed) * (inverse * scale)
    out[:, :rows, :] = mixed.astype(jnp.bfloat16).reshape(HEADS, rows, HEAD_DIM)
    out[:, rows:, :] = tangent.astype(jnp.bfloat16).reshape(HEADS, rows, HEAD_DIM)


def attention(rows, blocks):
    return pl.pallas_call(
        functools.partial(attention_kernel, rows),
        out_shape=jax.ShapeDtypeStruct((HEADS, 2 * rows, HEAD_DIM), jnp.bfloat16),
        in_specs=[pl.BlockSpec(memory_space=pltpu.VMEM)] * len(blocks),
        out_specs=pl.BlockSpec(memory_space=pltpu.VMEM),
        compiler_params=pltpu.CompilerParams(vmem_limit_bytes=(8 + len(blocks)) * 2**20),
        name="attention",
    )(*blocks)


def unpack_kernel(packed, *refs):
    outs, sems = refs[:2], refs[2]
    row_tiles = outs[0].shape[0]
    copies = []
    for at, out in enumerate(outs):
        for tile in range(row_tiles):
            slot = at * row_tiles + tile
            copies.append(pltpu.make_async_copy(packed.at[:, slot], out.at[tile], sems.at[slot]))
            copies[-1].start()
    for copy in copies:
        copy.wait()


def unpack(packed):
    slots = packed.shape[1] // TILE
    shape = (slots // 2, HEADS, TILE, HEAD_DIM)
    outs = pl.pallas_call(
        unpack_kernel,
        out_shape=[jax.ShapeDtypeStruct(shape, jnp.bfloat16)] * 2,
        in_specs=[pl.BlockSpec(memory_space=pltpu.VMEM)],
        out_specs=[pl.BlockSpec(memory_space=pltpu.HBM)] * 2,
        scratch_shapes=[pltpu.SemaphoreType.DMA((slots,))],
        compiler_params=pltpu.CompilerParams(vmem_limit_bytes=4 * 2**20),
        name="unpack",
    )(packed.reshape(HEADS, slots, TILE, HEAD_DIM))
    return tuple(from_tiles(out) for out in outs)


def solution(mesh):
    teams = plan(mesh)

    def swap(value):
        return lax.all_to_all(value, AXES, 0, 0, axis_index_groups=teams, tiled=True)

    def from_peer(value, by):
        pairs = [pair for at, team in enumerate(teams) for pair in zip(team, teams[(at + by) % len(teams)])]
        return lax.ppermute(value, AXES, pairs)

    def local(query_main, key_main, value_main, query_tan, key_tan, value_tan, positions):
        rows = query_main.shape[0]
        arrays = (query_main, key_main, value_main, query_tan, key_tan, value_tan)
        here = swap(pack(positions, arrays))
        blocks = [here] + [from_peer(here, by) for by in range(1, len(teams))]
        return unpack(swap(attention(rows, blocks)))

    placed = (P(AXES, None),) * 6 + (P(AXES),)
    return jax.shard_map(
        local,
        mesh=mesh,
        in_specs=placed,
        out_specs=(P(AXES, None), P(AXES, None)),
        check_vma=False,
    )
```

```python
import functools
import math

import jax
import jax.numpy as jnp
from jax import lax
from jax.experimental import pallas as pl
from jax.experimental.pallas import tpu as pltpu
from jax.sharding import PartitionSpec as P

HEADS = 16
HEAD_DIM = 128
LOG2_E = math.log2(math.e)
AXES = ("seq", "head")
TILE = 8
MIDDLE = 11
ARRAYS = 6
PIECES = 4


def plan(mesh):
    heads_axis = mesh.shape["head"]
    peers = mesh.shape["seq"] * heads_axis // HEADS
    assert mesh.shape["seq"] % peers == 0

    def flat(peer, head):
        member = head ^ MIDDLE
        return (member // heads_axis * peers + peer) * heads_axis + member % heads_axis

    return [[flat(peer, head) for head in range(HEADS)] for peer in range(peers)]


def as_tiles(array):
    rows, columns = array.shape
    return array.reshape(rows // TILE, TILE, columns // HEAD_DIM, HEAD_DIM).transpose(0, 2, 1, 3)


def from_tiles(tiles):
    row_tiles, heads = tiles.shape[:2]
    return tiles.transpose(0, 2, 1, 3).reshape(row_tiles * TILE, heads * HEAD_DIM)


def pack_kernel(positions, *refs):
    arrays, (out, here, held, sems) = refs[:ARRAYS], refs[ARRAYS:]
    row_tiles = arrays[0].shape[0]
    last = ARRAYS * row_tiles
    load = pltpu.make_async_copy(positions, here, sems.at[last])
    load.start()
    copies = []
    for at, array in enumerate(arrays):
        copies.append(pltpu.make_async_copy(array, held.at[at], sems.at[at]))
        copies[-1].start()
    token = lax.broadcasted_iota(jnp.int32, (TILE, HEAD_DIM), 0)
    lane = lax.broadcasted_iota(jnp.int32, (TILE, HEAD_DIM), 1)
    token = token + lane // (HEAD_DIM // row_tiles) * TILE
    place = jnp.zeros((TILE, HEAD_DIM), jnp.int32)
    load.wait()
    for t in range(row_tiles * TILE):
        place = jnp.where(token == t, here[t], place)
    place = lax.shift_right_logical(place, lane % PIECES * 8) & 255
    place = place.astype(jnp.float32).astype(jnp.bfloat16)
    for head in range(HEADS):
        out[head, last] = place
    for at, copy in enumerate(copies):
        copy.wait()
        for tile in range(row_tiles):
            out[:, at * row_tiles + tile] = held[at, tile]


def pack(positions, arrays):
    tiles = [as_tiles(array) for array in arrays]
    slots = ARRAYS * tiles[0].shape[0] + 1
    packed = pl.pallas_call(
        pack_kernel,
        out_shape=pltpu.VMEM((HEADS, slots, TILE, HEAD_DIM), jnp.bfloat16),
        in_specs=[pl.BlockSpec(memory_space=pltpu.HBM)] * (1 + ARRAYS),
        out_specs=pl.BlockSpec(memory_space=pltpu.VMEM),
        scratch_shapes=[
            pltpu.SMEM(positions.shape, jnp.int32),
            pltpu.VMEM((ARRAYS, *tiles[0].shape), jnp.bfloat16),
            pltpu.SemaphoreType.DMA((slots,)),
        ],
        compiler_params=pltpu.CompilerParams(vmem_limit_bytes=56 * 2**20),
        name="pack",
    )(positions, *tiles)
    return packed.reshape(HEADS, slots * TILE, HEAD_DIM)


def dot(a, b, contract):
    return lax.dot_general(a, b, (contract, ((), ())), preferred_element_type=jnp.float32)


def order_of(pair):
    high, low = pair
    return high.astype(jnp.int32) * 65536 + low.astype(jnp.int32)


def attention_kernel(rows, *refs):
    blocks, out = refs[:-1], refs[-1]
    count = HEADS * rows
    scale = HEAD_DIM ** (-0.5)
    lanes = HEAD_DIM * TILE // rows

    def part(ref, at):
        return ref[:, at * rows : (at + 1) * rows, :].reshape(count, HEAD_DIM)

    def places(ref):
        packed = ref[:, ARRAYS * rows :, :].astype(jnp.float32)
        lane = lax.broadcasted_iota(jnp.int32, packed.shape, 2)
        parts = [jnp.where(lane // lanes == at, packed, 0.0) for at in range(rows // TILE)]
        return jnp.stack(parts, axis=1).reshape(count, HEAD_DIM).astype(jnp.bfloat16)

    def weights(shape, axis, first):
        at = lax.broadcasted_iota(jnp.int32, shape, axis) % lanes
        chosen = jnp.where(at == first, 1.0, jnp.where(at == first + 1, 256.0, 0.0))
        return chosen.astype(jnp.bfloat16)

    own = blocks[0]
    queries = part(own, 0)
    query_pair = jnp.concatenate([part(own, 3), queries], axis=1)
    own_order = places(own)
    across = (HEAD_DIM, HEAD_DIM)
    query_order = order_of([dot(own_order, weights(across, 0, first), ((1,), (0,))) for first in (2, 0)])
    state = None
    for start in range(0, len(blocks), 2):
        group = blocks[start : start + 2]

        def keyed(at):
            return jnp.concatenate([part(ref, at) for ref in group], axis=0)

        keys, values, key_dot, value_dot = [keyed(at) for at in (1, 2, 4, 5)]
        order = jnp.concatenate([places(ref) for ref in group], axis=0)
        width = keys.shape[0]
        down = (8, HEAD_DIM)
        key_order = order_of([dot(weights(down, 1, first), order, ((1,), (1,))) for first in (2, 0)])
        wide_order = jnp.concatenate([query_order] * (width // HEAD_DIM), axis=1)
        visible = key_order[:1] <= wide_order
        scores = dot(queries, keys, ((1,), (1,)))
        scores = jnp.where(visible, scores, -1e30)
        key_pair = jnp.concatenate([keys, key_dot], axis=1)
        score_tan = dot(query_pair, key_pair, ((1,), (1,)))
        new_max = jnp.max(scores, axis=1, keepdims=True)
        if state is not None:
            new_max = jnp.maximum(new_max, state[0])
        expo = jnp.exp2((scores - new_max) * (scale * LOG2_E))
        total = jnp.sum(expo, axis=1, keepdims=True)
        both = dot(expo.astype(jnp.bfloat16), jnp.concatenate([values, value_dot], axis=1), ((1,), (0,)))
        summed = jnp.concatenate([values, jnp.ones_like(values)], axis=1)
        moved = dot((expo * score_tan).astype(jnp.bfloat16), summed, ((1,), (0,)))
        if state is not None:
            shrink = jnp.exp2((state[0] - new_max) * (scale * LOG2_E))
            total, both, moved = [new + old * shrink for new, old in zip((total, both, moved), state[1:])]
        state = (new_max, total, both, moved)
    _, total, both, moved = state
    inverse = 1.0 / total
    mixed = both[:, :HEAD_DIM] * inverse
    weighted, mass = moved[:, :HEAD_DIM], moved[:, HEAD_DIM:]
    tangent = both[:, HEAD_DIM:] * inverse + (weighted - mass * mixed) * (inverse * scale)
    out[:, :rows, :] = mixed.astype(jnp.bfloat16).reshape(HEADS, rows, HEAD_DIM)
    out[:, rows:, :] = tangent.astype(jnp.bfloat16).reshape(HEADS, rows, HEAD_DIM)


def attention(rows, blocks):
    return pl.pallas_call(
        functools.partial(attention_kernel, rows),
        out_shape=jax.ShapeDtypeStruct((HEADS, 2 * rows, HEAD_DIM), jnp.bfloat16),
        in_specs=[pl.BlockSpec(memory_space=pltpu.VMEM)] * len(blocks),
        out_specs=pl.BlockSpec(memory_space=pltpu.VMEM),
        compiler_params=pltpu.CompilerParams(vmem_limit_bytes=(8 + len(blocks)) * 2**20),
        name="attention",
    )(*blocks)


def unpack_kernel(packed, *refs):
    outs, (held, sems) = refs[:2], refs[2:]
    row_tiles = outs[0].shape[0]
    copies = []
    for at, out in enumerate(outs):
        for tile in range(row_tiles):
            held[at, tile] = packed[:, at * row_tiles + tile]
        copies.append(pltpu.make_async_copy(held.at[at], out, sems.at[at]))
        copies[-1].start()
    for copy in copies:
        copy.wait()


def unpack(packed):
    slots = packed.shape[1] // TILE
    shape = (slots // 2, HEADS, TILE, HEAD_DIM)
    outs = pl.pallas_call(
        unpack_kernel,
        out_shape=[jax.ShapeDtypeStruct(shape, jnp.bfloat16)] * 2,
        in_specs=[pl.BlockSpec(memory_space=pltpu.VMEM)],
        out_specs=[pl.BlockSpec(memory_space=pltpu.HBM)] * 2,
        scratch_shapes=[pltpu.VMEM((2, *shape), jnp.bfloat16), pltpu.SemaphoreType.DMA((2,))],
        compiler_params=pltpu.CompilerParams(vmem_limit_bytes=4 * 2**20),
        name="unpack",
    )(packed.reshape(HEADS, slots, TILE, HEAD_DIM))
    return tuple(from_tiles(out) for out in outs)


def solution(mesh):
    teams = plan(mesh)

    def swap(value):
        return lax.all_to_all(value, AXES, 0, 0, axis_index_groups=teams, tiled=True)

    def from_peer(value, by):
        pairs = [pair for at, team in enumerate(teams) for pair in zip(team, teams[(at + by) % len(teams)])]
        return lax.ppermute(value, AXES, pairs)

    def local(query_main, key_main, value_main, query_tan, key_tan, value_tan, positions):
        rows = query_main.shape[0]
        arrays = (query_main, key_main, value_main, query_tan, key_tan, value_tan)
        here = swap(pack(positions, arrays))
        blocks = [here] + [from_peer(here, by) for by in range(1, len(teams))]
        return unpack(swap(attention(rows, blocks)))

    placed = (P(AXES, None),) * 6 + (P(AXES),)
    return jax.shard_map(
        local,
        mesh=mesh,
        in_specs=placed,
        out_specs=(P(AXES, None), P(AXES, None)),
        check_vma=False,
    )
```

```python
import functools
import math

import jax
import jax.numpy as jnp
from jax import lax
from jax.experimental import pallas as pl
from jax.experimental.pallas import tpu as pltpu
from jax.sharding import PartitionSpec as P

HEADS = 16
HEAD_DIM = 128
LOG2_E = math.log2(math.e)
AXES = ("seq", "head")
TILE = 8
MIDDLE = 11
ARRAYS = 6
PIECES = 4


def plan(mesh):
    heads_axis = mesh.shape["head"]
    peers = mesh.shape["seq"] * heads_axis // HEADS
    assert mesh.shape["seq"] % peers == 0

    def flat(peer, head):
        member = head ^ MIDDLE
        return (member // heads_axis * peers + peer) * heads_axis + member % heads_axis

    return [[flat(peer, head) for head in range(HEADS)] for peer in range(peers)]


def as_tiles(array):
    rows, columns = array.shape
    return array.reshape(rows // TILE, TILE, columns // HEAD_DIM, HEAD_DIM).transpose(0, 2, 1, 3)


def from_tiles(tiles):
    row_tiles, heads = tiles.shape[:2]
    return tiles.transpose(0, 2, 1, 3).reshape(row_tiles * TILE, heads * HEAD_DIM)


def pack_kernel(positions, *refs):
    arrays, (out, here, sems) = refs[:ARRAYS], refs[ARRAYS:]
    row_tiles = arrays[0].shape[0]
    last = ARRAYS * row_tiles
    load = pltpu.make_async_copy(positions, here, sems.at[last])
    load.start()
    copies = []
    for at, array in enumerate(arrays):
        for tile in range(row_tiles):
            slot = at * row_tiles + tile
            copies.append(pltpu.make_async_copy(array.at[tile], out.at[:, slot], sems.at[slot]))
            copies[-1].start()
    token = lax.broadcasted_iota(jnp.int32, (TILE, HEAD_DIM), 0)
    lane = lax.broadcasted_iota(jnp.int32, (TILE, HEAD_DIM), 1)
    token = token + lane // (HEAD_DIM // row_tiles) * TILE
    place = jnp.zeros((TILE, HEAD_DIM), jnp.int32)
    load.wait()
    for t in range(row_tiles * TILE):
        place = jnp.where(token == t, here[t], place)
    place = lax.shift_right_logical(place, lane % PIECES * 8) & 255
    place = place.astype(jnp.float32).astype(jnp.bfloat16)
    for head in range(HEADS):
        out[head, last] = place
    for copy in copies:
        copy.wait()


def pack(positions, arrays):
    tiles = [as_tiles(array) for array in arrays]
    slots = ARRAYS * tiles[0].shape[0] + 1
    packed = pl.pallas_call(
        pack_kernel,
        out_shape=pltpu.VMEM((HEADS, slots, TILE, HEAD_DIM), jnp.bfloat16),
        in_specs=[pl.BlockSpec(memory_space=pltpu.HBM)] * (1 + ARRAYS),
        out_specs=pl.BlockSpec(memory_space=pltpu.VMEM),
        scratch_shapes=[
            pltpu.SMEM(positions.shape, jnp.int32),
            pltpu.SemaphoreType.DMA((slots,)),
        ],
        compiler_params=pltpu.CompilerParams(vmem_limit_bytes=56 * 2**20),
        name="pack",
    )(positions, *tiles)
    return packed.reshape(HEADS, slots * TILE, HEAD_DIM)


def dot(a, b, contract):
    return lax.dot_general(a, b, (contract, ((), ())), preferred_element_type=jnp.float32)


def order_of(pair):
    high, low = pair
    return high.astype(jnp.int32) * 65536 + low.astype(jnp.int32)


def attention_kernel(rows, peers, *refs):
    blocks, out = refs[:-1], refs[-1]
    if peers == 2:
        blocks = [blocks[0], blocks[1:]]
        early = lax.axis_index("seq") % 2 == 0
    count = HEADS * rows
    scale = HEAD_DIM ** (-0.5)
    lanes = HEAD_DIM * TILE // rows

    def read(ref, rows_read):
        if isinstance(ref, tuple):
            return jnp.where(early, ref[0][:, rows_read, :], ref[1][:, rows_read, :])
        return ref[:, rows_read, :]

    def part(ref, at):
        return read(ref, slice(at * rows, (at + 1) * rows)).reshape(count, HEAD_DIM)

    def places(ref):
        packed = read(ref, slice(ARRAYS * rows, None)).astype(jnp.float32)
        lane = lax.broadcasted_iota(jnp.int32, packed.shape, 2)
        parts = [jnp.where(lane // lanes == at, packed, 0.0) for at in range(rows // TILE)]
        return jnp.stack(parts, axis=1).reshape(count, HEAD_DIM).astype(jnp.bfloat16)

    def weights(shape, axis, first):
        at = lax.broadcasted_iota(jnp.int32, shape, axis) % lanes
        chosen = jnp.where(at == first, 1.0, jnp.where(at == first + 1, 256.0, 0.0))
        return chosen.astype(jnp.bfloat16)

    own = blocks[0]
    queries = part(own, 0)
    query_pair = jnp.concatenate([part(own, 3), queries], axis=1)
    own_order = places(own)
    across = (HEAD_DIM, HEAD_DIM)
    query_order = order_of([dot(own_order, weights(across, 0, first), ((1,), (0,))) for first in (2, 0)])
    state = None
    for start in range(0, len(blocks), 2):
        group = blocks[start : start + 2]

        def keyed(at):
            return jnp.concatenate([part(ref, at) for ref in group], axis=0)

        keys, values, key_dot, value_dot = [keyed(at) for at in (1, 2, 4, 5)]
        order = jnp.concatenate([places(ref) for ref in group], axis=0)
        width = keys.shape[0]
        down = (8, HEAD_DIM)
        key_order = order_of([dot(weights(down, 1, first), order, ((1,), (1,))) for first in (2, 0)])
        wide_order = jnp.concatenate([query_order] * (width // HEAD_DIM), axis=1)
        visible = key_order[:1] <= wide_order
        scores = dot(queries, keys, ((1,), (1,)))
        scores = jnp.where(visible, scores, -1e30)
        key_pair = jnp.concatenate([keys, key_dot], axis=1)
        score_tan = dot(query_pair, key_pair, ((1,), (1,)))
        new_max = jnp.max(scores, axis=1, keepdims=True)
        if state is not None:
            new_max = jnp.maximum(new_max, state[0])
        expo = jnp.exp2((scores - new_max) * (scale * LOG2_E))
        total = jnp.sum(expo, axis=1, keepdims=True)
        both = dot(expo.astype(jnp.bfloat16), jnp.concatenate([values, value_dot], axis=1), ((1,), (0,)))
        summed = jnp.concatenate([values, jnp.ones_like(values)], axis=1)
        moved = dot((expo * score_tan).astype(jnp.bfloat16), summed, ((1,), (0,)))
        if state is not None:
            shrink = jnp.exp2((state[0] - new_max) * (scale * LOG2_E))
            total, both, moved = [new + old * shrink for new, old in zip((total, both, moved), state[1:])]
        state = (new_max, total, both, moved)
    _, total, both, moved = state
    inverse = 1.0 / total
    mixed = both[:, :HEAD_DIM] * inverse
    weighted, mass = moved[:, :HEAD_DIM], moved[:, HEAD_DIM:]
    tangent = both[:, HEAD_DIM:] * inverse + (weighted - mass * mixed) * (inverse * scale)
    out[:, :rows, :] = mixed.astype(jnp.bfloat16).reshape(HEADS, rows, HEAD_DIM)
    out[:, rows:, :] = tangent.astype(jnp.bfloat16).reshape(HEADS, rows, HEAD_DIM)


def attention(rows, blocks, peers):
    return pl.pallas_call(
        functools.partial(attention_kernel, rows, peers),
        out_shape=jax.ShapeDtypeStruct((HEADS, 2 * rows, HEAD_DIM), jnp.bfloat16),
        in_specs=[pl.BlockSpec(memory_space=pltpu.VMEM)] * len(blocks),
        out_specs=pl.BlockSpec(memory_space=pltpu.VMEM),
        compiler_params=pltpu.CompilerParams(vmem_limit_bytes=(8 + len(blocks)) * 2**20),
        name="attention",
    )(*blocks)


def unpack_kernel(packed, *refs):
    outs, sems = refs[:2], refs[2]
    row_tiles = outs[0].shape[0]
    copies = []
    for at, out in enumerate(outs):
        for tile in range(row_tiles):
            slot = at * row_tiles + tile
            copies.append(pltpu.make_async_copy(packed.at[:, slot], out.at[tile], sems.at[slot]))
            copies[-1].start()
    for copy in copies:
        copy.wait()


def unpack(packed):
    slots = packed.shape[1] // TILE
    shape = (slots // 2, HEADS, TILE, HEAD_DIM)
    outs = pl.pallas_call(
        unpack_kernel,
        out_shape=[jax.ShapeDtypeStruct(shape, jnp.bfloat16)] * 2,
        in_specs=[pl.BlockSpec(memory_space=pltpu.VMEM)],
        out_specs=[pl.BlockSpec(memory_space=pltpu.HBM)] * 2,
        scratch_shapes=[pltpu.SemaphoreType.DMA((slots,))],
        compiler_params=pltpu.CompilerParams(vmem_limit_bytes=4 * 2**20),
        name="unpack",
    )(packed.reshape(HEADS, slots, TILE, HEAD_DIM))
    return tuple(from_tiles(out) for out in outs)


def solution(mesh):
    teams = plan(mesh)

    def swap(value):
        return lax.all_to_all(value, AXES, 0, 0, axis_index_groups=teams, tiled=True)

    def from_peer(value, by, takers=range(len(teams))):
        pairs = [pair for at in takers for pair in zip(teams[(at + by) % len(teams)], teams[at])]
        return lax.ppermute(value, AXES, pairs)

    def gather(packed):
        if len(teams) != 2:
            here = swap(packed)
            return [here] + [from_peer(here, by) for by in range(1, len(teams))]
        team = lax.axis_index("seq") % 2
        here = lax.cond(team == 1, swap, lambda value: value, packed)
        early = from_peer(here, 1, takers=[0])
        here = lax.cond(team == 0, lambda value, _: swap(value), lambda _, value: value, packed, here)
        return [here, early, from_peer(here, 1, takers=[1])]

    def local(query_main, key_main, value_main, query_tan, key_tan, value_tan, positions):
        rows = query_main.shape[0]
        arrays = (query_main, key_main, value_main, query_tan, key_tan, value_tan)
        return unpack(swap(attention(rows, gather(pack(positions, arrays)), len(teams))))

    placed = (P(AXES, None),) * 6 + (P(AXES),)
    return jax.shard_map(
        local,
        mesh=mesh,
        in_specs=placed,
        out_specs=(P(AXES, None), P(AXES, None)),
        check_vma=False,
    )
```

```python
import functools
import math

import jax
import jax.numpy as jnp
from jax import lax
from jax.experimental import pallas as pl
from jax.experimental.pallas import tpu as pltpu
from jax.sharding import PartitionSpec as P

HEADS = 16
HEAD_DIM = 128
LOG2_E = math.log2(math.e)
AXES = ("seq", "head")
TILE = 8
MIDDLE = 11
ARRAYS = 6
PIECES = 4


def plan(mesh):
    heads_axis = mesh.shape["head"]
    peers = mesh.shape["seq"] * heads_axis // HEADS
    assert mesh.shape["seq"] % peers == 0

    def distance(member):
        return sum(abs((member >> at) % span - (MIDDLE >> at) % span) for at, span in ((0, 2), (1, 2), (2, 4)))

    order = sorted(range(HEADS), key=lambda member: (member != MIDDLE, -distance(member)))

    def flat(peer, head):
        member = order[head]
        return (member // heads_axis * peers + peer) * heads_axis + member % heads_axis

    return [[flat(peer, head) for head in range(HEADS)] for peer in range(peers)]


def as_tiles(array):
    rows, columns = array.shape
    return array.reshape(rows // TILE, TILE, columns // HEAD_DIM, HEAD_DIM).transpose(0, 2, 1, 3)


def from_tiles(tiles):
    row_tiles, heads = tiles.shape[:2]
    return tiles.transpose(0, 2, 1, 3).reshape(row_tiles * TILE, heads * HEAD_DIM)


def pack_kernel(positions, *refs):
    arrays, (out, here, sems) = refs[:ARRAYS], refs[ARRAYS:]
    row_tiles = arrays[0].shape[0]
    last = ARRAYS * row_tiles
    load = pltpu.make_async_copy(positions, here, sems.at[last])
    load.start()
    copies = []
    for at, array in enumerate(arrays):
        for tile in range(row_tiles):
            slot = at * row_tiles + tile
            copies.append(pltpu.make_async_copy(array.at[tile], out.at[:, slot], sems.at[slot]))
            copies[-1].start()
    token = lax.broadcasted_iota(jnp.int32, (TILE, HEAD_DIM), 0)
    lane = lax.broadcasted_iota(jnp.int32, (TILE, HEAD_DIM), 1)
    token = token + lane // (HEAD_DIM // row_tiles) * TILE
    place = jnp.zeros((TILE, HEAD_DIM), jnp.int32)
    load.wait()
    for t in range(row_tiles * TILE):
        place = jnp.where(token == t, here[t], place)
    place = lax.shift_right_logical(place, lane % PIECES * 8) & 255
    place = place.astype(jnp.float32).astype(jnp.bfloat16)
    for head in range(HEADS):
        out[head, last] = place
    for copy in copies:
        copy.wait()


def pack(positions, arrays):
    tiles = [as_tiles(array) for array in arrays]
    slots = ARRAYS * tiles[0].shape[0] + 1
    packed = pl.pallas_call(
        pack_kernel,
        out_shape=pltpu.VMEM((HEADS, slots, TILE, HEAD_DIM), jnp.bfloat16),
        in_specs=[pl.BlockSpec(memory_space=pltpu.HBM)] * (1 + ARRAYS),
        out_specs=pl.BlockSpec(memory_space=pltpu.VMEM),
        scratch_shapes=[
            pltpu.SMEM(positions.shape, jnp.int32),
            pltpu.SemaphoreType.DMA((slots,)),
        ],
        compiler_params=pltpu.CompilerParams(vmem_limit_bytes=56 * 2**20),
        name="pack",
    )(positions, *tiles)
    return packed.reshape(HEADS, slots * TILE, HEAD_DIM)


def dot(a, b, contract):
    return lax.dot_general(a, b, (contract, ((), ())), preferred_element_type=jnp.float32)


def order_of(pair):
    high, low = pair
    return high.astype(jnp.int32) * 65536 + low.astype(jnp.int32)


def attention_kernel(rows, *refs):
    blocks, out = refs[:-1], refs[-1]
    count = HEADS * rows
    scale = HEAD_DIM ** (-0.5)
    lanes = HEAD_DIM * TILE // rows

    def part(ref, at):
        return ref[:, at * rows : (at + 1) * rows, :].reshape(count, HEAD_DIM)

    def places(ref):
        packed = ref[:, ARRAYS * rows :, :].astype(jnp.float32)
        lane = lax.broadcasted_iota(jnp.int32, packed.shape, 2)
        parts = [jnp.where(lane // lanes == at, packed, 0.0) for at in range(rows // TILE)]
        return jnp.stack(parts, axis=1).reshape(count, HEAD_DIM).astype(jnp.bfloat16)

    def weights(shape, axis, first):
        at = lax.broadcasted_iota(jnp.int32, shape, axis) % lanes
        chosen = jnp.where(at == first, 1.0, jnp.where(at == first + 1, 256.0, 0.0))
        return chosen.astype(jnp.bfloat16)

    own = blocks[0]
    queries = part(own, 0)
    query_pair = jnp.concatenate([part(own, 3), queries], axis=1)
    own_order = places(own)
    across = (HEAD_DIM, HEAD_DIM)
    query_order = order_of([dot(own_order, weights(across, 0, first), ((1,), (0,))) for first in (2, 0)])
    state = None
    for start in range(0, len(blocks), 2):
        group = blocks[start : start + 2]

        def keyed(at):
            return jnp.concatenate([part(ref, at) for ref in group], axis=0)

        keys, values, key_dot, value_dot = [keyed(at) for at in (1, 2, 4, 5)]
        order = jnp.concatenate([places(ref) for ref in group], axis=0)
        width = keys.shape[0]
        down = (8, HEAD_DIM)
        key_order = order_of([dot(weights(down, 1, first), order, ((1,), (1,))) for first in (2, 0)])
        wide_order = jnp.concatenate([query_order] * (width // HEAD_DIM), axis=1)
        visible = key_order[:1] <= wide_order
        scores = dot(queries, keys, ((1,), (1,)))
        scores = jnp.where(visible, scores, -1e30)
        key_pair = jnp.concatenate([keys, key_dot], axis=1)
        score_tan = dot(query_pair, key_pair, ((1,), (1,)))
        new_max = jnp.max(scores, axis=1, keepdims=True)
        if state is not None:
            new_max = jnp.maximum(new_max, state[0])
        expo = jnp.exp2((scores - new_max) * (scale * LOG2_E))
        total = jnp.sum(expo, axis=1, keepdims=True)
        both = dot(expo.astype(jnp.bfloat16), jnp.concatenate([values, value_dot], axis=1), ((1,), (0,)))
        summed = jnp.concatenate([values, jnp.ones_like(values)], axis=1)
        moved = dot((expo * score_tan).astype(jnp.bfloat16), summed, ((1,), (0,)))
        if state is not None:
            shrink = jnp.exp2((state[0] - new_max) * (scale * LOG2_E))
            total, both, moved = [new + old * shrink for new, old in zip((total, both, moved), state[1:])]
        state = (new_max, total, both, moved)
    _, total, both, moved = state
    inverse = 1.0 / total
    mixed = both[:, :HEAD_DIM] * inverse
    weighted, mass = moved[:, :HEAD_DIM], moved[:, HEAD_DIM:]
    tangent = both[:, HEAD_DIM:] * inverse + (weighted - mass * mixed) * (inverse * scale)
    out[:, :rows, :] = mixed.astype(jnp.bfloat16).reshape(HEADS, rows, HEAD_DIM)
    out[:, rows:, :] = tangent.astype(jnp.bfloat16).reshape(HEADS, rows, HEAD_DIM)


def attention(rows, blocks):
    return pl.pallas_call(
        functools.partial(attention_kernel, rows),
        out_shape=jax.ShapeDtypeStruct((HEADS, 2 * rows, HEAD_DIM), jnp.bfloat16),
        in_specs=[pl.BlockSpec(memory_space=pltpu.VMEM)] * len(blocks),
        out_specs=pl.BlockSpec(memory_space=pltpu.VMEM),
        compiler_params=pltpu.CompilerParams(vmem_limit_bytes=(8 + len(blocks)) * 2**20),
        name="attention",
    )(*blocks)


def unpack_kernel(packed, *refs):
    outs, sems = refs[:2], refs[2]
    row_tiles = outs[0].shape[0]
    copies = []
    for at, out in enumerate(outs):
        for tile in range(row_tiles):
            slot = at * row_tiles + tile
            copies.append(pltpu.make_async_copy(packed.at[:, slot], out.at[tile], sems.at[slot]))
            copies[-1].start()
    for copy in copies:
        copy.wait()


def unpack(packed):
    slots = packed.shape[1] // TILE
    shape = (slots // 2, HEADS, TILE, HEAD_DIM)
    outs = pl.pallas_call(
        unpack_kernel,
        out_shape=[jax.ShapeDtypeStruct(shape, jnp.bfloat16)] * 2,
        in_specs=[pl.BlockSpec(memory_space=pltpu.VMEM)],
        out_specs=[pl.BlockSpec(memory_space=pltpu.HBM)] * 2,
        scratch_shapes=[pltpu.SemaphoreType.DMA((slots,))],
        compiler_params=pltpu.CompilerParams(vmem_limit_bytes=4 * 2**20),
        name="unpack",
    )(packed.reshape(HEADS, slots, TILE, HEAD_DIM))
    return tuple(from_tiles(out) for out in outs)


def solution(mesh):
    teams = plan(mesh)

    def swap(value):
        return lax.all_to_all(value, AXES, 0, 0, axis_index_groups=teams, tiled=True)

    def from_peer(value, by):
        pairs = [pair for at, team in enumerate(teams) for pair in zip(team, teams[(at + by) % len(teams)])]
        return lax.ppermute(value, AXES, pairs)

    def local(query_main, key_main, value_main, query_tan, key_tan, value_tan, positions):
        rows = query_main.shape[0]
        arrays = (query_main, key_main, value_main, query_tan, key_tan, value_tan)
        here = swap(pack(positions, arrays))
        blocks = [here] + [from_peer(here, by) for by in range(1, len(teams))]
        return unpack(swap(attention(rows, blocks)))

    placed = (P(AXES, None),) * 6 + (P(AXES),)
    return jax.shard_map(
        local,
        mesh=mesh,
        in_specs=placed,
        out_specs=(P(AXES, None), P(AXES, None)),
        check_vma=False,
    )
```

```python
import functools
import math

import jax
import jax.numpy as jnp
from jax import lax
from jax.experimental import pallas as pl
from jax.experimental.pallas import tpu as pltpu
from jax.sharding import PartitionSpec as P

HEADS = 16
HEAD_DIM = 128
LOG2_E = math.log2(math.e)
AXES = ("seq", "head")
TILE = 8
MIDDLE = 11
ARRAYS = 6
PIECES = 4


def plan(mesh):
    heads_axis = mesh.shape["head"]
    peers = mesh.shape["seq"] * heads_axis // HEADS
    assert mesh.shape["seq"] % peers == 0

    def flat(peer, head):
        member = head ^ MIDDLE
        return (member // heads_axis * peers + peer) * heads_axis + member % heads_axis

    return [[flat(peer, head) for head in range(HEADS)] for peer in range(peers)]


def as_tiles(array):
    rows, columns = array.shape
    return array.reshape(rows // TILE, TILE, columns // HEAD_DIM, HEAD_DIM).transpose(0, 2, 1, 3)


def from_tiles(tiles):
    row_tiles, heads = tiles.shape[:2]
    return tiles.transpose(0, 2, 1, 3).reshape(row_tiles * TILE, heads * HEAD_DIM)


def pack_kernel(positions, *refs):
    arrays, (out, here, sems) = refs[:ARRAYS], refs[ARRAYS:]
    row_tiles = arrays[0].shape[0]
    last = ARRAYS * row_tiles
    load = pltpu.make_async_copy(positions, here, sems.at[last])
    load.start()
    copies = []
    for at, array in enumerate(arrays):
        for tile in range(row_tiles):
            slot = at * row_tiles + tile
            copies.append(pltpu.make_async_copy(array.at[tile], out.at[:, slot], sems.at[slot]))
            copies[-1].start()
    token = lax.broadcasted_iota(jnp.int32, (TILE, HEAD_DIM), 0)
    lane = lax.broadcasted_iota(jnp.int32, (TILE, HEAD_DIM), 1)
    token = token + lane // (HEAD_DIM // row_tiles) * TILE
    place = jnp.zeros((TILE, HEAD_DIM), jnp.int32)
    load.wait()
    for t in range(row_tiles * TILE):
        place = jnp.where(token == t, here[t], place)
    place = lax.shift_right_logical(place, lane % PIECES * 8) & 255
    place = place.astype(jnp.float32).astype(jnp.bfloat16)
    for head in range(HEADS):
        out[head, last] = place
    for copy in copies:
        copy.wait()


def pack(positions, arrays):
    tiles = [as_tiles(array) for array in arrays]
    slots = ARRAYS * tiles[0].shape[0] + 1
    packed = pl.pallas_call(
        pack_kernel,
        out_shape=pltpu.VMEM((HEADS, slots, TILE, HEAD_DIM), jnp.bfloat16),
        in_specs=[pl.BlockSpec(memory_space=pltpu.HBM)] * (1 + ARRAYS),
        out_specs=pl.BlockSpec(memory_space=pltpu.VMEM),
        scratch_shapes=[
            pltpu.SMEM(positions.shape, jnp.int32),
            pltpu.SemaphoreType.DMA((slots,)),
        ],
        compiler_params=pltpu.CompilerParams(vmem_limit_bytes=56 * 2**20),
        name="pack",
    )(positions, *tiles)
    return packed.reshape(HEADS, slots * TILE, HEAD_DIM)


def dot(a, b, contract):
    return lax.dot_general(a, b, (contract, ((), ())), preferred_element_type=jnp.float32)


def order_of(pair):
    high, low = pair
    return high.astype(jnp.int32) * 65536 + low.astype(jnp.int32)


def attention_kernel(rows, *refs):
    blocks, out = refs[:-1], refs[-1]
    count = HEADS * rows
    scale = HEAD_DIM ** (-0.5)
    lanes = HEAD_DIM * TILE // rows

    def part(ref, at):
        return ref[:, at * rows : (at + 1) * rows, :].reshape(count, HEAD_DIM)

    def places(ref):
        packed = ref[:, ARRAYS * rows :, :].astype(jnp.float32)
        lane = lax.broadcasted_iota(jnp.int32, packed.shape, 2)
        parts = [jnp.where(lane // lanes == at, packed, 0.0) for at in range(rows // TILE)]
        return jnp.stack(parts, axis=1).reshape(count, HEAD_DIM).astype(jnp.bfloat16)

    def weights(shape, axis, first):
        at = lax.broadcasted_iota(jnp.int32, shape, axis) % lanes
        chosen = jnp.where(at == first, 1.0, jnp.where(at == first + 1, 256.0, 0.0))
        return chosen.astype(jnp.bfloat16)

    own = blocks[0]
    queries = part(own, 0)
    pair = jnp.concatenate([part(own, 3), queries], axis=1)
    rows_pair = jnp.concatenate([queries, jnp.zeros_like(queries)], axis=1)
    query_rows = jnp.concatenate([rows_pair, pair], axis=0)
    own_order = places(own)
    across = (HEAD_DIM, HEAD_DIM)
    query_order = order_of([dot(own_order, weights(across, 0, first), ((1,), (0,))) for first in (2, 0)])
    state = None
    for start in range(0, len(blocks), 2):
        group = blocks[start : start + 2]

        def keyed(at):
            return jnp.concatenate([part(ref, at) for ref in group], axis=0)

        keys, values, key_dot, value_dot = [keyed(at) for at in (1, 2, 4, 5)]
        order = jnp.concatenate([places(ref) for ref in group], axis=0)
        width = keys.shape[0]
        down = (8, HEAD_DIM)
        key_order = order_of([dot(weights(down, 1, first), order, ((1,), (1,))) for first in (2, 0)])
        wide_order = jnp.concatenate([query_order] * (width // HEAD_DIM), axis=1)
        visible = key_order[:1] <= wide_order
        raw = dot(query_rows, jnp.concatenate([keys, key_dot], axis=1), ((1,), (1,)))
        scores = jnp.where(visible, raw[:count], -1e30)
        new_max = jnp.max(scores, axis=1, keepdims=True)
        if state is not None:
            new_max = jnp.maximum(new_max, state[0])
        expo = jnp.exp2((scores - new_max) * (scale * LOG2_E))
        weighted = expo * raw[count:]
        total = jnp.sum(expo, axis=1, keepdims=True)
        mass = jnp.sum(weighted, axis=1, keepdims=True)
        low = jnp.concatenate([expo.astype(jnp.bfloat16), weighted.astype(jnp.bfloat16)], axis=0)
        mixes = dot(low, jnp.concatenate([values, value_dot], axis=1), ((1,), (0,)))
        both, moved = mixes[:count], mixes[count:, :HEAD_DIM]
        if state is not None:
            shrink = jnp.exp2((state[0] - new_max) * (scale * LOG2_E))
            total, mass, both, moved = [
                new + old * shrink for new, old in zip((total, mass, both, moved), state[1:])
            ]
        state = (new_max, total, mass, both, moved)
    _, total, mass, both, moved = state
    inverse = 1.0 / total
    mixed = both[:, :HEAD_DIM] * inverse
    tangent = both[:, HEAD_DIM:] * inverse + (moved - mass * mixed) * (inverse * scale)
    out[:, :rows, :] = mixed.astype(jnp.bfloat16).reshape(HEADS, rows, HEAD_DIM)
    out[:, rows:, :] = tangent.astype(jnp.bfloat16).reshape(HEADS, rows, HEAD_DIM)


def attention(rows, blocks):
    return pl.pallas_call(
        functools.partial(attention_kernel, rows),
        out_shape=jax.ShapeDtypeStruct((HEADS, 2 * rows, HEAD_DIM), jnp.bfloat16),
        in_specs=[pl.BlockSpec(memory_space=pltpu.VMEM)] * len(blocks),
        out_specs=pl.BlockSpec(memory_space=pltpu.VMEM),
        compiler_params=pltpu.CompilerParams(vmem_limit_bytes=(8 + len(blocks)) * 2**20),
        name="attention",
    )(*blocks)


def unpack_kernel(packed, *refs):
    outs, sems = refs[:2], refs[2]
    row_tiles = outs[0].shape[0]
    copies = []
    for at, out in enumerate(outs):
        for tile in range(row_tiles):
            slot = at * row_tiles + tile
            copies.append(pltpu.make_async_copy(packed.at[:, slot], out.at[tile], sems.at[slot]))
            copies[-1].start()
    for copy in copies:
        copy.wait()


def unpack(packed):
    slots = packed.shape[1] // TILE
    shape = (slots // 2, HEADS, TILE, HEAD_DIM)
    outs = pl.pallas_call(
        unpack_kernel,
        out_shape=[jax.ShapeDtypeStruct(shape, jnp.bfloat16)] * 2,
        in_specs=[pl.BlockSpec(memory_space=pltpu.VMEM)],
        out_specs=[pl.BlockSpec(memory_space=pltpu.HBM)] * 2,
        scratch_shapes=[pltpu.SemaphoreType.DMA((slots,))],
        compiler_params=pltpu.CompilerParams(vmem_limit_bytes=4 * 2**20),
        name="unpack",
    )(packed.reshape(HEADS, slots, TILE, HEAD_DIM))
    return tuple(from_tiles(out) for out in outs)


def solution(mesh):
    teams = plan(mesh)

    def swap(value):
        return lax.all_to_all(value, AXES, 0, 0, axis_index_groups=teams, tiled=True)

    def from_peer(value, by):
        pairs = [pair for at, team in enumerate(teams) for pair in zip(team, teams[(at + by) % len(teams)])]
        return lax.ppermute(value, AXES, pairs)

    def local(query_main, key_main, value_main, query_tan, key_tan, value_tan, positions):
        rows = query_main.shape[0]
        arrays = (query_main, key_main, value_main, query_tan, key_tan, value_tan)
        here = swap(pack(positions, arrays))
        blocks = [here] + [from_peer(here, by) for by in range(1, len(teams))]
        return unpack(swap(attention(rows, blocks)))

    placed = (P(AXES, None),) * 6 + (P(AXES),)
    return jax.shard_map(
        local,
        mesh=mesh,
        in_specs=placed,
        out_specs=(P(AXES, None), P(AXES, None)),
        check_vma=False,
    )
```

```python
import functools
import math

import jax
import jax.numpy as jnp
from jax import lax
from jax.experimental import pallas as pl
from jax.experimental.pallas import tpu as pltpu
from jax.sharding import PartitionSpec as P

HEADS = 16
HEAD_DIM = 128
LOG2_E = math.log2(math.e)
AXES = ("seq", "head")
TILE = 8
MIDDLE = 11
ARRAYS = 6
PIECES = 4


def plan(mesh):
    heads_axis = mesh.shape["head"]
    peers = mesh.shape["seq"] * heads_axis // HEADS
    assert mesh.shape["seq"] % peers == 0

    def flat(peer, head):
        member = head ^ MIDDLE
        return (member // heads_axis * peers + peer) * heads_axis + member % heads_axis

    return [[flat(peer, head) for head in range(HEADS)] for peer in range(peers)]


def as_tiles(array):
    rows, columns = array.shape
    return array.reshape(rows // TILE, TILE, columns // HEAD_DIM, HEAD_DIM).transpose(0, 2, 1, 3)


def from_tiles(tiles):
    row_tiles, heads = tiles.shape[:2]
    return tiles.transpose(0, 2, 1, 3).reshape(row_tiles * TILE, heads * HEAD_DIM)


def pack_kernel(positions, *refs):
    arrays, (out, here, sems) = refs[:ARRAYS], refs[ARRAYS:]
    row_tiles = arrays[0].shape[0]
    last = ARRAYS * row_tiles
    load = pltpu.make_async_copy(positions, here, sems.at[last])
    load.start()
    copies = []
    for at, array in enumerate(arrays):
        for tile in range(row_tiles):
            slot = at * row_tiles + tile
            copies.append(pltpu.make_async_copy(array.at[tile], out.at[:, slot], sems.at[slot]))
            copies[-1].start()
    token = lax.broadcasted_iota(jnp.int32, (TILE, HEAD_DIM), 0)
    lane = lax.broadcasted_iota(jnp.int32, (TILE, HEAD_DIM), 1)
    token = token + lane // (HEAD_DIM // row_tiles) * TILE
    place = jnp.zeros((TILE, HEAD_DIM), jnp.int32)
    load.wait()
    for t in range(row_tiles * TILE):
        place = jnp.where(token == t, here[t], place)
    place = lax.shift_right_logical(place, lane % PIECES * 8) & 255
    place = place.astype(jnp.float32).astype(jnp.bfloat16)
    for head in range(HEADS):
        out[head, last] = place
    for copy in copies:
        copy.wait()


def pack(positions, arrays):
    tiles = [as_tiles(array) for array in arrays]
    slots = ARRAYS * tiles[0].shape[0] + 1
    packed = pl.pallas_call(
        pack_kernel,
        out_shape=pltpu.VMEM((HEADS, slots, TILE, HEAD_DIM), jnp.bfloat16),
        in_specs=[pl.BlockSpec(memory_space=pltpu.HBM)] * (1 + ARRAYS),
        out_specs=pl.BlockSpec(memory_space=pltpu.VMEM),
        scratch_shapes=[
            pltpu.SMEM(positions.shape, jnp.int32),
            pltpu.SemaphoreType.DMA((slots,)),
        ],
        compiler_params=pltpu.CompilerParams(vmem_limit_bytes=56 * 2**20),
        name="pack",
    )(positions, *tiles)
    return packed.reshape(HEADS, slots * TILE, HEAD_DIM)


def dot(a, b, contract):
    return lax.dot_general(a, b, (contract, ((), ())), preferred_element_type=jnp.float32)


def order_of(pair):
    high, low = pair
    return high.astype(jnp.int32) * 65536 + low.astype(jnp.int32)


def attention_kernel(rows, *refs):
    blocks, out = refs[:-1], refs[-1]
    count = HEADS * rows
    scale = HEAD_DIM ** (-0.5)
    lanes = HEAD_DIM * TILE // rows

    def part(ref, at):
        return ref[:, at * rows : (at + 1) * rows, :].reshape(count, HEAD_DIM)

    def places(ref):
        packed = ref[:, ARRAYS * rows :, :].astype(jnp.float32)
        lane = lax.broadcasted_iota(jnp.int32, packed.shape, 2)
        parts = [jnp.where(lane // lanes == at, packed, 0.0) for at in range(rows // TILE)]
        return jnp.stack(parts, axis=1).reshape(count, HEAD_DIM).astype(jnp.bfloat16)

    def weights(shape, axis, first):
        at = lax.broadcasted_iota(jnp.int32, shape, axis) % lanes
        chosen = jnp.where(at == first, 1.0, jnp.where(at == first + 1, 256.0, 0.0))
        return chosen.astype(jnp.bfloat16)

    own = blocks[0]
    queries = part(own, 0)
    query_pair = jnp.concatenate([part(own, 3), queries], axis=1)
    own_order = places(own)
    across = (HEAD_DIM, HEAD_DIM)
    query_order = order_of([dot(own_order, weights(across, 0, first), ((1,), (0,))) for first in (2, 0)])
    wide_order = jnp.concatenate([query_order] * (count // HEAD_DIM), axis=1)
    down = (8, HEAD_DIM)
    masked = []
    for ref in blocks:
        key_order = order_of([dot(weights(down, 1, first), places(ref), ((1,), (1,))) for first in (2, 0)])
        scores = dot(queries, part(ref, 1), ((1,), (1,)))
        masked.append(jnp.where(key_order[:1] <= wide_order, scores, -1e30))
    tops = [jnp.max(scores, axis=1, keepdims=True) for scores in masked]
    top = functools.reduce(jnp.maximum, tops)
    total, both, moved = 0.0, 0.0, 0.0
    for ref, scores in zip(blocks, masked):
        keys, values, key_dot, value_dot = [part(ref, at) for at in (1, 2, 4, 5)]
        score_tan = dot(query_pair, jnp.concatenate([keys, key_dot], axis=1), ((1,), (1,)))
        expo = jnp.exp2((scores - top) * (scale * LOG2_E))
        total += jnp.sum(expo, axis=1, keepdims=True)
        both += dot(expo.astype(jnp.bfloat16), jnp.concatenate([values, value_dot], axis=1), ((1,), (0,)))
        summed = jnp.concatenate([values, jnp.ones_like(values)], axis=1)
        moved += dot((expo * score_tan).astype(jnp.bfloat16), summed, ((1,), (0,)))
    inverse = 1.0 / total
    mixed = both[:, :HEAD_DIM] * inverse
    weighted, mass = moved[:, :HEAD_DIM], moved[:, HEAD_DIM:]
    tangent = both[:, HEAD_DIM:] * inverse + (weighted - mass * mixed) * (inverse * scale)
    out[:, :rows, :] = mixed.astype(jnp.bfloat16).reshape(HEADS, rows, HEAD_DIM)
    out[:, rows:, :] = tangent.astype(jnp.bfloat16).reshape(HEADS, rows, HEAD_DIM)


def attention(rows, blocks):
    return pl.pallas_call(
        functools.partial(attention_kernel, rows),
        out_shape=jax.ShapeDtypeStruct((HEADS, 2 * rows, HEAD_DIM), jnp.bfloat16),
        in_specs=[pl.BlockSpec(memory_space=pltpu.VMEM)] * len(blocks),
        out_specs=pl.BlockSpec(memory_space=pltpu.VMEM),
        compiler_params=pltpu.CompilerParams(vmem_limit_bytes=(12 + len(blocks)) * 2**20),
        name="attention",
    )(*blocks)


def unpack_kernel(packed, *refs):
    outs, sems = refs[:2], refs[2]
    row_tiles = outs[0].shape[0]
    copies = []
    for at, out in enumerate(outs):
        for tile in range(row_tiles):
            slot = at * row_tiles + tile
            copies.append(pltpu.make_async_copy(packed.at[:, slot], out.at[tile], sems.at[slot]))
            copies[-1].start()
    for copy in copies:
        copy.wait()


def unpack(packed):
    slots = packed.shape[1] // TILE
    shape = (slots // 2, HEADS, TILE, HEAD_DIM)
    outs = pl.pallas_call(
        unpack_kernel,
        out_shape=[jax.ShapeDtypeStruct(shape, jnp.bfloat16)] * 2,
        in_specs=[pl.BlockSpec(memory_space=pltpu.VMEM)],
        out_specs=[pl.BlockSpec(memory_space=pltpu.HBM)] * 2,
        scratch_shapes=[pltpu.SemaphoreType.DMA((slots,))],
        compiler_params=pltpu.CompilerParams(vmem_limit_bytes=4 * 2**20),
        name="unpack",
    )(packed.reshape(HEADS, slots, TILE, HEAD_DIM))
    return tuple(from_tiles(out) for out in outs)


def solution(mesh):
    teams = plan(mesh)

    def swap(value):
        return lax.all_to_all(value, AXES, 0, 0, axis_index_groups=teams, tiled=True)

    def from_peer(value, by):
        pairs = [pair for at, team in enumerate(teams) for pair in zip(team, teams[(at + by) % len(teams)])]
        return lax.ppermute(value, AXES, pairs)

    def local(query_main, key_main, value_main, query_tan, key_tan, value_tan, positions):
        rows = query_main.shape[0]
        arrays = (query_main, key_main, value_main, query_tan, key_tan, value_tan)
        here = swap(pack(positions, arrays))
        blocks = [here] + [from_peer(here, by) for by in range(1, len(teams))]
        return unpack(swap(attention(rows, blocks)))

    placed = (P(AXES, None),) * 6 + (P(AXES),)
    return jax.shard_map(
        local,
        mesh=mesh,
        in_specs=placed,
        out_specs=(P(AXES, None), P(AXES, None)),
        check_vma=False,
    )
```

```python
import functools
import math

import jax
import jax.numpy as jnp
from jax import lax
from jax.experimental import pallas as pl
from jax.experimental.pallas import tpu as pltpu
from jax.sharding import PartitionSpec as P

HEADS = 16
HEAD_DIM = 128
LOG2_E = math.log2(math.e)
AXES = ("seq", "head")
TILE = 8
MIDDLE = 11
ARRAYS = 6
PIECES = 4


def plan(mesh):
    heads_axis = mesh.shape["head"]
    peers = mesh.shape["seq"] * heads_axis // HEADS
    assert mesh.shape["seq"] % peers == 0

    def flat(peer, head):
        member = head ^ MIDDLE
        return (member // heads_axis * peers + peer) * heads_axis + member % heads_axis

    return [[flat(peer, head) for head in range(HEADS)] for peer in range(peers)]


def as_tiles(array):
    rows, columns = array.shape
    return array.reshape(rows // TILE, TILE, columns // HEAD_DIM, HEAD_DIM).transpose(0, 2, 1, 3)


def from_tiles(tiles):
    row_tiles, heads = tiles.shape[:2]
    return tiles.transpose(0, 2, 1, 3).reshape(row_tiles * TILE, heads * HEAD_DIM)


def pack_kernel(positions, *refs):
    arrays, (out, here, sems) = refs[:ARRAYS], refs[ARRAYS:]
    row_tiles = arrays[0].shape[0]
    last = ARRAYS * row_tiles
    load = pltpu.make_async_copy(positions, here, sems.at[last])
    load.start()
    copies = []
    for at, array in enumerate(arrays):
        for tile in range(row_tiles):
            slot = at * row_tiles + tile
            copies.append(pltpu.make_async_copy(array.at[tile], out.at[:, slot], sems.at[slot]))
            copies[-1].start()
    token = lax.broadcasted_iota(jnp.int32, (TILE, HEAD_DIM), 0)
    lane = lax.broadcasted_iota(jnp.int32, (TILE, HEAD_DIM), 1)
    token = token + lane // (HEAD_DIM // row_tiles) * TILE
    place = jnp.zeros((TILE, HEAD_DIM), jnp.int32)
    load.wait()
    for t in range(row_tiles * TILE):
        place = jnp.where(token == t, here[t], place)
    place = lax.shift_right_logical(place, lane % PIECES * 8) & 255
    place = place.astype(jnp.float32).astype(jnp.bfloat16)
    for head in range(HEADS):
        out[head, last] = place
    for copy in copies:
        copy.wait()


def pack(positions, arrays):
    tiles = [as_tiles(array) for array in arrays]
    slots = ARRAYS * tiles[0].shape[0] + 1
    packed = pl.pallas_call(
        pack_kernel,
        out_shape=pltpu.VMEM((HEADS, slots, TILE, HEAD_DIM), jnp.bfloat16),
        in_specs=[pl.BlockSpec(memory_space=pltpu.HBM)] * (1 + ARRAYS),
        out_specs=pl.BlockSpec(memory_space=pltpu.VMEM),
        scratch_shapes=[
            pltpu.SMEM(positions.shape, jnp.int32),
            pltpu.SemaphoreType.DMA((slots,)),
        ],
        compiler_params=pltpu.CompilerParams(vmem_limit_bytes=56 * 2**20),
        name="pack",
    )(positions, *tiles)
    return packed.reshape(HEADS, slots * TILE, HEAD_DIM)


def without_queries(messages, rows):
    heads, length, lanes = messages.shape

    def kernel(whole, out):
        out[...] = whole[:, 2 * rows :, :]

    return pl.pallas_call(
        kernel,
        out_shape=jax.ShapeDtypeStruct((heads, length - 2 * rows, lanes), messages.dtype),
        in_specs=[pl.BlockSpec(memory_space=pltpu.VMEM)],
        out_specs=pl.BlockSpec(memory_space=pltpu.VMEM),
        compiler_params=pltpu.CompilerParams(vmem_limit_bytes=4 * 2**20),
        name="shared",
    )(messages)


def dot(a, b, contract):
    return lax.dot_general(a, b, (contract, ((), ())), preferred_element_type=jnp.float32)


def order_of(pair):
    high, low = pair
    return high.astype(jnp.int32) * 65536 + low.astype(jnp.int32)


def attention_kernel(rows, *refs):
    blocks, out = refs[:-1], refs[-1]
    own = blocks[0]
    count = HEADS * rows
    scale = HEAD_DIM ** (-0.5)
    lanes = HEAD_DIM * TILE // rows

    def part(ref, at):
        return ref[:, at * rows : (at + 1) * rows, :].reshape(count, HEAD_DIM)

    def key_part(ref, at):
        return part(ref, at + 2 if ref is own else at)

    def places(ref):
        packed = ref[:, ref.shape[1] - TILE :, :].astype(jnp.float32)
        lane = lax.broadcasted_iota(jnp.int32, packed.shape, 2)
        parts = [jnp.where(lane // lanes == at, packed, 0.0) for at in range(rows // TILE)]
        return jnp.stack(parts, axis=1).reshape(count, HEAD_DIM).astype(jnp.bfloat16)

    def weights(shape, axis, first):
        at = lax.broadcasted_iota(jnp.int32, shape, axis) % lanes
        chosen = jnp.where(at == first, 1.0, jnp.where(at == first + 1, 256.0, 0.0))
        return chosen.astype(jnp.bfloat16)

    queries = part(own, 0)
    query_pair = jnp.concatenate([part(own, 1), queries], axis=1)
    own_order = places(own)
    across = (HEAD_DIM, HEAD_DIM)
    query_order = order_of([dot(own_order, weights(across, 0, first), ((1,), (0,))) for first in (2, 0)])
    state = None
    for start in range(0, len(blocks), 2):
        group = blocks[start : start + 2]

        def keyed(at):
            return jnp.concatenate([key_part(ref, at) for ref in group], axis=0)

        keys, values, key_dot, value_dot = [keyed(at) for at in range(4)]
        order = jnp.concatenate([places(ref) for ref in group], axis=0)
        width = keys.shape[0]
        down = (8, HEAD_DIM)
        key_order = order_of([dot(weights(down, 1, first), order, ((1,), (1,))) for first in (2, 0)])
        wide_order = jnp.concatenate([query_order] * (width // HEAD_DIM), axis=1)
        visible = key_order[:1] <= wide_order
        scores = dot(queries, keys, ((1,), (1,)))
        scores = jnp.where(visible, scores, -1e30)
        key_pair = jnp.concatenate([keys, key_dot], axis=1)
        score_tan = dot(query_pair, key_pair, ((1,), (1,)))
        new_max = jnp.max(scores, axis=1, keepdims=True)
        if state is not None:
            new_max = jnp.maximum(new_max, state[0])
        expo = jnp.exp2((scores - new_max) * (scale * LOG2_E))
        total = jnp.sum(expo, axis=1, keepdims=True)
        both = dot(expo.astype(jnp.bfloat16), jnp.concatenate([values, value_dot], axis=1), ((1,), (0,)))
        summed = jnp.concatenate([values, jnp.ones_like(values)], axis=1)
        moved = dot((expo * score_tan).astype(jnp.bfloat16), summed, ((1,), (0,)))
        if state is not None:
            shrink = jnp.exp2((state[0] - new_max) * (scale * LOG2_E))
            total, both, moved = [new + old * shrink for new, old in zip((total, both, moved), state[1:])]
        state = (new_max, total, both, moved)
    _, total, both, moved = state
    inverse = 1.0 / total
    mixed = both[:, :HEAD_DIM] * inverse
    weighted, mass = moved[:, :HEAD_DIM], moved[:, HEAD_DIM:]
    tangent = both[:, HEAD_DIM:] * inverse + (weighted - mass * mixed) * (inverse * scale)
    out[:, :rows, :] = mixed.astype(jnp.bfloat16).reshape(HEADS, rows, HEAD_DIM)
    out[:, rows:, :] = tangent.astype(jnp.bfloat16).reshape(HEADS, rows, HEAD_DIM)


def attention(rows, blocks):
    return pl.pallas_call(
        functools.partial(attention_kernel, rows),
        out_shape=jax.ShapeDtypeStruct((HEADS, 2 * rows, HEAD_DIM), jnp.bfloat16),
        in_specs=[pl.BlockSpec(memory_space=pltpu.VMEM)] * len(blocks),
        out_specs=pl.BlockSpec(memory_space=pltpu.VMEM),
        compiler_params=pltpu.CompilerParams(vmem_limit_bytes=(8 + len(blocks)) * 2**20),
        name="attention",
    )(*blocks)


def unpack_kernel(packed, *refs):
    outs, sems = refs[:2], refs[2]
    row_tiles = outs[0].shape[0]
    copies = []
    for at, out in enumerate(outs):
        for tile in range(row_tiles):
            slot = at * row_tiles + tile
            copies.append(pltpu.make_async_copy(packed.at[:, slot], out.at[tile], sems.at[slot]))
            copies[-1].start()
    for copy in copies:
        copy.wait()


def unpack(packed):
    slots = packed.shape[1] // TILE
    shape = (slots // 2, HEADS, TILE, HEAD_DIM)
    outs = pl.pallas_call(
        unpack_kernel,
        out_shape=[jax.ShapeDtypeStruct(shape, jnp.bfloat16)] * 2,
        in_specs=[pl.BlockSpec(memory_space=pltpu.VMEM)],
        out_specs=[pl.BlockSpec(memory_space=pltpu.HBM)] * 2,
        scratch_shapes=[pltpu.SemaphoreType.DMA((slots,))],
        compiler_params=pltpu.CompilerParams(vmem_limit_bytes=4 * 2**20),
        name="unpack",
    )(packed.reshape(HEADS, slots, TILE, HEAD_DIM))
    return tuple(from_tiles(out) for out in outs)


def solution(mesh):
    teams = plan(mesh)

    def swap(value):
        return lax.all_to_all(value, AXES, 0, 0, axis_index_groups=teams, tiled=True)

    def from_peer(value, by):
        pairs = [pair for at, team in enumerate(teams) for pair in zip(team, teams[(at + by) % len(teams)])]
        return lax.ppermute(value, AXES, pairs)

    def local(query_main, key_main, value_main, query_tan, key_tan, value_tan, positions):
        rows = query_main.shape[0]
        arrays = (query_main, query_tan, key_main, value_main, key_tan, value_tan)
        here = swap(pack(positions, arrays))
        shared = without_queries(here, rows)
        blocks = [here] + [from_peer(shared, by) for by in range(1, len(teams))]
        return unpack(swap(attention(rows, blocks)))

    placed = (P(AXES, None),) * 6 + (P(AXES),)
    return jax.shard_map(
        local,
        mesh=mesh,
        in_specs=placed,
        out_specs=(P(AXES, None), P(AXES, None)),
        check_vma=False,
    )
```

```python
import functools
import math

import jax
import jax.numpy as jnp
from jax import lax
from jax.experimental import pallas as pl
from jax.experimental.pallas import tpu as pltpu
from jax.sharding import PartitionSpec as P

HEADS = 16
HEAD_DIM = 128
LOG2_E = math.log2(math.e)
AXES = ("seq", "head")
TILE = 8
MIDDLE = 11
ARRAYS = 6
PIECES = 4


def plan(mesh):
    heads_axis = mesh.shape["head"]
    peers = mesh.shape["seq"] * heads_axis // HEADS
    assert mesh.shape["seq"] % peers == 0

    def flat(peer, head):
        member = head ^ MIDDLE
        return (member // heads_axis * peers + peer) * heads_axis + member % heads_axis

    return [[flat(peer, head) for head in range(HEADS)] for peer in range(peers)]


def as_tiles(array):
    rows, columns = array.shape
    return array.reshape(rows // TILE, TILE, columns // HEAD_DIM, HEAD_DIM).transpose(0, 2, 1, 3)


def from_tiles(tiles):
    row_tiles, heads = tiles.shape[:2]
    return tiles.transpose(0, 2, 1, 3).reshape(row_tiles * TILE, heads * HEAD_DIM)


def pack_kernel(positions, *refs):
    arrays, (out, here, sems) = refs[:ARRAYS], refs[ARRAYS:]
    row_tiles = arrays[0].shape[0]
    last = ARRAYS * row_tiles
    load = pltpu.make_async_copy(positions, here, sems.at[last])
    load.start()
    copies = []
    for at, array in enumerate(arrays):
        for tile in range(row_tiles):
            slot = at * row_tiles + tile
            copies.append(pltpu.make_async_copy(array.at[tile], out.at[:, slot], sems.at[slot]))
            copies[-1].start()
    token = lax.broadcasted_iota(jnp.int32, (TILE, HEAD_DIM), 0)
    lane = lax.broadcasted_iota(jnp.int32, (TILE, HEAD_DIM), 1)
    token = token + lane // (HEAD_DIM // row_tiles) * TILE
    place = jnp.zeros((TILE, HEAD_DIM), jnp.int32)
    load.wait()
    for t in range(row_tiles * TILE):
        place = jnp.where(token == t, here[t], place)
    place = lax.shift_right_logical(place, lane % PIECES * 8) & 255
    place = place.astype(jnp.float32).astype(jnp.bfloat16)
    for head in range(HEADS):
        out[head, last] = place
    for copy in copies:
        copy.wait()


def pack(positions, arrays):
    tiles = [as_tiles(array) for array in arrays]
    slots = ARRAYS * tiles[0].shape[0] + 1
    packed = pl.pallas_call(
        pack_kernel,
        out_shape=pltpu.VMEM((HEADS, slots, TILE, HEAD_DIM), jnp.bfloat16),
        in_specs=[pl.BlockSpec(memory_space=pltpu.HBM)] * (1 + ARRAYS),
        out_specs=pl.BlockSpec(memory_space=pltpu.VMEM),
        scratch_shapes=[
            pltpu.SMEM(positions.shape, jnp.int32),
            pltpu.SemaphoreType.DMA((slots,)),
        ],
        compiler_params=pltpu.CompilerParams(vmem_limit_bytes=56 * 2**20),
        name="pack",
    )(positions, *tiles)
    return packed.reshape(HEADS, slots * TILE, HEAD_DIM)


def without_queries(messages, rows):
    heads, length, lanes = messages.shape

    def kernel(whole, out):
        out[...] = whole[:, 2 * rows :, :]

    return pl.pallas_call(
        kernel,
        out_shape=jax.ShapeDtypeStruct((heads, length - 2 * rows, lanes), messages.dtype),
        in_specs=[pl.BlockSpec(memory_space=pltpu.VMEM)],
        out_specs=pl.BlockSpec(memory_space=pltpu.VMEM),
        compiler_params=pltpu.CompilerParams(vmem_limit_bytes=4 * 2**20),
        name="shared",
    )(messages)


def dot(a, b, contract):
    return lax.dot_general(a, b, (contract, ((), ())), preferred_element_type=jnp.float32)


def order_of(pair):
    high, low = pair
    return high.astype(jnp.int32) * 65536 + low.astype(jnp.int32)


def part(ref, at, rows):
    return ref[:, at * rows : (at + 1) * rows, :].reshape(-1, HEAD_DIM)


def places(ref, rows):
    lanes = HEAD_DIM * TILE // rows
    packed = ref[:, ref.shape[1] - TILE :, :].astype(jnp.float32)
    lane = lax.broadcasted_iota(jnp.int32, packed.shape, 2)
    parts = [jnp.where(lane // lanes == at, packed, 0.0) for at in range(rows // TILE)]
    return jnp.stack(parts, axis=1).reshape(-1, HEAD_DIM).astype(jnp.bfloat16)


def weights(shape, axis, first, rows):
    at = lax.broadcasted_iota(jnp.int32, shape, axis) % (HEAD_DIM * TILE // rows)
    chosen = jnp.where(at == first, 1.0, jnp.where(at == first + 1, 256.0, 0.0))
    return chosen.astype(jnp.bfloat16)


def score(ref, at, queries, query_pair, query_order, rows):
    keys, key_dot = part(ref, at, rows), part(ref, at + 2, rows)
    order = places(ref, rows)
    pieces = [weights((8, HEAD_DIM), 1, first, rows) for first in (2, 0)]
    key_order = order_of([dot(piece, order, ((1,), (1,))) for piece in pieces])
    wide_order = jnp.concatenate([query_order] * (keys.shape[0] // HEAD_DIM), axis=1)
    scores = dot(queries, keys, ((1,), (1,)))
    scores = jnp.where(key_order[:1] <= wide_order, scores, -1e30)
    return scores, dot(query_pair, jnp.concatenate([keys, key_dot], axis=1), ((1,), (1,)))


def queries_of(own, rows):
    queries = part(own, 0, rows)
    return queries, jnp.concatenate([part(own, 1, rows), queries], axis=1)


def own_kernel(rows, own, scores_out, tan_out, order_out):
    own_order = places(own, rows)
    pieces = [weights((HEAD_DIM, HEAD_DIM), 0, first, rows) for first in (2, 0)]
    query_order = order_of([dot(own_order, piece, ((1,), (0,))) for piece in pieces])
    order_out[...] = query_order
    scores_out[...], tan_out[...] = score(own, 2, *queries_of(own, rows), query_order, rows)


def own_scores(rows, here):
    count = HEADS * rows
    square = jax.ShapeDtypeStruct((count, count), jnp.float32)
    return pl.pallas_call(
        functools.partial(own_kernel, rows),
        out_shape=(square, square, jax.ShapeDtypeStruct((count, HEAD_DIM), jnp.int32)),
        in_specs=[pl.BlockSpec(memory_space=pltpu.VMEM)],
        out_specs=[pl.BlockSpec(memory_space=pltpu.VMEM)] * 3,
        compiler_params=pltpu.CompilerParams(vmem_limit_bytes=10 * 2**20),
        name="own_scores",
    )(here)


def attention_kernel(rows, own_raw, own_tan, order, *refs):
    blocks, out = refs[:-1], refs[-1]
    own = blocks[0]
    scale = HEAD_DIM ** (-0.5)
    queries, query_pair = queries_of(own, rows)
    state = None
    for start in range(0, len(blocks), 2):
        group = blocks[start : start + 2]
        raw = [
            (own_raw[...], own_tan[...])
            if ref is own
            else score(ref, 0, queries, query_pair, order[...], rows)
            for ref in group
        ]
        scores, score_tan = [jnp.concatenate(each, axis=1) for each in zip(*raw)]
        values, value_dot = [
            jnp.concatenate([part(ref, at + 2 if ref is own else at, rows) for ref in group], axis=0)
            for at in (1, 3)
        ]
        new_max = jnp.max(scores, axis=1, keepdims=True)
        if state is not None:
            new_max = jnp.maximum(new_max, state[0])
        expo = jnp.exp2((scores - new_max) * (scale * LOG2_E))
        total = jnp.sum(expo, axis=1, keepdims=True)
        both = dot(expo.astype(jnp.bfloat16), jnp.concatenate([values, value_dot], axis=1), ((1,), (0,)))
        summed = jnp.concatenate([values, jnp.ones_like(values)], axis=1)
        moved = dot((expo * score_tan).astype(jnp.bfloat16), summed, ((1,), (0,)))
        if state is not None:
            shrink = jnp.exp2((state[0] - new_max) * (scale * LOG2_E))
            total, both, moved = [new + old * shrink for new, old in zip((total, both, moved), state[1:])]
        state = (new_max, total, both, moved)
    _, total, both, moved = state
    inverse = 1.0 / total
    mixed = both[:, :HEAD_DIM] * inverse
    weighted, mass = moved[:, :HEAD_DIM], moved[:, HEAD_DIM:]
    tangent = both[:, HEAD_DIM:] * inverse + (weighted - mass * mixed) * (inverse * scale)
    out[:, :rows, :] = mixed.astype(jnp.bfloat16).reshape(HEADS, rows, HEAD_DIM)
    out[:, rows:, :] = tangent.astype(jnp.bfloat16).reshape(HEADS, rows, HEAD_DIM)


def attention(rows, raw, blocks):
    operands = (*raw, *blocks)
    return pl.pallas_call(
        functools.partial(attention_kernel, rows),
        out_shape=jax.ShapeDtypeStruct((HEADS, 2 * rows, HEAD_DIM), jnp.bfloat16),
        in_specs=[pl.BlockSpec(memory_space=pltpu.VMEM)] * len(operands),
        out_specs=pl.BlockSpec(memory_space=pltpu.VMEM),
        compiler_params=pltpu.CompilerParams(vmem_limit_bytes=(10 + len(blocks)) * 2**20),
        name="attention",
    )(*operands)


def unpack_kernel(packed, *refs):
    outs, sems = refs[:2], refs[2]
    row_tiles = outs[0].shape[0]
    copies = []
    for at, out in enumerate(outs):
        for tile in range(row_tiles):
            slot = at * row_tiles + tile
            copies.append(pltpu.make_async_copy(packed.at[:, slot], out.at[tile], sems.at[slot]))
            copies[-1].start()
    for copy in copies:
        copy.wait()


def unpack(packed):
    slots = packed.shape[1] // TILE
    shape = (slots // 2, HEADS, TILE, HEAD_DIM)
    outs = pl.pallas_call(
        unpack_kernel,
        out_shape=[jax.ShapeDtypeStruct(shape, jnp.bfloat16)] * 2,
        in_specs=[pl.BlockSpec(memory_space=pltpu.VMEM)],
        out_specs=[pl.BlockSpec(memory_space=pltpu.HBM)] * 2,
        scratch_shapes=[pltpu.SemaphoreType.DMA((slots,))],
        compiler_params=pltpu.CompilerParams(vmem_limit_bytes=4 * 2**20),
        name="unpack",
    )(packed.reshape(HEADS, slots, TILE, HEAD_DIM))
    return tuple(from_tiles(out) for out in outs)


def solution(mesh):
    teams = plan(mesh)

    def swap(value):
        return lax.all_to_all(value, AXES, 0, 0, axis_index_groups=teams, tiled=True)

    def from_peer(value, by):
        pairs = [pair for at, team in enumerate(teams) for pair in zip(team, teams[(at + by) % len(teams)])]
        return lax.ppermute(value, AXES, pairs)

    def local(query_main, key_main, value_main, query_tan, key_tan, value_tan, positions):
        rows = query_main.shape[0]
        arrays = (query_main, query_tan, key_main, value_main, key_tan, value_tan)
        here = swap(pack(positions, arrays))
        shared = without_queries(here, rows)
        blocks = [here] + [from_peer(shared, by) for by in range(1, len(teams))]
        return unpack(swap(attention(rows, own_scores(rows, here), blocks)))

    placed = (P(AXES, None),) * 6 + (P(AXES),)
    return jax.shard_map(
        local,
        mesh=mesh,
        in_specs=placed,
        out_specs=(P(AXES, None), P(AXES, None)),
        check_vma=False,
    )
```

```python
import functools
import math

import jax
import jax.numpy as jnp
from jax import lax
from jax.experimental import pallas as pl
from jax.experimental.pallas import tpu as pltpu
from jax.sharding import PartitionSpec as P

HEADS = 16
HEAD_DIM = 128
LOG2_E = math.log2(math.e)
AXES = ("seq", "head")
TILE = 8
MIDDLE = 11
ARRAYS = 6
PIECES = 4


def plan(mesh):
    heads_axis = mesh.shape["head"]
    peers = mesh.shape["seq"] * heads_axis // HEADS
    assert mesh.shape["seq"] % peers == 0

    def flat(peer, head):
        member = head ^ MIDDLE
        return (member // heads_axis * peers + peer) * heads_axis + member % heads_axis

    return [[flat(peer, head) for head in range(HEADS)] for peer in range(peers)]


def as_tiles(array):
    rows, columns = array.shape
    return array.reshape(rows // TILE, TILE, columns // HEAD_DIM, HEAD_DIM).transpose(0, 2, 1, 3)


def from_tiles(tiles):
    row_tiles, heads = tiles.shape[:2]
    return tiles.transpose(0, 2, 1, 3).reshape(row_tiles * TILE, heads * HEAD_DIM)


def pack_kernel(positions, *refs):
    arrays, (out, here, sems) = refs[:ARRAYS], refs[ARRAYS:]
    row_tiles = arrays[0].shape[0]
    last = ARRAYS * row_tiles
    load = pltpu.make_async_copy(positions, here, sems.at[last])
    load.start()
    copies = []
    for at, array in enumerate(arrays):
        for tile in range(row_tiles):
            slot = at * row_tiles + tile
            copies.append(pltpu.make_async_copy(array.at[tile], out.at[:, slot], sems.at[slot]))
            copies[-1].start()
    token = lax.broadcasted_iota(jnp.int32, (TILE, HEAD_DIM), 0)
    lane = lax.broadcasted_iota(jnp.int32, (TILE, HEAD_DIM), 1)
    token = token + lane // (HEAD_DIM // row_tiles) * TILE
    place = jnp.zeros((TILE, HEAD_DIM), jnp.int32)
    load.wait()
    for t in range(row_tiles * TILE):
        place = jnp.where(token == t, here[t], place)
    place = lax.shift_right_logical(place, lane % PIECES * 8) & 255
    place = place.astype(jnp.float32).astype(jnp.bfloat16)
    for head in range(HEADS):
        out[head, last] = place
    for copy in copies:
        copy.wait()


def pack(positions, arrays):
    tiles = [as_tiles(array) for array in arrays]
    slots = ARRAYS * tiles[0].shape[0] + 1
    packed = pl.pallas_call(
        pack_kernel,
        out_shape=pltpu.VMEM((HEADS, slots, TILE, HEAD_DIM), jnp.bfloat16),
        in_specs=[pl.BlockSpec(memory_space=pltpu.HBM)] * (1 + ARRAYS),
        out_specs=pl.BlockSpec(memory_space=pltpu.VMEM),
        scratch_shapes=[
            pltpu.SMEM(positions.shape, jnp.int32),
            pltpu.SemaphoreType.DMA((slots,)),
        ],
        compiler_params=pltpu.CompilerParams(vmem_limit_bytes=56 * 2**20),
        name="pack",
    )(positions, *tiles)
    return packed.reshape(HEADS, slots * TILE, HEAD_DIM)


def without_queries(messages, rows):
    heads, length, lanes = messages.shape

    def kernel(whole, out):
        out[...] = whole[:, 2 * rows :, :]

    return pl.pallas_call(
        kernel,
        out_shape=jax.ShapeDtypeStruct((heads, length - 2 * rows, lanes), messages.dtype),
        in_specs=[pl.BlockSpec(memory_space=pltpu.VMEM)],
        out_specs=pl.BlockSpec(memory_space=pltpu.VMEM),
        compiler_params=pltpu.CompilerParams(vmem_limit_bytes=4 * 2**20),
        name="shared",
    )(messages)


def dot(a, b, contract):
    return lax.dot_general(a, b, (contract, ((), ())), preferred_element_type=jnp.float32)


def order_of(pair):
    high, low = pair
    return high.astype(jnp.int32) * 65536 + low.astype(jnp.int32)


def part(ref, at, rows):
    return ref[:, at * rows : (at + 1) * rows, :].reshape(-1, HEAD_DIM)


def places(ref, rows):
    lanes = HEAD_DIM * TILE // rows
    packed = ref[:, ref.shape[1] - TILE :, :].astype(jnp.float32)
    lane = lax.broadcasted_iota(jnp.int32, packed.shape, 2)
    parts = [jnp.where(lane // lanes == at, packed, 0.0) for at in range(rows // TILE)]
    return jnp.stack(parts, axis=1).reshape(-1, HEAD_DIM).astype(jnp.bfloat16)


def weights(shape, axis, first, rows):
    at = lax.broadcasted_iota(jnp.int32, shape, axis) % (HEAD_DIM * TILE // rows)
    chosen = jnp.where(at == first, 1.0, jnp.where(at == first + 1, 256.0, 0.0))
    return chosen.astype(jnp.bfloat16)


def score(ref, at, queries, query_pair, query_order, rows):
    keys, key_dot = part(ref, at, rows), part(ref, at + 2, rows)
    order = places(ref, rows)
    pieces = [weights((8, HEAD_DIM), 1, first, rows) for first in (2, 0)]
    key_order = order_of([dot(piece, order, ((1,), (1,))) for piece in pieces])
    wide_order = jnp.concatenate([query_order] * (keys.shape[0] // HEAD_DIM), axis=1)
    scores = dot(queries, keys, ((1,), (1,)))
    scores = jnp.where(key_order[:1] <= wide_order, scores, -1e30)
    return scores, dot(query_pair, jnp.concatenate([keys, key_dot], axis=1), ((1,), (1,)))


def queries_of(own, rows):
    queries = part(own, 0, rows)
    return queries, jnp.concatenate([part(own, 1, rows), queries], axis=1)


def sums(scores, score_tan, top, values, value_dot):
    scale = HEAD_DIM ** (-0.5)
    expo = jnp.exp2((scores - top) * (scale * LOG2_E))
    both = dot(expo.astype(jnp.bfloat16), jnp.concatenate([values, value_dot], axis=1), ((1,), (0,)))
    summed = jnp.concatenate([values, jnp.ones_like(values)], axis=1)
    moved = dot((expo * score_tan).astype(jnp.bfloat16), summed, ((1,), (0,)))
    return jnp.sum(expo, axis=1, keepdims=True), both, moved


def own_kernel(rows, own, top_out, total_out, both_out, moved_out, order_out):
    own_order = places(own, rows)
    pieces = [weights((HEAD_DIM, HEAD_DIM), 0, first, rows) for first in (2, 0)]
    query_order = order_of([dot(own_order, piece, ((1,), (0,))) for piece in pieces])
    scores, score_tan = score(own, 2, *queries_of(own, rows), query_order, rows)
    top = jnp.max(scores, axis=1, keepdims=True)
    total, both, moved = sums(scores, score_tan, top, part(own, 3, rows), part(own, 5, rows))
    order_out[...] = query_order
    top_out[...] = jnp.broadcast_to(top, top_out.shape)
    total_out[...] = jnp.broadcast_to(total, total_out.shape)
    both_out[...], moved_out[...] = both, moved


def own_keys(rows, here):
    count = HEADS * rows
    narrow, wide = [jax.ShapeDtypeStruct((count, at * HEAD_DIM), jnp.float32) for at in (1, 2)]
    order = jax.ShapeDtypeStruct((count, HEAD_DIM), jnp.int32)
    return pl.pallas_call(
        functools.partial(own_kernel, rows),
        out_shape=(narrow, narrow, wide, wide, order),
        in_specs=[pl.BlockSpec(memory_space=pltpu.VMEM)],
        out_specs=[pl.BlockSpec(memory_space=pltpu.VMEM)] * 5,
        compiler_params=pltpu.CompilerParams(vmem_limit_bytes=10 * 2**20),
        name="own_keys",
    )(here)


def attention_kernel(rows, own, top_in, total_in, both_in, moved_in, order, *refs):
    blocks, out = refs[:-1], refs[-1]
    scale = HEAD_DIM ** (-0.5)
    queries, query_pair = queries_of(own, rows)
    top, total, both, moved = top_in[...][:, :1], total_in[...][:, :1], both_in[...], moved_in[...]
    for ref in blocks:
        scores, score_tan = score(ref, 0, queries, query_pair, order[...], rows)
        new_top = jnp.maximum(jnp.max(scores, axis=1, keepdims=True), top)
        new = sums(scores, score_tan, new_top, part(ref, 1, rows), part(ref, 3, rows))
        shrink = jnp.exp2((top - new_top) * (scale * LOG2_E))
        total, both, moved = [now + old * shrink for now, old in zip(new, (total, both, moved))]
        top = new_top
    inverse = 1.0 / total
    mixed = both[:, :HEAD_DIM] * inverse
    weighted, mass = moved[:, :HEAD_DIM], moved[:, HEAD_DIM:]
    tangent = both[:, HEAD_DIM:] * inverse + (weighted - mass * mixed) * (inverse * scale)
    out[:, :rows, :] = mixed.astype(jnp.bfloat16).reshape(HEADS, rows, HEAD_DIM)
    out[:, rows:, :] = tangent.astype(jnp.bfloat16).reshape(HEADS, rows, HEAD_DIM)


def attention(rows, here, others):
    operands = (here, *own_keys(rows, here), *others)
    return pl.pallas_call(
        functools.partial(attention_kernel, rows),
        out_shape=jax.ShapeDtypeStruct((HEADS, 2 * rows, HEAD_DIM), jnp.bfloat16),
        in_specs=[pl.BlockSpec(memory_space=pltpu.VMEM)] * len(operands),
        out_specs=pl.BlockSpec(memory_space=pltpu.VMEM),
        compiler_params=pltpu.CompilerParams(vmem_limit_bytes=(10 + len(others)) * 2**20),
        name="attention",
    )(*operands)


def unpack_kernel(packed, *refs):
    outs, sems = refs[:2], refs[2]
    row_tiles = outs[0].shape[0]
    copies = []
    for at, out in enumerate(outs):
        for tile in range(row_tiles):
            slot = at * row_tiles + tile
            copies.append(pltpu.make_async_copy(packed.at[:, slot], out.at[tile], sems.at[slot]))
            copies[-1].start()
    for copy in copies:
        copy.wait()


def unpack(packed):
    slots = packed.shape[1] // TILE
    shape = (slots // 2, HEADS, TILE, HEAD_DIM)
    outs = pl.pallas_call(
        unpack_kernel,
        out_shape=[jax.ShapeDtypeStruct(shape, jnp.bfloat16)] * 2,
        in_specs=[pl.BlockSpec(memory_space=pltpu.VMEM)],
        out_specs=[pl.BlockSpec(memory_space=pltpu.HBM)] * 2,
        scratch_shapes=[pltpu.SemaphoreType.DMA((slots,))],
        compiler_params=pltpu.CompilerParams(vmem_limit_bytes=4 * 2**20),
        name="unpack",
    )(packed.reshape(HEADS, slots, TILE, HEAD_DIM))
    return tuple(from_tiles(out) for out in outs)


def solution(mesh):
    teams = plan(mesh)

    def swap(value):
        return lax.all_to_all(value, AXES, 0, 0, axis_index_groups=teams, tiled=True)

    def from_peer(value, by):
        pairs = [pair for at, team in enumerate(teams) for pair in zip(team, teams[(at + by) % len(teams)])]
        return lax.ppermute(value, AXES, pairs)

    def local(query_main, key_main, value_main, query_tan, key_tan, value_tan, positions):
        rows = query_main.shape[0]
        arrays = (query_main, query_tan, key_main, value_main, key_tan, value_tan)
        here = swap(pack(positions, arrays))
        shared = without_queries(here, rows)
        others = [from_peer(shared, by) for by in range(1, len(teams))]
        return unpack(swap(attention(rows, here, others)))

    placed = (P(AXES, None),) * 6 + (P(AXES),)
    return jax.shard_map(
        local,
        mesh=mesh,
        in_specs=placed,
        out_specs=(P(AXES, None), P(AXES, None)),
        check_vma=False,
    )
```

```python
import functools
import math

import jax
import jax.numpy as jnp
from jax import lax
from jax.experimental import pallas as pl
from jax.experimental.pallas import tpu as pltpu
from jax.sharding import PartitionSpec as P

HEADS = 16
HEAD_DIM = 128
LOG2_E = math.log2(math.e)
AXES = ("seq", "head")
TILE = 8
MIDDLE = 11
ARRAYS = 6
PIECES = 4


def plan(mesh):
    heads_axis = mesh.shape["head"]
    peers = mesh.shape["seq"] * heads_axis // HEADS
    assert mesh.shape["seq"] % peers == 0

    def flat(peer, head):
        member = head ^ MIDDLE
        return (member // heads_axis * peers + peer) * heads_axis + member % heads_axis

    return [[flat(peer, head) for head in range(HEADS)] for peer in range(peers)]


def as_tiles(array):
    rows, columns = array.shape
    return array.reshape(rows // TILE, TILE, columns // HEAD_DIM, HEAD_DIM).transpose(0, 2, 1, 3)


def from_tiles(tiles):
    row_tiles, heads = tiles.shape[:2]
    return tiles.transpose(0, 2, 1, 3).reshape(row_tiles * TILE, heads * HEAD_DIM)


def pack_kernel(positions, *refs):
    arrays, (out, here, sems) = refs[:ARRAYS], refs[ARRAYS:]
    row_tiles = arrays[0].shape[0]
    last = ARRAYS * row_tiles
    load = pltpu.make_async_copy(positions, here, sems.at[2 * last])
    load.start()
    copies = []
    for at, array in enumerate(arrays):
        for tile in range(row_tiles):
            slot = at * row_tiles + tile
            for half in range(2):
                heads = pl.ds(half * HEADS // 2, HEADS // 2)
                sem = sems.at[len(copies)]
                copies.append(pltpu.make_async_copy(array.at[tile, heads], out.at[heads, slot], sem))
                copies[-1].start()
    token = lax.broadcasted_iota(jnp.int32, (TILE, HEAD_DIM), 0)
    lane = lax.broadcasted_iota(jnp.int32, (TILE, HEAD_DIM), 1)
    token = token + lane // (HEAD_DIM // row_tiles) * TILE
    place = jnp.zeros((TILE, HEAD_DIM), jnp.int32)
    load.wait()
    for t in range(row_tiles * TILE):
        place = jnp.where(token == t, here[t], place)
    place = lax.shift_right_logical(place, lane % PIECES * 8) & 255
    place = place.astype(jnp.float32).astype(jnp.bfloat16)
    for head in range(HEADS):
        out[head, last] = place
    for copy in copies:
        copy.wait()


def pack(positions, arrays):
    tiles = [as_tiles(array) for array in arrays]
    slots = ARRAYS * tiles[0].shape[0] + 1
    packed = pl.pallas_call(
        pack_kernel,
        out_shape=pltpu.VMEM((HEADS, slots, TILE, HEAD_DIM), jnp.bfloat16),
        in_specs=[pl.BlockSpec(memory_space=pltpu.HBM)] * (1 + ARRAYS),
        out_specs=pl.BlockSpec(memory_space=pltpu.VMEM),
        scratch_shapes=[
            pltpu.SMEM(positions.shape, jnp.int32),
            pltpu.SemaphoreType.DMA((2 * slots - 1,)),
        ],
        compiler_params=pltpu.CompilerParams(vmem_limit_bytes=56 * 2**20),
        name="pack",
    )(positions, *tiles)
    return packed.reshape(HEADS, slots * TILE, HEAD_DIM)


def without_queries(messages, rows):
    heads, length, lanes = messages.shape

    def kernel(whole, out):
        out[...] = whole[:, 2 * rows :, :]

    return pl.pallas_call(
        kernel,
        out_shape=jax.ShapeDtypeStruct((heads, length - 2 * rows, lanes), messages.dtype),
        in_specs=[pl.BlockSpec(memory_space=pltpu.VMEM)],
        out_specs=pl.BlockSpec(memory_space=pltpu.VMEM),
        compiler_params=pltpu.CompilerParams(vmem_limit_bytes=4 * 2**20),
        name="shared",
    )(messages)


def dot(a, b, contract):
    return lax.dot_general(a, b, (contract, ((), ())), preferred_element_type=jnp.float32)


def order_of(pair):
    high, low = pair
    return high.astype(jnp.int32) * 65536 + low.astype(jnp.int32)


def part(ref, at, rows):
    return ref[:, at * rows : (at + 1) * rows, :].reshape(-1, HEAD_DIM)


def places(ref, rows):
    lanes = HEAD_DIM * TILE // rows
    packed = ref[:, ref.shape[1] - TILE :, :].astype(jnp.float32)
    lane = lax.broadcasted_iota(jnp.int32, packed.shape, 2)
    parts = [jnp.where(lane // lanes == at, packed, 0.0) for at in range(rows // TILE)]
    return jnp.stack(parts, axis=1).reshape(-1, HEAD_DIM).astype(jnp.bfloat16)


def weights(shape, axis, first, rows):
    at = lax.broadcasted_iota(jnp.int32, shape, axis) % (HEAD_DIM * TILE // rows)
    chosen = jnp.where(at == first, 1.0, jnp.where(at == first + 1, 256.0, 0.0))
    return chosen.astype(jnp.bfloat16)


def score(ref, at, queries, query_pair, query_order, rows):
    keys, key_dot = part(ref, at, rows), part(ref, at + 2, rows)
    order = places(ref, rows)
    pieces = [weights((8, HEAD_DIM), 1, first, rows) for first in (2, 0)]
    key_order = order_of([dot(piece, order, ((1,), (1,))) for piece in pieces])
    wide_order = jnp.concatenate([query_order] * (keys.shape[0] // HEAD_DIM), axis=1)
    scores = dot(queries, keys, ((1,), (1,)))
    scores = jnp.where(key_order[:1] <= wide_order, scores, -1e30)
    return scores, dot(query_pair, jnp.concatenate([keys, key_dot], axis=1), ((1,), (1,)))


def queries_of(own, rows):
    queries = part(own, 0, rows)
    return queries, jnp.concatenate([part(own, 1, rows), queries], axis=1)


def own_kernel(rows, own, scores_out, tan_out, order_out):
    own_order = places(own, rows)
    pieces = [weights((HEAD_DIM, HEAD_DIM), 0, first, rows) for first in (2, 0)]
    query_order = order_of([dot(own_order, piece, ((1,), (0,))) for piece in pieces])
    order_out[...] = query_order
    scores_out[...], tan_out[...] = score(own, 2, *queries_of(own, rows), query_order, rows)


def own_scores(rows, here):
    count = HEADS * rows
    square = jax.ShapeDtypeStruct((count, count), jnp.float32)
    return pl.pallas_call(
        functools.partial(own_kernel, rows),
        out_shape=(square, square, jax.ShapeDtypeStruct((count, HEAD_DIM), jnp.int32)),
        in_specs=[pl.BlockSpec(memory_space=pltpu.VMEM)],
        out_specs=[pl.BlockSpec(memory_space=pltpu.VMEM)] * 3,
        compiler_params=pltpu.CompilerParams(vmem_limit_bytes=10 * 2**20),
        name="own_scores",
    )(here)


def attention_kernel(rows, own_raw, own_tan, order, *refs):
    blocks, out = refs[:-1], refs[-1]
    own = blocks[0]
    scale = HEAD_DIM ** (-0.5)
    queries, query_pair = queries_of(own, rows)
    state = None
    for start in range(0, len(blocks), 2):
        group = blocks[start : start + 2]
        raw = [
            (own_raw[...], own_tan[...])
            if ref is own
            else score(ref, 0, queries, query_pair, order[...], rows)
            for ref in group
        ]
        scores, score_tan = [jnp.concatenate(each, axis=1) for each in zip(*raw)]
        values, value_dot = [
            jnp.concatenate([part(ref, at + 2 if ref is own else at, rows) for ref in group], axis=0)
            for at in (1, 3)
        ]
        new_max = jnp.max(scores, axis=1, keepdims=True)
        if state is not None:
            new_max = jnp.maximum(new_max, state[0])
        expo = jnp.exp2((scores - new_max) * (scale * LOG2_E))
        total = jnp.sum(expo, axis=1, keepdims=True)
        both = dot(expo.astype(jnp.bfloat16), jnp.concatenate([values, value_dot], axis=1), ((1,), (0,)))
        summed = jnp.concatenate([values, jnp.ones_like(values)], axis=1)
        moved = dot((expo * score_tan).astype(jnp.bfloat16), summed, ((1,), (0,)))
        if state is not None:
            shrink = jnp.exp2((state[0] - new_max) * (scale * LOG2_E))
            total, both, moved = [new + old * shrink for new, old in zip((total, both, moved), state[1:])]
        state = (new_max, total, both, moved)
    _, total, both, moved = state
    inverse = 1.0 / total
    mixed = both[:, :HEAD_DIM] * inverse
    weighted, mass = moved[:, :HEAD_DIM], moved[:, HEAD_DIM:]
    tangent = both[:, HEAD_DIM:] * inverse + (weighted - mass * mixed) * (inverse * scale)
    out[:, :rows, :] = mixed.astype(jnp.bfloat16).reshape(HEADS, rows, HEAD_DIM)
    out[:, rows:, :] = tangent.astype(jnp.bfloat16).reshape(HEADS, rows, HEAD_DIM)


def attention(rows, raw, blocks):
    operands = (*raw, *blocks)
    return pl.pallas_call(
        functools.partial(attention_kernel, rows),
        out_shape=jax.ShapeDtypeStruct((HEADS, 2 * rows, HEAD_DIM), jnp.bfloat16),
        in_specs=[pl.BlockSpec(memory_space=pltpu.VMEM)] * len(operands),
        out_specs=pl.BlockSpec(memory_space=pltpu.VMEM),
        compiler_params=pltpu.CompilerParams(vmem_limit_bytes=(10 + len(blocks)) * 2**20),
        name="attention",
    )(*operands)


def unpack_kernel(packed, *refs):
    outs, sems = refs[:2], refs[2]
    row_tiles = outs[0].shape[0]
    copies = []
    for at, out in enumerate(outs):
        for tile in range(row_tiles):
            slot = at * row_tiles + tile
            copies.append(pltpu.make_async_copy(packed.at[:, slot], out.at[tile], sems.at[slot]))
            copies[-1].start()
    for copy in copies:
        copy.wait()


def unpack(packed):
    slots = packed.shape[1] // TILE
    shape = (slots // 2, HEADS, TILE, HEAD_DIM)
    outs = pl.pallas_call(
        unpack_kernel,
        out_shape=[jax.ShapeDtypeStruct(shape, jnp.bfloat16)] * 2,
        in_specs=[pl.BlockSpec(memory_space=pltpu.VMEM)],
        out_specs=[pl.BlockSpec(memory_space=pltpu.HBM)] * 2,
        scratch_shapes=[pltpu.SemaphoreType.DMA((slots,))],
        compiler_params=pltpu.CompilerParams(vmem_limit_bytes=4 * 2**20),
        name="unpack",
    )(packed.reshape(HEADS, slots, TILE, HEAD_DIM))
    return tuple(from_tiles(out) for out in outs)


def solution(mesh):
    teams = plan(mesh)

    def swap(value):
        return lax.all_to_all(value, AXES, 0, 0, axis_index_groups=teams, tiled=True)

    def from_peer(value, by):
        pairs = [pair for at, team in enumerate(teams) for pair in zip(team, teams[(at + by) % len(teams)])]
        return lax.ppermute(value, AXES, pairs)

    def local(query_main, key_main, value_main, query_tan, key_tan, value_tan, positions):
        rows = query_main.shape[0]
        arrays = (query_main, query_tan, key_main, value_main, key_tan, value_tan)
        here = swap(pack(positions, arrays))
        shared = without_queries(here, rows)
        blocks = [here] + [from_peer(shared, by) for by in range(1, len(teams))]
        return unpack(swap(attention(rows, own_scores(rows, here), blocks)))

    placed = (P(AXES, None),) * 6 + (P(AXES),)
    return jax.shard_map(
        local,
        mesh=mesh,
        in_specs=placed,
        out_specs=(P(AXES, None), P(AXES, None)),
        check_vma=False,
    )
```

```python
import functools
import math

import jax
import jax.numpy as jnp
from jax import lax
from jax.experimental import pallas as pl
from jax.experimental.pallas import tpu as pltpu
from jax.sharding import PartitionSpec as P

HEADS = 16
HEAD_DIM = 128
LOG2_E = math.log2(math.e)
AXES = ("seq", "head")
TILE = 8
MIDDLE = 11
ARRAYS = 6
PIECES = 4


def plan(mesh):
    heads_axis = mesh.shape["head"]
    peers = mesh.shape["seq"] * heads_axis // HEADS
    assert mesh.shape["seq"] % peers == 0

    def flat(peer, head):
        member = head ^ MIDDLE
        return (member // heads_axis * peers + peer) * heads_axis + member % heads_axis

    return [[flat(peer, head) for head in range(HEADS)] for peer in range(peers)]


def as_tiles(array):
    rows, columns = array.shape
    return array.reshape(rows // TILE, TILE, columns // HEAD_DIM, HEAD_DIM).transpose(0, 2, 1, 3)


def from_tiles(tiles):
    row_tiles, heads = tiles.shape[:2]
    return tiles.transpose(0, 2, 1, 3).reshape(row_tiles * TILE, heads * HEAD_DIM)


def pack_kernel(positions, *refs):
    arrays, (out, here, sems) = refs[:ARRAYS], refs[ARRAYS:]
    row_tiles = arrays[0].shape[0]
    last = ARRAYS * row_tiles
    load = pltpu.make_async_copy(positions, here, sems.at[last])
    copies = []
    for at, array in enumerate(arrays):
        for tile in range(row_tiles):
            slot = at * row_tiles + tile
            copies.append(pltpu.make_async_copy(array.at[tile], out.at[:, slot], sems.at[slot]))
            copies[-1].start()
    load.start()
    token = lax.broadcasted_iota(jnp.int32, (TILE, HEAD_DIM), 0)
    lane = lax.broadcasted_iota(jnp.int32, (TILE, HEAD_DIM), 1)
    token = token + lane // (HEAD_DIM // row_tiles) * TILE
    place = jnp.zeros((TILE, HEAD_DIM), jnp.int32)
    load.wait()
    for t in range(row_tiles * TILE):
        place = jnp.where(token == t, here[t], place)
    place = lax.shift_right_logical(place, lane % PIECES * 8) & 255
    place = place.astype(jnp.float32).astype(jnp.bfloat16)
    for head in range(HEADS):
        out[head, last] = place
    for copy in copies:
        copy.wait()


def pack(positions, arrays):
    tiles = [as_tiles(array) for array in arrays]
    slots = ARRAYS * tiles[0].shape[0] + 1
    packed = pl.pallas_call(
        pack_kernel,
        out_shape=pltpu.VMEM((HEADS, slots, TILE, HEAD_DIM), jnp.bfloat16),
        in_specs=[pl.BlockSpec(memory_space=pltpu.HBM)] * (1 + ARRAYS),
        out_specs=pl.BlockSpec(memory_space=pltpu.VMEM),
        scratch_shapes=[
            pltpu.SMEM(positions.shape, jnp.int32),
            pltpu.SemaphoreType.DMA((slots,)),
        ],
        compiler_params=pltpu.CompilerParams(vmem_limit_bytes=56 * 2**20),
        name="pack",
    )(positions, *tiles)
    return packed.reshape(HEADS, slots * TILE, HEAD_DIM)


def without_queries(messages, rows):
    heads, length, lanes = messages.shape

    def kernel(whole, out):
        out[...] = whole[:, 2 * rows :, :]

    return pl.pallas_call(
        kernel,
        out_shape=jax.ShapeDtypeStruct((heads, length - 2 * rows, lanes), messages.dtype),
        in_specs=[pl.BlockSpec(memory_space=pltpu.VMEM)],
        out_specs=pl.BlockSpec(memory_space=pltpu.VMEM),
        compiler_params=pltpu.CompilerParams(vmem_limit_bytes=4 * 2**20),
        name="shared",
    )(messages)


def dot(a, b, contract):
    return lax.dot_general(a, b, (contract, ((), ())), preferred_element_type=jnp.float32)


def order_of(pair):
    high, low = pair
    return high.astype(jnp.int32) * 65536 + low.astype(jnp.int32)


def part(ref, at, rows):
    return ref[:, at * rows : (at + 1) * rows, :].reshape(-1, HEAD_DIM)


def places(ref, rows):
    lanes = HEAD_DIM * TILE // rows
    packed = ref[:, ref.shape[1] - TILE :, :].astype(jnp.float32)
    lane = lax.broadcasted_iota(jnp.int32, packed.shape, 2)
    parts = [jnp.where(lane // lanes == at, packed, 0.0) for at in range(rows // TILE)]
    return jnp.stack(parts, axis=1).reshape(-1, HEAD_DIM).astype(jnp.bfloat16)


def weights(shape, axis, first, rows):
    at = lax.broadcasted_iota(jnp.int32, shape, axis) % (HEAD_DIM * TILE // rows)
    chosen = jnp.where(at == first, 1.0, jnp.where(at == first + 1, 256.0, 0.0))
    return chosen.astype(jnp.bfloat16)


def score(ref, at, queries, query_pair, query_order, rows):
    keys, key_dot = part(ref, at, rows), part(ref, at + 2, rows)
    order = places(ref, rows)
    pieces = [weights((8, HEAD_DIM), 1, first, rows) for first in (2, 0)]
    key_order = order_of([dot(piece, order, ((1,), (1,))) for piece in pieces])
    wide_order = jnp.concatenate([query_order] * (keys.shape[0] // HEAD_DIM), axis=1)
    scores = dot(queries, keys, ((1,), (1,)))
    scores = jnp.where(key_order[:1] <= wide_order, scores, -1e30)
    return scores, dot(query_pair, jnp.concatenate([keys, key_dot], axis=1), ((1,), (1,)))


def queries_of(own, rows):
    queries = part(own, 0, rows)
    return queries, jnp.concatenate([part(own, 1, rows), queries], axis=1)


def own_kernel(rows, own, scores_out, tan_out, order_out):
    own_order = places(own, rows)
    pieces = [weights((HEAD_DIM, HEAD_DIM), 0, first, rows) for first in (2, 0)]
    query_order = order_of([dot(own_order, piece, ((1,), (0,))) for piece in pieces])
    order_out[...] = query_order
    scores_out[...], tan_out[...] = score(own, 2, *queries_of(own, rows), query_order, rows)


def own_scores(rows, here):
    count = HEADS * rows
    square = jax.ShapeDtypeStruct((count, count), jnp.float32)
    return pl.pallas_call(
        functools.partial(own_kernel, rows),
        out_shape=(square, square, jax.ShapeDtypeStruct((count, HEAD_DIM), jnp.int32)),
        in_specs=[pl.BlockSpec(memory_space=pltpu.VMEM)],
        out_specs=[pl.BlockSpec(memory_space=pltpu.VMEM)] * 3,
        compiler_params=pltpu.CompilerParams(vmem_limit_bytes=10 * 2**20),
        name="own_scores",
    )(here)


def attention_kernel(rows, own_raw, own_tan, order, *refs):
    blocks, out = refs[:-1], refs[-1]
    own = blocks[0]
    scale = HEAD_DIM ** (-0.5)
    queries, query_pair = queries_of(own, rows)
    state = None
    for start in range(0, len(blocks), 2):
        group = blocks[start : start + 2]
        raw = [
            (own_raw[...], own_tan[...])
            if ref is own
            else score(ref, 0, queries, query_pair, order[...], rows)
            for ref in group
        ]
        scores, score_tan = [jnp.concatenate(each, axis=1) for each in zip(*raw)]
        values, value_dot = [
            jnp.concatenate([part(ref, at + 2 if ref is own else at, rows) for ref in group], axis=0)
            for at in (1, 3)
        ]
        new_max = jnp.max(scores, axis=1, keepdims=True)
        if state is not None:
            new_max = jnp.maximum(new_max, state[0])
        expo = jnp.exp2((scores - new_max) * (scale * LOG2_E))
        total = jnp.sum(expo, axis=1, keepdims=True)
        both = dot(expo.astype(jnp.bfloat16), jnp.concatenate([values, value_dot], axis=1), ((1,), (0,)))
        summed = jnp.concatenate([values, jnp.ones_like(values)], axis=1)
        moved = dot((expo * score_tan).astype(jnp.bfloat16), summed, ((1,), (0,)))
        if state is not None:
            shrink = jnp.exp2((state[0] - new_max) * (scale * LOG2_E))
            total, both, moved = [new + old * shrink for new, old in zip((total, both, moved), state[1:])]
        state = (new_max, total, both, moved)
    _, total, both, moved = state
    inverse = 1.0 / total
    mixed = both[:, :HEAD_DIM] * inverse
    weighted, mass = moved[:, :HEAD_DIM], moved[:, HEAD_DIM:]
    tangent = both[:, HEAD_DIM:] * inverse + (weighted - mass * mixed) * (inverse * scale)
    out[:, :rows, :] = mixed.astype(jnp.bfloat16).reshape(HEADS, rows, HEAD_DIM)
    out[:, rows:, :] = tangent.astype(jnp.bfloat16).reshape(HEADS, rows, HEAD_DIM)


def attention(rows, raw, blocks):
    operands = (*raw, *blocks)
    return pl.pallas_call(
        functools.partial(attention_kernel, rows),
        out_shape=jax.ShapeDtypeStruct((HEADS, 2 * rows, HEAD_DIM), jnp.bfloat16),
        in_specs=[pl.BlockSpec(memory_space=pltpu.VMEM)] * len(operands),
        out_specs=pl.BlockSpec(memory_space=pltpu.VMEM),
        compiler_params=pltpu.CompilerParams(vmem_limit_bytes=(10 + len(blocks)) * 2**20),
        name="attention",
    )(*operands)


def unpack_kernel(packed, *refs):
    outs, sems = refs[:2], refs[2]
    row_tiles = outs[0].shape[0]
    copies = []
    for at, out in enumerate(outs):
        for tile in range(row_tiles):
            slot = at * row_tiles + tile
            copies.append(pltpu.make_async_copy(packed.at[:, slot], out.at[tile], sems.at[slot]))
            copies[-1].start()
    for copy in copies:
        copy.wait()


def unpack(packed):
    slots = packed.shape[1] // TILE
    shape = (slots // 2, HEADS, TILE, HEAD_DIM)
    outs = pl.pallas_call(
        unpack_kernel,
        out_shape=[jax.ShapeDtypeStruct(shape, jnp.bfloat16)] * 2,
        in_specs=[pl.BlockSpec(memory_space=pltpu.VMEM)],
        out_specs=[pl.BlockSpec(memory_space=pltpu.HBM)] * 2,
        scratch_shapes=[pltpu.SemaphoreType.DMA((slots,))],
        compiler_params=pltpu.CompilerParams(vmem_limit_bytes=4 * 2**20),
        name="unpack",
    )(packed.reshape(HEADS, slots, TILE, HEAD_DIM))
    return tuple(from_tiles(out) for out in outs)


def solution(mesh):
    teams = plan(mesh)

    def swap(value):
        return lax.all_to_all(value, AXES, 0, 0, axis_index_groups=teams, tiled=True)

    def from_peer(value, by):
        pairs = [pair for at, team in enumerate(teams) for pair in zip(team, teams[(at + by) % len(teams)])]
        return lax.ppermute(value, AXES, pairs)

    def local(query_main, key_main, value_main, query_tan, key_tan, value_tan, positions):
        rows = query_main.shape[0]
        arrays = (query_main, query_tan, key_main, value_main, key_tan, value_tan)
        here = swap(pack(positions, arrays))
        shared = without_queries(here, rows)
        blocks = [here] + [from_peer(shared, by) for by in range(1, len(teams))]
        return unpack(swap(attention(rows, own_scores(rows, here), blocks)))

    placed = (P(AXES, None),) * 6 + (P(AXES),)
    return jax.shard_map(
        local,
        mesh=mesh,
        in_specs=placed,
        out_specs=(P(AXES, None), P(AXES, None)),
        check_vma=False,
    )
```
